128 devices in a mesh: section: 16 (over x_hi, y, core), dp: 8 (over x_lo, z).
Axes of the slice: x: 4 (x_hi: 2, x_lo: 2; x = x_hi * 2 + x_lo), y: 4, z: 4, core: 2. Of those that a mesh axis runs over, the one named last changes fastest.
Arguments:
- master_weights: float32 [16, 8192, 512], P('section', 'dp'), may hold values from -0.0625 to 0.0625
- first_moment: float32 [16, 8192, 512], P('section', 'dp'), may hold values from -2 to 2
- second_moment: float32 [16, 8192, 512], P('section', 'dp'), may hold values from 0.05 to 2
- gradient_shard: float32 [16, 8192, 512], P('section', 'dp'), may hold values from -6 to 6
- hidden_states: bfloat16 [16, 2, 1024, 8192], P('section', None, 'dp'), may hold values from -6 to 6
Outputs:
- new_master: float32 [16, 8192, 512], P('section', 'dp')
- new_first: float32 [16, 8192, 512], P('section', 'dp')
- new_second: float32 [16, 8192, 512], P('section', 'dp')
- hidden_out: bfloat16 [16, 2, 1024, 8192], P('section', None, 'dp')
The draws below stay inside these ranges and needn't reach their ends.
All inputs are finite; a program needn't handle non-finite values.
Results may differ from the reference program's by a relative error of at most 0.008.
Values may be sent and summed in bfloat16 or wider, within the bound.
No kernel may reach another device: no remote copies, remote signals or barrier semaphores. Data moves between devices by JAX's collectives and lax.ppermute only.
A program may use at most 192 MiB of HBM per device.

```python
import math
import jax
import jax.numpy as jnp
from jax import lax

D = 8192
KVW = 512
MB = 2
ROUNDS = 4
ADAM_STEP = 1000
SECTIONS = 16
TOKROWS = 1024


def levels(own_key, shape, shards, smallest, largest):
    level, own = 1.0, jax.random.fold_in(own_key, 6)
    for axis_at, blocks in shards:
        steps = jnp.exp(jax.random.uniform(jax.random.fold_in(own, axis_at), (blocks,), jnp.float32, smallest / len(shards), largest / len(shards)))
        level = level * jnp.repeat(steps, shape[axis_at] // blocks).reshape([-1 if axis == axis_at else 1 for axis in range(len(shape))])
    return level


def normal_values(stream_key, extent, width, reach, pieces=(), held_as=jnp.bfloat16):
    gain = levels(stream_key, extent, pieces, -0.22, 0.18) if pieces else 1.0
    result = jax.random.normal(stream_key, extent, jnp.float32) * width * gain
    return jnp.minimum(jnp.maximum(result, -reach), reach).astype(held_as)


def setup_inputs(seed: int = 0) -> dict:
    keys = jax.random.split(jax.random.key(seed), 6)
    master_weights = normal_values(keys[0], (SECTIONS, D, KVW), D ** -0.5, 0.0625, ((0, 16), (1, 8)), jnp.float32)
    first_moment = normal_values(keys[1], (SECTIONS, D, KVW), 0.3, 2.0, ((0, 16), (1, 8)), jnp.float32)
    second_moment = jnp.clip(jnp.exp(math.log(2.0) - 3.6888794 * jax.random.uniform(keys[2], (SECTIONS, D, KVW), jnp.float32) ** levels(keys[2], (SECTIONS, D, KVW), ((0, 16), (1, 8)), -0.2, 0.2)), 0.05, 2.0)
    gradient_shard = normal_values(keys[3], (SECTIONS, D, KVW), 1.0, 6.0, ((0, 16), (1, 8)), jnp.float32)
    hidden_states = normal_values(keys[4], (SECTIONS, MB, TOKROWS, D), 1.0, 6.0, ((0, 16), (2, 8)))
    return {"master_weights": master_weights, "first_moment": first_moment, "second_moment": second_moment, "gradient_shard": gradient_shard, "hidden_states": hidden_states}


beta_one = 0.9
beta_two = 0.95
learn_rate = 0.0003
decay_rate = 0.1
adam_eps = 1e-08
norm_eps = 1e-05

def adamw_update(master, moment, second, gradient):
    moment_new = beta_one * moment + (1.0 - beta_one) * gradient
    second_new = beta_two * second + (1.0 - beta_two) * gradient * gradient
    corr_one = 1.0 - beta_one ** ADAM_STEP
    corr_two = 1.0 - beta_two ** ADAM_STEP
    step_size = moment_new / corr_one / (jnp.sqrt(second_new / corr_two) + adam_eps)
    master_new = master - learn_rate * (step_size + decay_rate * master)
    return (master_new, moment_new, second_new)

def layer_apply(block, weight):
    shape_in = block.shape
    flat = block.reshape(-1, shape_in[-1]).astype(jnp.float32)
    normed = (flat * lax.rsqrt(lax.optimization_barrier(jnp.mean(flat * flat, axis=-1, keepdims=True)) + norm_eps)).astype(jnp.bfloat16)
    projected = jnp.dot(normed, weight, preferred_element_type=jnp.float32).astype(jnp.bfloat16)
    update = jnp.dot(projected, weight.T, preferred_element_type=jnp.float32)
    return (flat + update).astype(jnp.bfloat16).reshape(shape_in)

def reference(master_weights, first_moment, second_moment, gradient_shard, hidden_states):
    new_master, new_first, new_second = adamw_update(master_weights, first_moment, second_moment, gradient_shard)
    weights = new_master.astype(jnp.bfloat16)
    hidden = hidden_states
    for step in range(ROUNDS):
        hidden = lax.map(lambda pair: layer_apply(pair[0], pair[1]), (hidden, weights))
        hidden = jnp.roll(hidden, 1, axis=0)
    return (new_master, new_first, new_second, hidden)
```

```python
import functools

import jax
import jax.numpy as jnp
from jax import lax
from jax.experimental import pallas as pl
from jax.experimental.pallas import tpu as pltpu
from jax.sharding import PartitionSpec as P

ADAM_STEP = 1000

beta_one = 0.9
beta_two = 0.95
learn_rate = 0.0003
decay_rate = 0.1
adam_eps = 1e-08
norm_eps = 1e-05

AXES = ("section", "dp")
D = 8192
KVW = 512
ROWS = 256
SUB = 512
HALF = D // 2
LANES = 128
VMEM = 56 * 1024 * 1024


def place(linear):
    section, dp = divmod(linear, 8)
    return section // 2, section % 2, dp // 4, dp % 4


def linear_of(chip, core, xlo, z):
    return ((chip % 8) * 2 + core) * 8 + (xlo % 2) * 4 + z % 4


def shift(value, move):
    pairs = [(source, linear_of(*move(*place(source)))) for source in range(128)]
    return lax.ppermute(value, AXES, pairs)


def to_core(value):
    return shift(value, lambda chip, core, xlo, z: (chip, 1 - core, xlo, z))


def to_pair(value):
    return shift(value, lambda chip, core, xlo, z: (chip, core, xlo + 1, z))


def to_ring(value):
    return shift(value, lambda chip, core, xlo, z: (chip, core, xlo, z + 1 - 2 * core))


def to_chip(value, steps):
    return shift(value, lambda chip, core, xlo, z: (chip + steps, core, xlo, z))


def adamw_update(master, moment, second, gradient):
    moment_new = beta_one * moment + (1.0 - beta_one) * gradient
    second_new = beta_two * second + (1.0 - beta_two) * gradient * gradient
    corr_one = 1.0 - beta_one**ADAM_STEP
    corr_two = 1.0 - beta_two**ADAM_STEP
    step_size = moment_new / corr_one / (jnp.sqrt(second_new / corr_two) + adam_eps)
    master_new = master - learn_rate * (step_size + decay_rate * master)
    return (master_new, moment_new, second_new)


def split_kernel(core_ref, whole_ref, keep_ref, give_ref):
    first = whole_ref[:, :SUB]
    last = whole_ref[:, SUB:]
    upper = core_ref[0] == 1
    keep_ref[...] = jnp.where(upper, last, first)
    give_ref[...] = jnp.where(upper, first, last)


def split_halves(core, whole):
    spec = pl.BlockSpec((ROWS, SUB), lambda i, core: (0, i))
    return pl.pallas_call(
        split_kernel,
        grid_spec=pltpu.PrefetchScalarGridSpec(
            num_scalar_prefetch=1,
            grid=(8,),
            in_specs=[pl.BlockSpec((ROWS, 2 * SUB), lambda i, core: (0, i))],
            out_specs=[spec, spec],
        ),
        out_shape=[jax.ShapeDtypeStruct((ROWS, HALF), jnp.bfloat16)] * 2,
        cost_estimate=pl.CostEstimate(flops=0, bytes_accessed=8 << 20, transcendentals=0),
        name="split_halves",
    )(core, whole)


def merge_kernel(core_ref, keep_ref, got_ref, whole_ref):
    upper = core_ref[0] == 1
    keep = keep_ref[...]
    got = got_ref[...]
    whole_ref[:, :SUB] = jnp.where(upper, got, keep)
    whole_ref[:, SUB:] = jnp.where(upper, keep, got)


def merge_halves(core, keep, got):
    spec = pl.BlockSpec((ROWS, SUB), lambda i, core: (0, i))
    return pl.pallas_call(
        merge_kernel,
        grid_spec=pltpu.PrefetchScalarGridSpec(
            num_scalar_prefetch=1,
            grid=(8,),
            in_specs=[spec, spec],
            out_specs=pl.BlockSpec((ROWS, 2 * SUB), lambda i, core: (0, i)),
        ),
        out_shape=jax.ShapeDtypeStruct((ROWS, D), jnp.bfloat16),
        cost_estimate=pl.CostEstimate(flops=0, bytes_accessed=8 << 20, transcendentals=0),
        name="merge_halves",
    )(core, keep, got)


def columns_of(place_ref, step, xlo):
    return pl.ds(pl.multiple_of(place_ref[step * 2 + xlo], SUB), SUB)


def project_into(place_ref, hidden, weights, out_ref):
    rows = out_ref.shape[0]
    total = jnp.zeros((rows, KVW), jnp.float32)
    squares = jnp.zeros((rows, 1), jnp.float32)
    for step in range(4):
        for xlo in range(2):
            part = hidden[:, columns_of(place_ref, step, xlo)]
            total += jnp.dot(
                part,
                weights[step][xlo * SUB : (xlo + 1) * SUB, :],
                preferred_element_type=jnp.float32,
            )
            flat = part.astype(jnp.float32)
            squares += jnp.sum(flat * flat, axis=1, keepdims=True)
    out_ref[:, :KVW] = total
    out_ref[:, KVW:] = jnp.broadcast_to(squares, (rows, LANES))


def expand_into(place_ref, hidden, mine, theirs, weights, out_ref):
    summed = mine[...] + theirs[...]
    scale = lax.rsqrt(summed[:, KVW : KVW + 1] * (1.0 / D) + norm_eps)
    projected = (summed[:, :KVW] * scale).astype(jnp.bfloat16)
    for step in range(4):
        for xlo in range(2):
            columns = columns_of(place_ref, step, xlo)
            update = lax.dot_general(
                projected,
                weights[step][xlo * SUB : (xlo + 1) * SUB, :],
                (((1,), (1,)), ((), ())),
                preferred_element_type=jnp.float32,
            )
            out_ref[:, columns] = (hidden[:, columns].astype(jnp.float32) + update).astype(
                jnp.bfloat16
            )


def project_kernel(place_ref, hidden, w0, w1, w2, w3, out_ref):
    project_into(place_ref, hidden, (w0, w1, w2, w3), out_ref)


def expand_kernel(place_ref, hidden, mine, theirs, w0, w1, w2, w3, out_ref):
    expand_into(place_ref, hidden, mine, theirs, (w0, w1, w2, w3), out_ref)


def whole_call(kernel, out_shape, place, operands, flops, name):
    moved = sum(a.size * a.dtype.itemsize for a in operands)
    moved += sum(a.size * a.dtype.itemsize for a in jax.tree.leaves(out_shape))
    return pl.pallas_call(
        kernel,
        in_specs=[pl.BlockSpec(memory_space=pltpu.SMEM)]
        + [pl.BlockSpec(memory_space=pltpu.VMEM)] * len(operands),
        out_specs=jax.tree.map(lambda a: pl.BlockSpec(memory_space=pltpu.VMEM), out_shape),
        out_shape=out_shape,
        compiler_params=pltpu.CompilerParams(vmem_limit_bytes=VMEM),
        cost_estimate=pl.CostEstimate(flops=flops, bytes_accessed=moved, transcendentals=0),
        name=name,
    )(place, *operands)


def project(place, hidden, weights):
    rows = hidden.shape[0]
    return whole_call(
        project_kernel,
        jax.ShapeDtypeStruct((rows, KVW + LANES), jnp.float32),
        place,
        (hidden, *weights),
        2 * rows * HALF * KVW,
        "project",
    )


def expand(place, hidden, mine, theirs, weights):
    rows = hidden.shape[0]
    return whole_call(
        expand_kernel,
        jax.ShapeDtypeStruct((rows, HALF), jnp.bfloat16),
        place,
        (hidden, mine, theirs, *weights),
        2 * rows * HALF * KVW,
        "expand",
    )


def apply_layer(place, hidden, weights):
    mine = project(place, hidden, weights)
    return expand(place, hidden, mine, to_core(mine), weights)


def gather_pieces(own, xlo):
    other = to_pair(own)
    lower = xlo == 0
    piece = jnp.concatenate([jnp.where(lower, own, other), jnp.where(lower, other, own)], axis=0)
    pieces = [piece]
    for _ in range(3):
        pieces.append(to_ring(pieces[-1]))
    return pieces


def per_device(master_weights, first_moment, second_moment, gradient_shard, hidden_states):
    core = lax.rem(lax.axis_index("section"), 2)
    xlo = lax.div(lax.axis_index("dp"), 4)
    z = lax.rem(lax.axis_index("dp"), 4)
    upper = core == 1
    core_word = jnp.reshape(core, (1,)).astype(jnp.int32)
    step = jnp.arange(4, dtype=jnp.int32)
    owner = lax.rem(z + jnp.where(upper, step, 4 - step), 4)
    table = jnp.stack([owner * SUB, (owner + 4) * SUB], axis=1).reshape(8).astype(jnp.int32)

    block = hidden_states.reshape(ROWS, D)
    keep, give = split_halves(core_word, block)
    got = to_core(give)
    even = jnp.where(upper, got, keep)
    odd = jnp.where(upper, keep, got)
    odd = to_chip(odd, 2)

    new_master, new_first, new_second = adamw_update(
        master_weights, first_moment, second_moment, gradient_shard
    )
    rows = new_master[0].astype(jnp.bfloat16)
    mine = lax.dynamic_slice_in_dim(rows, core * SUB, SUB, 0)
    theirs = lax.dynamic_slice_in_dim(rows, (1 - core) * SUB, SUB, 0)
    other = to_core(theirs)
    even_rows = jnp.where(upper, other, mine)
    odd_rows = jnp.where(upper, mine, other)

    home = gather_pieces(even_rows, xlo)
    far = to_chip(odd_rows, 2)
    near = to_chip(jnp.concatenate([even_rows, odd_rows], axis=0), 1)
    first = gather_pieces(far, xlo)
    second = gather_pieces(near[:SUB], xlo)
    third = gather_pieces(near[SUB:], xlo)

    even = to_chip(apply_layer(table, even, home), 2)
    both = jnp.concatenate([even, odd], axis=0)
    both = apply_layer(table, both, first)
    both = apply_layer(table, both, second)
    both = apply_layer(table, both, third)
    even = both[:ROWS]
    odd = apply_layer(table, both[ROWS:], home)
    keep = jnp.where(upper, odd, even)
    give = jnp.where(upper, even, odd)
    out = merge_halves(core_word, keep, to_core(give))
    return (new_master, new_first, new_second, out.reshape(hidden_states.shape))


def solution(mesh):
    placed = (
        P("section", "dp", None),
        P("section", "dp", None),
        P("section", "dp", None),
        P("section", "dp", None),
        P("section", None, "dp", None),
    )
    return jax.shard_map(
        per_device,
        mesh=mesh,
        in_specs=placed,
        out_specs=(
            P("section", "dp", None),
            P("section", "dp", None),
            P("section", "dp", None),
            P("section", None, "dp", None),
        ),
        check_vma=False,
    )
```

```python
import dataclasses
import functools

import jax
import jax.numpy as jnp
from jax import lax
from jax.experimental import pallas as pl
from jax.experimental.pallas import tpu as pltpu
from jax.sharding import PartitionSpec as P

ADAM_STEP = 1000

beta_one = 0.9
beta_two = 0.95
learn_rate = 0.0003
decay_rate = 0.1
adam_eps = 1e-08
norm_eps = 1e-05

AXES = ("section", "dp")
D = 8192
KVW = 512
ROWS = 256
SUB = 512
HALF = D // 2
LANES = 128
VMEM = 56 * 1024 * 1024


def place(linear):
    section, dp = divmod(linear, 8)
    return section // 2, section % 2, dp // 4, dp % 4


def linear_of(chip, core, xlo, z):
    return ((chip % 8) * 2 + core) * 8 + (xlo % 2) * 4 + z % 4


def shift(value, move):
    pairs = [(source, linear_of(*move(*place(source)))) for source in range(128)]
    return lax.ppermute(value, AXES, pairs)


def to_core(value):
    return shift(value, lambda chip, core, xlo, z: (chip, 1 - core, xlo, z))


def to_pair(value):
    return shift(value, lambda chip, core, xlo, z: (chip, core, xlo + 1, z))


def to_ring(value):
    return shift(value, lambda chip, core, xlo, z: (chip, core, xlo, z + 1 - 2 * core))


def to_chip(value, steps):
    return shift(value, lambda chip, core, xlo, z: (chip + steps, core, xlo, z))


def adamw_update(master, moment, second, gradient):
    moment_new = beta_one * moment + (1.0 - beta_one) * gradient
    second_new = beta_two * second + (1.0 - beta_two) * gradient * gradient
    corr_one = 1.0 - beta_one**ADAM_STEP
    corr_two = 1.0 - beta_two**ADAM_STEP
    step_size = moment_new / corr_one / (jnp.sqrt(second_new / corr_two) + adam_eps)
    master_new = master - learn_rate * (step_size + decay_rate * master)
    return (master_new, moment_new, second_new)


def split_kernel(core_ref, whole_ref, keep_ref, give_ref):
    first = whole_ref[:, :SUB]
    last = whole_ref[:, SUB:]
    upper = core_ref[0] == 1
    keep_ref[...] = jnp.where(upper, last, first)
    give_ref[...] = jnp.where(upper, first, last)


def split_halves(core, whole):
    spec = pl.BlockSpec((ROWS, SUB), lambda i, core: (0, i))
    return pl.pallas_call(
        split_kernel,
        grid_spec=pltpu.PrefetchScalarGridSpec(
            num_scalar_prefetch=1,
            grid=(8,),
            in_specs=[pl.BlockSpec((ROWS, 2 * SUB), lambda i, core: (0, i))],
            out_specs=[spec, spec],
        ),
        out_shape=[jax.ShapeDtypeStruct((ROWS, HALF), jnp.bfloat16)] * 2,
        cost_estimate=pl.CostEstimate(flops=0, bytes_accessed=8 << 20, transcendentals=0),
        name="split_halves",
    )(core, whole)


def read_columns(table, blocks, slots, sems, order):
    copies = {}
    for chunk in order:
        column = pl.multiple_of(table[chunk], SUB)
        for index, block in enumerate(blocks):
            copies[chunk, index] = pltpu.make_async_copy(
                block.at[:, pl.ds(column, SUB)],
                slots.at[chunk, pl.ds(index * ROWS, ROWS)],
                sems.at[chunk, index],
            )
    return copies


def chunks_of(pieces):
    return [
        piece.at[pl.ds(start, SUB)] for piece in pieces for start in range(0, piece.shape[0], SUB)
    ]


def read_pieces(pieces, slots, sems):
    return [
        pltpu.make_async_copy(chunk, slots.at[index], sems.at[index])
        for index, chunk in enumerate(chunks_of(pieces))
    ]


def layer_kernel(plan, *refs):
    refs = list(refs)

    def take(count):
        taken, refs[:count] = refs[:count], []
        return taken

    (table,) = take(1)
    blocks = take(plan.blocks)
    mine, theirs = take(2) if plan.last else (None, None)
    last = take(plan.last)
    begun = take(1) if plan.adds else []
    after = take(plan.after)
    fresh = take(plan.blocks) if plan.last else []
    out = take(1) if plan.after else []
    columns, column_sems = take(2)
    last_slots, last_sems = take(2) if plan.last else (None, None)
    after_slots, after_sems = take(2) if plan.after else (None, None)
    (store_sems,) = take(1) if plan.last else (None,)

    taken_up = range(plan.first, plan.first + plan.count)
    chunks = range(8) if plan.last else taken_up
    reads = read_columns(table, blocks, columns, column_sems, chunks)
    last_reads = read_pieces(last, last_slots, last_sems) if plan.last else []
    after_reads = read_pieces(after, after_slots, after_sems) if plan.after else []
    for chunk in chunks:
        for index in range(plan.blocks):
            reads[chunk, index].start()
        if plan.last:
            last_reads[chunk].start()
        if chunk in taken_up:
            after_reads[chunk - plan.first].start()

    rows = plan.blocks * ROWS
    if plan.last:
        summed = mine[...] + theirs[...]
        scale = lax.rsqrt(summed[:, KVW : KVW + 1] * (1.0 / D) + norm_eps)
        projected = (summed[:, :KVW] * scale).astype(jnp.bfloat16)
    skip = plan.skip * ROWS
    if plan.after:
        total = jnp.zeros((rows - skip, KVW), jnp.float32)
        squares = jnp.zeros((rows - skip, 1), jnp.float32)
        if plan.adds:
            total += begun[0][:, :KVW]
            squares += begun[0][:, KVW : KVW + 1]
    stores = []
    for chunk in chunks:
        for index in range(plan.blocks):
            reads[chunk, index].wait()
        part = columns[chunk]
        if plan.last:
            last_reads[chunk].wait()
            update = lax.dot_general(
                projected,
                last_slots[chunk],
                (((1,), (1,)), ((), ())),
                preferred_element_type=jnp.float32,
            )
            part = (part.astype(jnp.float32) + update).astype(jnp.bfloat16)
            columns[chunk] = part
            column = pl.multiple_of(table[chunk], SUB)
            if plan.swaps:
                own = table[8]
                sources = [own * ROWS, (1 - own) * ROWS]
            else:
                sources = [index * ROWS for index in range(plan.blocks)]
            for index in range(plan.blocks):
                stores.append(
                    pltpu.make_async_copy(
                        columns.at[chunk, pl.ds(sources[index], ROWS)],
                        fresh[index].at[:, pl.ds(column, SUB)],
                        store_sems.at[chunk, index],
                    )
                )
                stores[-1].start()
        if chunk in taken_up:
            after_reads[chunk - plan.first].wait()
            part = part[skip:]
            total += jnp.dot(
                part,
                after_slots[chunk - plan.first],
                preferred_element_type=jnp.float32,
            )
            flat = part.astype(jnp.float32)
            squares += jnp.sum(flat * flat, axis=1, keepdims=True)
    if plan.after:
        out[0][:, :KVW] = total
        out[0][:, KVW:] = jnp.broadcast_to(squares, (rows - skip, LANES))
    for store in stores:
        store.wait()


@dataclasses.dataclass(frozen=True)
class Plan:
    blocks: int
    last: int
    after: int
    first: int = 0
    count: int = 0
    adds: bool = False
    skip: int = 0
    swaps: bool = False


def layer_call(table, blocks, sums=(), last=(), begun=(), after=(), name="layer", **plan):
    count = sum(piece.shape[0] for piece in after) // SUB
    plan = Plan(len(blocks), len(last), len(after), count=count, adds=len(begun) > 0, **plan)
    rows = plan.blocks * ROWS
    any_space = pl.BlockSpec(memory_space=pl.ANY)
    vmem = pl.BlockSpec(memory_space=pltpu.VMEM)
    out_shape, out_specs = [], []
    scratch = [
        pltpu.VMEM((8, rows, SUB), jnp.bfloat16),
        pltpu.SemaphoreType.DMA((8, plan.blocks)),
    ]
    if plan.last:
        out_shape += [jax.ShapeDtypeStruct((ROWS, HALF), jnp.bfloat16)] * plan.blocks
        out_specs += [any_space] * plan.blocks
        scratch += [pltpu.VMEM((8, SUB, KVW), jnp.bfloat16), pltpu.SemaphoreType.DMA((8,))]
    if plan.after:
        out_shape.append(jax.ShapeDtypeStruct((rows - plan.skip * ROWS, KVW + LANES), jnp.float32))
        out_specs.append(vmem)
        scratch += [
            pltpu.VMEM((plan.count, SUB, KVW), jnp.bfloat16),
            pltpu.SemaphoreType.DMA((plan.count,)),
        ]
    if plan.last:
        scratch.append(pltpu.SemaphoreType.DMA((8, plan.blocks)))
    flops = 2 * SUB * KVW * (rows * 8 * (plan.last > 0) + (rows - plan.skip * ROWS) * count)
    moved = (2 << 20) * plan.blocks * (1 + (plan.last > 0)) + (4 << 20) * (plan.last > 0)
    moved += count << 19
    return pl.pallas_call(
        functools.partial(layer_kernel, plan),
        in_specs=[pl.BlockSpec(memory_space=pltpu.SMEM)]
        + [any_space] * len(blocks)
        + [vmem] * len(sums)
        + [any_space] * len(last)
        + [vmem] * len(begun)
        + [any_space] * len(after),
        out_specs=out_specs,
        out_shape=out_shape,
        scratch_shapes=scratch,
        compiler_params=pltpu.CompilerParams(vmem_limit_bytes=VMEM),
        cost_estimate=pl.CostEstimate(flops=flops, bytes_accessed=moved, transcendentals=0),
        name=name,
    )(table, *blocks, *sums, *last, *begun, *after)


def final_kernel(table, keep, got, mine, theirs, *refs):
    pieces, (whole, slots, slot_sems, w_slots, w_sems, store_sems) = refs[:-6], refs[-6:]
    upper = table[8] == 1
    reads, stores = [], []
    for chunk in range(16):
        source = keep if chunk < 8 else got
        column = pl.multiple_of(table[(0 if chunk < 8 else 16) + chunk % 8], SUB)
        reads.append(
            pltpu.make_async_copy(
                source.at[:, pl.ds(column, SUB)], slots.at[chunk], slot_sems.at[chunk]
            )
        )
        side = table[8] if chunk < 8 else 1 - table[8]
        target = pl.multiple_of(2 * column + side * SUB, SUB)
        stores.append(
            pltpu.make_async_copy(
                slots.at[chunk], whole.at[:, pl.ds(target, SUB)], store_sems.at[chunk]
            )
        )
    weights = read_pieces(pieces, w_slots, w_sems)
    for chunk in range(16):
        reads[chunk].start()
        weights[chunk].start()
    summed = mine[...] + theirs[...]
    scale = lax.rsqrt(summed[:, KVW : KVW + 1] * (1.0 / D) + norm_eps)
    projected = (summed[:, :KVW] * scale).astype(jnp.bfloat16)
    for chunk in range(16):
        reads[chunk].wait()
        weights[chunk].wait()

        @pl.when(upper)
        def _():
            update = lax.dot_general(
                projected,
                w_slots[chunk],
                (((1,), (1,)), ((), ())),
                preferred_element_type=jnp.float32,
            )
            slots[chunk] = (slots[chunk].astype(jnp.float32) + update).astype(jnp.bfloat16)

        stores[chunk].start()
    for store in stores:
        store.wait()


def final_call(table, keep, got, mine, theirs, here, there):
    any_space = pl.BlockSpec(memory_space=pl.ANY)
    vmem = pl.BlockSpec(memory_space=pltpu.VMEM)
    return pl.pallas_call(
        final_kernel,
        in_specs=[pl.BlockSpec(memory_space=pltpu.SMEM), any_space, any_space, vmem, vmem]
        + [any_space] * (len(here) + len(there)),
        out_specs=any_space,
        out_shape=jax.ShapeDtypeStruct((ROWS, D), jnp.bfloat16),
        scratch_shapes=[
            pltpu.VMEM((16, ROWS, SUB), jnp.bfloat16),
            pltpu.SemaphoreType.DMA((16,)),
            pltpu.VMEM((16, SUB, KVW), jnp.bfloat16),
            pltpu.SemaphoreType.DMA((16,)),
            pltpu.SemaphoreType.DMA((16,)),
        ],
        compiler_params=pltpu.CompilerParams(vmem_limit_bytes=VMEM),
        cost_estimate=pl.CostEstimate(
            flops=2 * ROWS * D * KVW, bytes_accessed=16 << 20, transcendentals=0
        ),
        name="final_layer",
    )(table, keep, got, mine, theirs, *here, *there)


def after(value, *events):
    return lax.optimization_barrier((value, *events))[0]


def together(own, other):
    return jnp.concatenate([own, other], axis=0)


def per_device(master_weights, first_moment, second_moment, gradient_shard, hidden_states):
    core = lax.rem(lax.axis_index("section"), 2)
    xlo = lax.div(lax.axis_index("dp"), 4)
    z = lax.rem(lax.axis_index("dp"), 4)
    upper = core == 1
    core_word = jnp.reshape(core, (1,)).astype(jnp.int32)
    step = jnp.arange(4, dtype=jnp.int32)

    def columns(is_upper):
        owner = lax.rem(z + jnp.where(is_upper, step, 4 - step), 4)
        return jnp.stack([owner + 4 * xlo, owner + 4 * (1 - xlo)], axis=1).reshape(8) * SUB

    filler = jnp.zeros((7,), jnp.int32)
    table = jnp.concatenate([columns(upper), core_word, filler, columns(~upper)]).astype(jnp.int32)

    new_master, new_first, new_second = adamw_update(
        master_weights, first_moment, second_moment, gradient_shard
    )
    rows = new_master[0].astype(jnp.bfloat16)
    mine = lax.dynamic_slice_in_dim(rows, core * SUB, SUB, 0)
    theirs = lax.dynamic_slice_in_dim(rows, (1 - core) * SUB, SUB, 0)
    other = to_core(theirs)
    even_rows = jnp.where(upper, other, mine)
    odd_rows = jnp.where(upper, mine, other)

    home_other = to_pair(even_rows)
    home_own = [even_rows, to_ring(even_rows)]
    far = to_chip(odd_rows, 2)
    near = to_chip(together(even_rows, odd_rows), 1)

    block = hidden_states.reshape(ROWS, D)
    keep, give = split_halves(core_word, after(block, even_rows))
    got = to_core(give)
    even = jnp.where(upper, got, keep)
    odd = jnp.where(upper, keep, got)

    phase = (home_own[1], home_other, far)
    home_other, far = after(home_other, *phase), after(far, *phase)
    home_own.append(to_ring(after(home_own[1], *phase)))
    home_others = [home_other, to_ring(home_other)]
    far_other = to_pair(far)
    odd = to_chip(after(odd, *phase), 2)

    phase = (home_own[2], home_others[1], far_other)
    home_own.append(to_ring(after(home_own[2], *phase)))
    home_others.append(to_ring(after(home_others[1], *phase)))
    first = [after(together(far, far_other), *phase)]
    first.append(to_ring(first[0]))

    phase = (home_own[3], home_others[2], near)
    home_others.append(to_ring(after(home_others[2], *phase)))
    near = after(near, *phase)
    near_other = to_pair(near)

    phase = (home_others[3], first[1])
    first.append(to_ring(after(first[1], *phase)))
    home = [piece for pair in zip(home_own, home_others) for piece in pair]
    even = after(even, *phase)
    (product,) = layer_call(table, (even,), after=home, name="project_home")
    (even,) = layer_call(
        table, (even,), sums=(product, to_core(product)), last=home, name="expand_home"
    )
    near_other = after(near_other, even)
    even = to_chip(even, 2)

    second = [together(near[:SUB], near_other[:SUB])]
    third = [together(near[SUB:], near_other[SUB:])]
    second.append(to_ring(second[0]))
    phase = (first[2], second[0], odd)
    first.append(to_ring(after(first[2], *phase)))
    home_there = to_core(after(jnp.concatenate(home, axis=0), *phase))
    phase = (second[1], first[2])
    second.append(to_ring(after(second[1], *phase)))
    phase = (first[3], second[1], home_there)
    third.append(to_ring(after(third[0], *phase)))
    second.append(to_ring(second[2]))
    even = after(even, second[2], third[1], home_there)
    third.append(to_ring(after(third[1], even)))
    third.append(to_ring(third[2]))

    (product,) = layer_call(table, (even, odd), after=first, name="project_first")
    even, odd, product = layer_call(
        table,
        (even, odd),
        sums=(product, to_core(product)),
        last=first,
        after=second,
        name="first_second",
    )
    even, odd, product = layer_call(
        table,
        (even, odd),
        sums=(product, to_core(product)),
        last=second,
        after=third[:3],
        name="second_third",
    )
    (product,) = layer_call(
        table, (even, odd), begun=(product,), after=third[3:], first=6, name="third_rest"
    )
    keep, give, product = layer_call(
        table,
        (even, odd),
        sums=(product, to_core(product)),
        last=third,
        after=home,
        skip=1,
        swaps=True,
        name="third_home",
    )
    out = final_call(
        table, keep, to_core(give), product, to_core(product), home, [home_there]
    )
    return (new_master, new_first, new_second, out.reshape(hidden_states.shape))


def solution(mesh):
    placed = (
        P("section", "dp", None),
        P("section", "dp", None),
        P("section", "dp", None),
        P("section", "dp", None),
        P("section", None, "dp", None),
    )
    return jax.shard_map(
        per_device,
        mesh=mesh,
        in_specs=placed,
        out_specs=(
            P("section", "dp", None),
            P("section", "dp", None),
            P("section", "dp", None),
            P("section", None, "dp", None),
        ),
        check_vma=False,
    )
```

```python
import dataclasses
import functools

import jax
import jax.numpy as jnp
from jax import lax
from jax.experimental import pallas as pl
from jax.experimental.pallas import tpu as pltpu
from jax.sharding import PartitionSpec as P

ADAM_STEP = 1000

beta_one = 0.9
beta_two = 0.95
learn_rate = 0.0003
decay_rate = 0.1
adam_eps = 1e-08
norm_eps = 1e-05

AXES = ("section", "dp")
D = 8192
KVW = 512
ROWS = 256
SUB = 512
HALF = D // 2
LANES = 128
VMEM = 56 * 1024 * 1024
UPDATE_STEPS = 4
SUB_STEP = SUB // UPDATE_STEPS
AHEAD = 3


def place(linear):
    section, dp = divmod(linear, 8)
    return section // 2, section % 2, dp // 4, dp % 4


def linear_of(chip, core, xlo, z):
    return ((chip % 8) * 2 + core) * 8 + (xlo % 2) * 4 + z % 4


def shift(value, move):
    pairs = [(source, linear_of(*move(*place(source)))) for source in range(128)]
    return lax.ppermute(value, AXES, pairs)


def to_core(value):
    return shift(value, lambda chip, core, xlo, z: (chip, 1 - core, xlo, z))


def to_pair(value):
    return shift(value, lambda chip, core, xlo, z: (chip, core, xlo + 1, z))


def to_ring(value):
    return shift(value, lambda chip, core, xlo, z: (chip, core, xlo, z + 1 - 2 * core))


def to_chip(value, steps):
    return shift(value, lambda chip, core, xlo, z: (chip + steps, core, xlo, z))


def to_next(value, hop):
    def move(chip, core, xlo, z):
        xhi, y = divmod(chip, 4)
        start = (y - hop + 2 * hop * core) % 4
        if start >= 2 and hop == ((start + core) % 2):
            xhi = 1 - xhi
        return xhi * 4 + (y + 1 - 2 * core) % 4, core, xlo, z

    return shift(value, move)


def adamw_update(master, moment, second, gradient):
    moment_new = beta_one * moment + (1.0 - beta_one) * gradient
    second_new = beta_two * second + (1.0 - beta_two) * gradient * gradient
    corr_one = 1.0 - beta_one**ADAM_STEP
    corr_two = 1.0 - beta_two**ADAM_STEP
    step_size = moment_new / corr_one / (jnp.sqrt(second_new / corr_two) + adam_eps)
    master_new = master - learn_rate * (step_size + decay_rate * master)
    return (master_new, moment_new, second_new)


def update_kernel(
    core_ref,
    master_ref,
    moment_ref,
    second_ref,
    gradient_ref,
    whole,
    master_out,
    moment_out,
    second_out,
    keep_rows,
    give_rows,
    keep,
    give,
    sems,
):
    step = pl.program_id(0)
    core = core_ref[0]

    def copies():
        for part in range(8):
            for side, target in ((core, keep), (1 - core, give)):
                column = pl.multiple_of(part * 2 * SUB + side * SUB, SUB)
                yield pltpu.make_async_copy(
                    whole.at[:, pl.ds(column, SUB)],
                    target.at[:, pl.ds(part * SUB, SUB)],
                    sems.at[part, 0 if target is keep else 1],
                )

    @pl.when(step == 0)
    def _():
        for copy in copies():
            copy.start()

    new_master, new_moment, new_second = adamw_update(
        master_ref[...], moment_ref[...], second_ref[...], gradient_ref[...]
    )
    master_out[...] = new_master
    moment_out[...] = new_moment
    second_out[...] = new_second
    first = new_master[0].astype(jnp.bfloat16)
    last = new_master[1].astype(jnp.bfloat16)
    keep_rows[...] = jnp.where(core == 0, first, last)
    give_rows[...] = jnp.where(core == 0, last, first)

    @pl.when(step == UPDATE_STEPS - 1)
    def _():
        for copy in copies():
            copy.wait()


def update_call(core, master, moment, second, gradient, whole):
    any_space = pl.BlockSpec(memory_space=pl.ANY)
    state = pl.BlockSpec((2, SUB_STEP, KVW), lambda i, core: (0, i, 0))
    half = pl.BlockSpec((SUB_STEP, KVW), lambda i, core: (i, 0))
    shaped = [a.reshape(2, SUB, KVW) for a in (master, moment, second, gradient)]
    outs = pl.pallas_call(
        update_kernel,
        grid_spec=pltpu.PrefetchScalarGridSpec(
            num_scalar_prefetch=1,
            grid=(UPDATE_STEPS,),
            in_specs=[state] * 4 + [any_space],
            out_specs=[state] * 3 + [half] * 2 + [any_space] * 2,
            scratch_shapes=[pltpu.SemaphoreType.DMA((8, 2))],
        ),
        out_shape=[jax.ShapeDtypeStruct((2, SUB, KVW), jnp.float32)] * 3
        + [jax.ShapeDtypeStruct((SUB, KVW), jnp.bfloat16)] * 2
        + [jax.ShapeDtypeStruct((ROWS, HALF), jnp.bfloat16)] * 2,
        compiler_params=pltpu.CompilerParams(vmem_limit_bytes=VMEM),
        cost_estimate=pl.CostEstimate(flops=0, bytes_accessed=23 << 20, transcendentals=0),
        name="update",
    )(core, *shaped, whole)
    return [a.reshape(master.shape) for a in outs[:3]], *outs[3:]


def read_columns(table, blocks, slots, sems, order):
    copies = {}
    for chunk in order:
        column = pl.multiple_of(table[chunk], SUB)
        for index, block in enumerate(blocks):
            copies[chunk, index] = pltpu.make_async_copy(
                block.at[:, pl.ds(column, SUB)],
                slots.at[chunk, pl.ds(index * ROWS, ROWS)],
                sems.at[chunk, index],
            )
    return copies


def picked_columns(table, arrays, slots, sems, order):
    return {
        (chunk, 0): Picked(
            table[8],
            *(
                read_columns(table, (array,), slots, sems, (chunk,))[chunk, 0]
                for array in arrays
            ),
        )
        for chunk in order
    }


@dataclasses.dataclass(frozen=True)
class Picked:
    core: jax.Array
    lower: object
    upper: object

    def start(self):
        pl.when(self.core == 0)(self.lower.start)
        pl.when(self.core == 1)(self.upper.start)

    def wait(self):
        self.lower.wait()


def chunks_of(pieces):
    return [
        piece.at[pl.ds(start, SUB)] for piece in pieces for start in range(0, piece.shape[0], SUB)
    ]


def read_pieces(pieces, slots, sems):
    return [
        pltpu.make_async_copy(chunk, slots.at[index], sems.at[index])
        for index, chunk in enumerate(chunks_of(pieces))
    ]


def layer_kernel(plan, *refs):
    refs = list(refs)

    def take(count):
        taken, refs[:count] = refs[:count], []
        return taken

    (table,) = take(1)
    blocks = take(plan.blocks + plan.picks)
    mine, theirs = take(2) if plan.last else (None, None)
    last = take(plan.last)
    begun = take(1) if plan.adds else []
    after = take(plan.after)
    fresh = take(plan.blocks) if plan.last else []
    out = take(1) if plan.after else []
    columns, column_sems = take(2)
    last_slots, last_sems = take(2) if plan.last else (None, None)
    after_slots, after_sems = take(2) if plan.after else (None, None)
    (store_sems,) = take(1) if plan.last else (None,)

    taken_up = range(plan.first, plan.first + plan.count)
    chunks = range(8) if plan.last else taken_up
    read = picked_columns if plan.picks else read_columns
    reads = read(table, blocks, columns, column_sems, chunks)
    last_reads = read_pieces(last, last_slots, last_sems) if plan.last else []
    after_reads = read_pieces(after, after_slots, after_sems) if plan.after else []

    def begin(chunk):
        if chunk not in chunks:
            return
        for index in range(plan.blocks):
            reads[chunk, index].start()
        if plan.last:
            last_reads[chunk].start()
        if chunk in taken_up:
            after_reads[chunk - plan.first].start()

    for ahead in range(AHEAD):
        begin(chunks[0] + ahead)
    rows = plan.blocks * ROWS
    if plan.last:
        summed = mine[...] + theirs[...]
        scale = lax.rsqrt(summed[:, KVW : KVW + 1] * (1.0 / D) + norm_eps)
        projected = (summed[:, :KVW] * scale).astype(jnp.bfloat16)
    skip = plan.skip * ROWS
    if plan.after:
        total = jnp.zeros((rows - skip, KVW), jnp.float32)
        squares = jnp.zeros((rows - skip, 1), jnp.float32)
        if plan.adds:
            total += begun[0][:, :KVW]
            squares += begun[0][:, KVW : KVW + 1]
    stores = []
    for chunk in chunks:
        begin(chunk + AHEAD)
        for index in range(plan.blocks):
            reads[chunk, index].wait()
        part = columns[chunk]
        if plan.last:
            last_reads[chunk].wait()
            update = lax.dot_general(
                projected,
                last_slots[chunk],
                (((1,), (1,)), ((), ())),
                preferred_element_type=jnp.float32,
            )
            part = (part.astype(jnp.float32) + update).astype(jnp.bfloat16)
            columns[chunk] = part
            column = pl.multiple_of(table[chunk], SUB)
            if plan.swaps:
                own = table[8]
                sources = [own * ROWS, (1 - own) * ROWS]
            else:
                sources = [index * ROWS for index in range(plan.blocks)]
            for index in range(plan.blocks):
                stores.append(
                    pltpu.make_async_copy(
                        columns.at[chunk, pl.ds(sources[index], ROWS)],
                        fresh[index].at[:, pl.ds(column, SUB)],
                        store_sems.at[chunk, index],
                    )
                )
                stores[-1].start()
        if chunk in taken_up:
            after_reads[chunk - plan.first].wait()
            part = part[skip:]
            total += jnp.dot(
                part,
                after_slots[chunk - plan.first],
                preferred_element_type=jnp.float32,
            )
            flat = part.astype(jnp.float32)
            squares += jnp.sum(flat * flat, axis=1, keepdims=True)
    if plan.after:
        out[0][:, :KVW] = total
        out[0][:, KVW:] = jnp.broadcast_to(squares, (rows - skip, LANES))
    for store in stores:
        store.wait()


@dataclasses.dataclass(frozen=True)
class Plan:
    blocks: int
    last: int
    after: int
    first: int = 0
    count: int = 0
    adds: bool = False
    skip: int = 0
    swaps: bool = False
    picks: bool = False


def layer_call(table, blocks, sums=(), last=(), begun=(), after=(), name="layer", **plan):
    count = sum(piece.shape[0] for piece in after) // SUB
    picks = plan.get("picks", False)
    plan = Plan(len(blocks) - picks, len(last), len(after), count=count, adds=len(begun) > 0, **plan)
    rows = plan.blocks * ROWS
    any_space = pl.BlockSpec(memory_space=pl.ANY)
    vmem = pl.BlockSpec(memory_space=pltpu.VMEM)
    out_shape, out_specs = [], []
    scratch = [
        pltpu.VMEM((8, rows, SUB), jnp.bfloat16),
        pltpu.SemaphoreType.DMA((8, plan.blocks)),
    ]
    if plan.last:
        out_shape += [jax.ShapeDtypeStruct((ROWS, HALF), jnp.bfloat16)] * plan.blocks
        out_specs += [any_space] * plan.blocks
        scratch += [pltpu.VMEM((8, SUB, KVW), jnp.bfloat16), pltpu.SemaphoreType.DMA((8,))]
    if plan.after:
        out_shape.append(jax.ShapeDtypeStruct((rows - plan.skip * ROWS, KVW + LANES), jnp.float32))
        out_specs.append(vmem)
        scratch += [
            pltpu.VMEM((plan.count, SUB, KVW), jnp.bfloat16),
            pltpu.SemaphoreType.DMA((plan.count,)),
        ]
    if plan.last:
        scratch.append(pltpu.SemaphoreType.DMA((8, plan.blocks)))
    flops = 2 * SUB * KVW * (rows * 8 * (plan.last > 0) + (rows - plan.skip * ROWS) * count)
    moved = (2 << 20) * plan.blocks * (1 + (plan.last > 0)) + (4 << 20) * (plan.last > 0)
    moved += count << 19
    return pl.pallas_call(
        functools.partial(layer_kernel, plan),
        in_specs=[pl.BlockSpec(memory_space=pltpu.SMEM)]
        + [any_space] * len(blocks)
        + [vmem] * len(sums)
        + [any_space] * len(last)
        + [vmem] * len(begun)
        + [any_space] * len(after),
        out_specs=out_specs,
        out_shape=out_shape,
        scratch_shapes=scratch,
        compiler_params=pltpu.CompilerParams(vmem_limit_bytes=VMEM),
        cost_estimate=pl.CostEstimate(flops=flops, bytes_accessed=moved, transcendentals=0),
        name=name,
    )(table, *blocks, *sums, *last, *begun, *after)


def final_kernel(table, keep, got, mine, theirs, *refs):
    pieces, (whole, slots, slot_sems, w_slots, w_sems, store_sems) = refs[:-6], refs[-6:]
    upper = table[8] == 1
    reads, stores = [], []
    for chunk in range(16):
        source = keep if chunk < 8 else got
        column = pl.multiple_of(table[(0 if chunk < 8 else 16) + chunk % 8], SUB)
        reads.append(
            pltpu.make_async_copy(
                source.at[:, pl.ds(column, SUB)], slots.at[chunk], slot_sems.at[chunk]
            )
        )
        side = table[8] if chunk < 8 else 1 - table[8]
        target = pl.multiple_of(2 * column + side * SUB, SUB)
        stores.append(
            pltpu.make_async_copy(
                slots.at[chunk], whole.at[:, pl.ds(target, SUB)], store_sems.at[chunk]
            )
        )
    weights = read_pieces(pieces, w_slots, w_sems)

    def begin(chunk):
        if chunk < 16:
            reads[chunk].start()
            weights[chunk].start()

    for ahead in range(2 * AHEAD):
        begin(ahead)
    summed = mine[...] + theirs[...]
    scale = lax.rsqrt(summed[:, KVW : KVW + 1] * (1.0 / D) + norm_eps)
    projected = (summed[:, :KVW] * scale).astype(jnp.bfloat16)
    for chunk in range(16):
        begin(chunk + 2 * AHEAD)
        reads[chunk].wait()
        weights[chunk].wait()

        @pl.when(upper)
        def _():
            update = lax.dot_general(
                projected,
                w_slots[chunk],
                (((1,), (1,)), ((), ())),
                preferred_element_type=jnp.float32,
            )
            slots[chunk] = (slots[chunk].astype(jnp.float32) + update).astype(jnp.bfloat16)

        stores[chunk].start()
    for store in stores:
        store.wait()


def final_call(table, keep, got, mine, theirs, here, there):
    any_space = pl.BlockSpec(memory_space=pl.ANY)
    vmem = pl.BlockSpec(memory_space=pltpu.VMEM)
    return pl.pallas_call(
        final_kernel,
        in_specs=[pl.BlockSpec(memory_space=pltpu.SMEM), any_space, any_space, vmem, vmem]
        + [any_space] * (len(here) + len(there)),
        out_specs=any_space,
        out_shape=jax.ShapeDtypeStruct((ROWS, D), jnp.bfloat16),
        scratch_shapes=[
            pltpu.VMEM((16, ROWS, SUB), jnp.bfloat16),
            pltpu.SemaphoreType.DMA((16,)),
            pltpu.VMEM((16, SUB, KVW), jnp.bfloat16),
            pltpu.SemaphoreType.DMA((16,)),
            pltpu.SemaphoreType.DMA((16,)),
        ],
        compiler_params=pltpu.CompilerParams(vmem_limit_bytes=VMEM),
        cost_estimate=pl.CostEstimate(
            flops=2 * ROWS * D * KVW, bytes_accessed=16 << 20, transcendentals=0
        ),
        name="final_layer",
    )(table, keep, got, mine, theirs, *here, *there)


def after(value, *events):
    return lax.optimization_barrier((value, *events))[0]


def together(own, other):
    return jnp.concatenate([own, other], axis=0)


def per_device(master_weights, first_moment, second_moment, gradient_shard, hidden_states):
    core = lax.rem(lax.axis_index("section"), 2)
    xlo = lax.div(lax.axis_index("dp"), 4)
    z = lax.rem(lax.axis_index("dp"), 4)
    upper = core == 1
    core_word = jnp.reshape(core, (1,)).astype(jnp.int32)
    step = jnp.arange(4, dtype=jnp.int32)

    def columns(is_upper):
        owner = lax.rem(z + jnp.where(is_upper, step, 4 - step), 4)
        return jnp.stack([owner + 4 * xlo, owner + 4 * (1 - xlo)], axis=1).reshape(8) * SUB

    filler = jnp.zeros((7,), jnp.int32)
    table = jnp.concatenate([columns(upper), core_word, filler, columns(~upper)]).astype(jnp.int32)

    states, mine, theirs, keep, give = update_call(
        core_word,
        master_weights,
        first_moment,
        second_moment,
        gradient_shard,
        hidden_states.reshape(ROWS, D),
    )
    other = to_core(theirs)
    even_rows = jnp.where(upper, other, mine)
    odd_rows = jnp.where(upper, mine, other)
    got = to_core(after(give, other))

    home_own = [even_rows, to_ring(even_rows)]
    home_other = to_pair(even_rows)
    near_odd = to_chip(odd_rows, 1)
    odd = to_next(jnp.where(upper, keep, got), 0)

    phase = (home_own[1], home_other, near_odd)
    home_own.append(to_ring(after(home_own[1], *phase)))
    home_others = [after(home_other, *phase)]
    home_others.append(to_ring(home_others[0]))
    far = to_chip(after(near_odd, *phase), 1)
    near_even = to_chip(after(even_rows, *phase), 1)

    phase = (home_own[2], home_others[1], far)
    home_own.append(to_ring(after(home_own[2], *phase)))
    home_others.append(to_ring(after(home_others[1], *phase)))
    far = after(far, *phase)
    far_other = to_pair(far)

    phase = (home_own[3], home_others[2], far_other, odd)
    home_others.append(to_ring(after(home_others[2], *phase)))
    first = [after(together(far, far_other), *phase)]
    first.append(to_ring(first[0]))
    odd = to_next(after(odd, *phase), 1)

    home = [piece for pair in zip(home_own, home_others) for piece in pair]
    (product,) = layer_call(table, (keep, got), after=home, picks=True, name="project_home")
    phase = (first[1], home_others[3], near_even)
    first.append(to_ring(after(first[1], *phase)))
    second_own = [after(near_even, *phase)]
    second_own.append(to_ring(second_own[0]))
    second_others = [to_pair(second_own[0])]
    (even,) = layer_call(
        table,
        (keep, got),
        sums=(product, to_core(after(product, *phase))),
        last=home,
        picks=True,
        name="expand_home",
    )
    even = to_next(even, 0)
    third_other = to_pair(after(near_odd, even))

    phase = (first[2], second_own[1], odd)
    first.append(to_ring(after(first[2], *phase)))
    second_own.append(to_ring(after(second_own[1], *phase)))
    second_others.append(to_pair(second_own[1]))
    home_there = to_core(jnp.concatenate([after(piece, *phase) for piece in home], axis=0))

    phase = (first[3], second_own[2], even, third_other, second_others[0])
    even = to_next(after(even, *phase), 1)
    third = [after(together(near_odd, third_other), *phase)]
    third.append(to_ring(third[0]))
    second_own.append(to_ring(after(second_own[2], *phase)))
    second_others.append(to_pair(after(second_own[2], *phase)))

    phase = (third[1], second_own[3], home_there, second_others[1])
    third.append(to_ring(after(third[1], *phase)))
    second_others.append(to_pair(after(second_own[3], *phase)))
    second = [piece for pair in zip(second_own, second_others) for piece in pair]
    even = after(even, *phase, second_others[2])
    third.append(to_ring(third[2]))

    (product,) = layer_call(table, (even, odd), after=first, name="project_first")
    even, odd, product = layer_call(
        table,
        (even, odd),
        sums=(product, to_core(product)),
        last=first,
        after=second,
        name="first_second",
    )
    even, odd, product = layer_call(
        table,
        (even, odd),
        sums=(product, to_core(product)),
        last=second,
        after=third[:3],
        name="second_third",
    )
    (product,) = layer_call(
        table, (even, odd), begun=(product,), after=third[3:], first=6, name="third_rest"
    )
    keep, give, product = layer_call(
        table,
        (even, odd),
        sums=(product, to_core(product)),
        last=third,
        after=home,
        skip=1,
        swaps=True,
        name="third_home",
    )
    out = final_call(
        table, keep, to_core(give), product, to_core(product), home, [home_there]
    )
    return (*states, out.reshape(hidden_states.shape))


def solution(mesh):
    placed = (
        P("section", "dp", None),
        P("section", "dp", None),
        P("section", "dp", None),
        P("section", "dp", None),
        P("section", None, "dp", None),
    )
    return jax.shard_map(
        per_device,
        mesh=mesh,
        in_specs=placed,
        out_specs=(
            P("section", "dp", None),
            P("section", "dp", None),
            P("section", "dp", None),
            P("section", None, "dp", None),
        ),
        check_vma=False,
    )
```

```python
import dataclasses
import functools

import jax
import jax.numpy as jnp
from jax import lax
from jax.experimental import pallas as pl
from jax.experimental.pallas import tpu as pltpu
from jax.sharding import PartitionSpec as P

ADAM_STEP = 1000

beta_one = 0.9
beta_two = 0.95
learn_rate = 0.0003
decay_rate = 0.1
adam_eps = 1e-08
norm_eps = 1e-05

AXES = ("section", "dp")
D = 8192
KVW = 512
ROWS = 256
SUB = 512
HALF = D // 2
LANES = 128
VMEM = 56 * 1024 * 1024
UPDATE_STEPS = 8
SUB_STEP = SUB // UPDATE_STEPS
COST = pl.CostEstimate(flops=1, bytes_accessed=1, transcendentals=0)
AHEAD = 3


def place(linear):
    section, dp = divmod(linear, 8)
    return section // 2, section % 2, dp // 4, dp % 4


def linear_of(chip, core, xlo, z):
    return ((chip % 8) * 2 + core) * 8 + (xlo % 2) * 4 + z % 4


def shift(value, move):
    pairs = [(source, linear_of(*move(*place(source)))) for source in range(128)]
    return lax.ppermute(value, AXES, pairs)


def to_core(value):
    return shift(value, lambda chip, core, xlo, z: (chip, 1 - core, xlo, z))


def to_pair(value):
    return shift(value, lambda chip, core, xlo, z: (chip, core, xlo + 1, z))


def to_ring(value):
    return shift(value, lambda chip, core, xlo, z: (chip, core, xlo, z + 1 - 2 * core))


def to_chip(value, steps):
    return shift(value, lambda chip, core, xlo, z: (chip + steps, core, xlo, z))


def adamw_update(master, moment, second, gradient):
    moment_new = beta_one * moment + (1.0 - beta_one) * gradient
    second_new = beta_two * second + (1.0 - beta_two) * gradient * gradient
    corr_one = 1.0 - beta_one**ADAM_STEP
    corr_two = 1.0 - beta_two**ADAM_STEP
    step_size = moment_new / corr_one / (jnp.sqrt(second_new / corr_two) + adam_eps)
    master_new = master - learn_rate * (step_size + decay_rate * master)
    return (master_new, moment_new, second_new)


def update_kernel(
    core_ref,
    master_ref,
    moment_ref,
    second_ref,
    gradient_ref,
    whole_ref,
    master_out,
    moment_out,
    second_out,
    keep_rows,
    give_rows,
    keep,
    give,
):
    lower = core_ref[0] == 0
    new_master, new_moment, new_second = adamw_update(
        master_ref[...], moment_ref[...], second_ref[...], gradient_ref[...]
    )
    master_out[...] = new_master
    moment_out[...] = new_moment
    second_out[...] = new_second
    first = new_master[0].astype(jnp.bfloat16)
    last = new_master[1].astype(jnp.bfloat16)
    keep_rows[...] = jnp.where(lower, first, last)
    give_rows[...] = jnp.where(lower, last, first)
    for part in range(8 // UPDATE_STEPS):
        first = whole_ref[:, 2 * part * SUB : (2 * part + 1) * SUB]
        last = whole_ref[:, (2 * part + 1) * SUB : (2 * part + 2) * SUB]
        keep[:, part * SUB : (part + 1) * SUB] = jnp.where(lower, first, last)
        give[:, part * SUB : (part + 1) * SUB] = jnp.where(lower, last, first)


def update_call(core, master, moment, second, gradient, whole):
    state = pl.BlockSpec((2, SUB_STEP, KVW), lambda i, core: (0, i, 0))
    half = pl.BlockSpec((SUB_STEP, KVW), lambda i, core: (i, 0))
    part = pl.BlockSpec((ROWS, HALF // UPDATE_STEPS), lambda i, core: (0, i))
    shaped = [a.reshape(2, SUB, KVW) for a in (master, moment, second, gradient)]
    outs = pl.pallas_call(
        update_kernel,
        grid_spec=pltpu.PrefetchScalarGridSpec(
            num_scalar_prefetch=1,
            grid=(UPDATE_STEPS,),
            in_specs=[state] * 4
            + [pl.BlockSpec((ROWS, D // UPDATE_STEPS), lambda i, core: (0, i))],
            out_specs=[state] * 3 + [half] * 2 + [part] * 2,
        ),
        out_shape=[jax.ShapeDtypeStruct((2, SUB, KVW), jnp.float32)] * 3
        + [jax.ShapeDtypeStruct((SUB, KVW), jnp.bfloat16)] * 2
        + [jax.ShapeDtypeStruct((ROWS, HALF), jnp.bfloat16)] * 2,
        compiler_params=pltpu.CompilerParams(vmem_limit_bytes=VMEM),
        cost_estimate=COST,
        name="update",
    )(core, *shaped, whole)
    return [a.reshape(master.shape) for a in outs[:3]], *outs[3:]


def read_columns(table, blocks, slots, sems, order):
    copies = {}
    for chunk in order:
        column = pl.multiple_of(table[chunk], SUB)
        for index, block in enumerate(blocks):
            copies[chunk, index] = pltpu.make_async_copy(
                block.at[:, pl.ds(column, SUB)],
                slots.at[chunk, pl.ds(index * ROWS, ROWS)],
                sems.at[chunk, index],
            )
    return copies


def picked_columns(table, arrays, slots, sems, order):
    return {
        (chunk, 0): Picked(
            table[8],
            *(
                read_columns(table, (array,), slots, sems, (chunk,))[chunk, 0]
                for array in arrays
            ),
        )
        for chunk in order
    }


@dataclasses.dataclass(frozen=True)
class Picked:
    core: jax.Array
    lower: object
    upper: object

    def start(self):
        pl.when(self.core == 0)(self.lower.start)
        pl.when(self.core == 1)(self.upper.start)

    def wait(self):
        self.lower.wait()


def chunks_of(pieces):
    return [
        piece.at[pl.ds(start, SUB)] for piece in pieces for start in range(0, piece.shape[0], SUB)
    ]


def read_pieces(pieces, slots, sems):
    return [
        pltpu.make_async_copy(chunk, slots.at[index], sems.at[index])
        for index, chunk in enumerate(chunks_of(pieces))
    ]


def layer_kernel(plan, *refs):
    refs = list(refs)

    def take(count):
        taken, refs[:count] = refs[:count], []
        return taken

    (table,) = take(1)
    blocks = take(plan.blocks + plan.picks)
    mine, theirs = take(2) if plan.last else (None, None)
    last = take(plan.last)
    begun = take(1) if plan.adds else []
    after = take(plan.after)
    fresh = take(plan.blocks) if plan.last else []
    kept = take(1) if plan.keeps else []
    out = take(1) if plan.after else []
    columns, column_sems = take(2)
    last_slots, last_sems = take(2) if plan.last else (None, None)
    after_slots, after_sems = take(2) if plan.after else (None, None)
    (store_sems,) = take(1) if plan.last else (None,)
    (keep_sems,) = take(1) if plan.keeps else (None,)

    taken_up = range(plan.first, plan.first + plan.count)
    chunks = range(8) if plan.last else taken_up
    read = picked_columns if plan.picks else read_columns
    reads = read(table, blocks, columns, column_sems, chunks)
    last_reads = read_pieces(last, last_slots, last_sems) if plan.last else []
    after_reads = read_pieces(after, after_slots, after_sems) if plan.after else []

    def begin(chunk):
        if chunk not in chunks:
            return
        for index in range(plan.blocks):
            reads[chunk, index].start()
        if plan.last:
            last_reads[chunk].start()
        if chunk in taken_up:
            after_reads[chunk - plan.first].start()

    for ahead in range(AHEAD):
        begin(chunks[0] + ahead)
    rows = plan.blocks * ROWS
    if plan.last:
        summed = mine[...] + theirs[...]
        scale = lax.rsqrt(summed[:, KVW : KVW + 1] * (1.0 / D) + norm_eps)
        projected = (summed[:, :KVW] * scale).astype(jnp.bfloat16)
    skip = plan.skip * ROWS
    if plan.after:
        total = jnp.zeros((rows - skip, KVW), jnp.float32)
        squares = jnp.zeros((rows - skip, 1), jnp.float32)
        if plan.adds:
            total += begun[0][:, :KVW]
            squares += begun[0][:, KVW : KVW + 1]
    stores = []
    for chunk in chunks:
        begin(chunk + AHEAD)
        for index in range(plan.blocks):
            reads[chunk, index].wait()
        part = columns[chunk]
        if plan.last:
            last_reads[chunk].wait()
            if plan.keeps:
                stores.append(
                    pltpu.make_async_copy(
                        last_slots.at[chunk],
                        kept[0].at[pl.ds(chunk * SUB, SUB)],
                        keep_sems.at[chunk],
                    )
                )
                stores[-1].start()
            update = lax.dot_general(
                projected,
                last_slots[chunk],
                (((1,), (1,)), ((), ())),
                preferred_element_type=jnp.float32,
            )
            part = (part.astype(jnp.float32) + update).astype(jnp.bfloat16)
            columns[chunk] = part
            column = pl.multiple_of(table[chunk], SUB)
            if plan.swaps:
                own = table[8]
                sources = [own * ROWS, (1 - own) * ROWS]
            else:
                sources = [index * ROWS for index in range(plan.blocks)]
            for index in range(plan.blocks):
                stores.append(
                    pltpu.make_async_copy(
                        columns.at[chunk, pl.ds(sources[index], ROWS)],
                        fresh[index].at[:, pl.ds(column, SUB)],
                        store_sems.at[chunk, index],
                    )
                )
                stores[-1].start()
        if chunk in taken_up:
            after_reads[chunk - plan.first].wait()
            part = part[skip:]
            total += jnp.dot(
                part,
                after_slots[chunk - plan.first],
                preferred_element_type=jnp.float32,
            )
            flat = part.astype(jnp.float32)
            squares += jnp.sum(flat * flat, axis=1, keepdims=True)
    if plan.after:
        out[0][:, :KVW] = total
        out[0][:, KVW:] = jnp.broadcast_to(squares, (rows - skip, LANES))
    for store in stores:
        store.wait()


@dataclasses.dataclass(frozen=True)
class Plan:
    blocks: int
    last: int
    after: int
    first: int = 0
    count: int = 0
    adds: bool = False
    skip: int = 0
    swaps: bool = False
    keeps: bool = False
    picks: bool = False


def layer_call(table, blocks, sums=(), last=(), begun=(), after=(), name="layer", **plan):
    count = sum(piece.shape[0] for piece in after) // SUB
    picks = plan.get("picks", False)
    plan = Plan(len(blocks) - picks, len(last), len(after), count=count, adds=len(begun) > 0, **plan)
    rows = plan.blocks * ROWS
    any_space = pl.BlockSpec(memory_space=pl.ANY)
    vmem = pl.BlockSpec(memory_space=pltpu.VMEM)
    out_shape, out_specs = [], []
    scratch = [
        pltpu.VMEM((8, rows, SUB), jnp.bfloat16),
        pltpu.SemaphoreType.DMA((8, plan.blocks)),
    ]
    if plan.last:
        out_shape += [jax.ShapeDtypeStruct((ROWS, HALF), jnp.bfloat16)] * plan.blocks
        out_specs += [any_space] * plan.blocks
        scratch += [pltpu.VMEM((8, SUB, KVW), jnp.bfloat16), pltpu.SemaphoreType.DMA((8,))]
    if plan.keeps:
        out_shape.append(jax.ShapeDtypeStruct((HALF, KVW), jnp.bfloat16))
        out_specs.append(any_space)
    if plan.after:
        out_shape.append(jax.ShapeDtypeStruct((rows - plan.skip * ROWS, KVW + LANES), jnp.float32))
        out_specs.append(vmem)
        scratch += [
            pltpu.VMEM((plan.count, SUB, KVW), jnp.bfloat16),
            pltpu.SemaphoreType.DMA((plan.count,)),
        ]
    if plan.last:
        scratch.append(pltpu.SemaphoreType.DMA((8, plan.blocks)))
    if plan.keeps:
        scratch.append(pltpu.SemaphoreType.DMA((8,)))
    return pl.pallas_call(
        functools.partial(layer_kernel, plan),
        in_specs=[pl.BlockSpec(memory_space=pltpu.SMEM)]
        + [any_space] * len(blocks)
        + [vmem] * len(sums)
        + [any_space] * len(last)
        + [vmem] * len(begun)
        + [any_space] * len(after),
        out_specs=out_specs,
        out_shape=out_shape,
        scratch_shapes=scratch,
        compiler_params=pltpu.CompilerParams(vmem_limit_bytes=VMEM),
        cost_estimate=COST,
        name=name,
    )(table, *blocks, *sums, *last, *begun, *after)


def final_kernel(table, keep, got, mine, theirs, *refs):
    pieces, (whole, slots, slot_sems, w_slots, w_sems, store_sems) = refs[:-6], refs[-6:]
    upper = table[8] == 1
    reads, stores = [], []
    for chunk in range(16):
        source = keep if chunk < 8 else got
        column = pl.multiple_of(table[(0 if chunk < 8 else 16) + chunk % 8], SUB)
        reads.append(
            pltpu.make_async_copy(
                source.at[:, pl.ds(column, SUB)], slots.at[chunk], slot_sems.at[chunk]
            )
        )
        side = table[8] if chunk < 8 else 1 - table[8]
        target = pl.multiple_of(2 * column + side * SUB, SUB)
        stores.append(
            pltpu.make_async_copy(
                slots.at[chunk], whole.at[:, pl.ds(target, SUB)], store_sems.at[chunk]
            )
        )
    weights = read_pieces(pieces, w_slots, w_sems)

    def begin(chunk):
        if chunk < 16:
            reads[chunk].start()
            weights[chunk].start()

    for ahead in range(2 * AHEAD):
        begin(ahead)
    summed = mine[...] + theirs[...]
    scale = lax.rsqrt(summed[:, KVW : KVW + 1] * (1.0 / D) + norm_eps)
    projected = (summed[:, :KVW] * scale).astype(jnp.bfloat16)
    for chunk in range(16):
        begin(chunk + 2 * AHEAD)
        reads[chunk].wait()
        weights[chunk].wait()

        @pl.when(upper)
        def _():
            update = lax.dot_general(
                projected,
                w_slots[chunk],
                (((1,), (1,)), ((), ())),
                preferred_element_type=jnp.float32,
            )
            slots[chunk] = (slots[chunk].astype(jnp.float32) + update).astype(jnp.bfloat16)

        stores[chunk].start()
    for store in stores:
        store.wait()


def final_call(table, keep, got, mine, theirs, here, there):
    any_space = pl.BlockSpec(memory_space=pl.ANY)
    vmem = pl.BlockSpec(memory_space=pltpu.VMEM)
    return pl.pallas_call(
        final_kernel,
        in_specs=[pl.BlockSpec(memory_space=pltpu.SMEM), any_space, any_space, vmem, vmem]
        + [any_space] * (len(here) + len(there)),
        out_specs=any_space,
        out_shape=jax.ShapeDtypeStruct((ROWS, D), jnp.bfloat16),
        scratch_shapes=[
            pltpu.VMEM((16, ROWS, SUB), jnp.bfloat16),
            pltpu.SemaphoreType.DMA((16,)),
            pltpu.VMEM((16, SUB, KVW), jnp.bfloat16),
            pltpu.SemaphoreType.DMA((16,)),
            pltpu.SemaphoreType.DMA((16,)),
        ],
        compiler_params=pltpu.CompilerParams(vmem_limit_bytes=VMEM),
        cost_estimate=COST,
        name="final_layer",
    )(table, keep, got, mine, theirs, *here, *there)


def after(value, *events):
    return lax.optimization_barrier((value, *events))[0]


def together(own, other):
    return jnp.concatenate([own, other], axis=0)


def per_device(master_weights, first_moment, second_moment, gradient_shard, hidden_states):
    core = lax.rem(lax.axis_index("section"), 2)
    xlo = lax.div(lax.axis_index("dp"), 4)
    z = lax.rem(lax.axis_index("dp"), 4)
    upper = core == 1
    core_word = jnp.reshape(core, (1,)).astype(jnp.int32)
    step = jnp.arange(4, dtype=jnp.int32)

    def columns(is_upper):
        owner = lax.rem(z + jnp.where(is_upper, step, 4 - step), 4)
        return jnp.stack([owner + 4 * xlo, owner + 4 * (1 - xlo)], axis=1).reshape(8) * SUB

    filler = jnp.zeros((7,), jnp.int32)
    table = jnp.concatenate([columns(upper), core_word, filler, columns(~upper)]).astype(jnp.int32)

    states, mine, theirs, keep, give = update_call(
        core_word,
        master_weights,
        first_moment,
        second_moment,
        gradient_shard,
        hidden_states.reshape(ROWS, D),
    )
    other = to_core(theirs)
    even_rows = jnp.where(upper, other, mine)
    odd_rows = jnp.where(upper, mine, other)
    got = to_core(after(give, other))

    home_own = [even_rows, to_ring(even_rows)]
    home_other = to_pair(even_rows)
    near_odd = to_chip(odd_rows, 1)

    phase = (home_own[1], home_other, near_odd)
    home_own.append(to_ring(after(home_own[1], *phase)))
    home_others = [after(home_other, *phase)]
    home_others.append(to_ring(home_others[0]))
    near_odd = after(near_odd, *phase)
    far = to_chip(near_odd, 1)
    third_other = to_pair(near_odd)
    odd = jnp.where(upper, keep, got)

    phase = (home_own[2], home_others[1], far, third_other, odd)
    home_own.append(to_ring(after(home_own[2], *phase)))
    home_others.append(to_ring(after(home_others[1], *phase)))
    far = after(far, *phase)
    far_other = to_pair(far)
    near_even = to_chip(after(even_rows, *phase), 1)
    odd = to_chip(after(odd, *phase), 2)

    phase = (home_own[3], home_others[2], far_other, near_even)
    home_others.append(to_ring(after(home_others[2], *phase)))
    first = [after(together(far, far_other), *phase)]
    first.append(to_ring(first[0]))
    near_even = after(near_even, *phase)
    second_other = to_pair(near_even)
    third = [together(near_odd, third_other)]

    home = [piece for pair in zip(home_own, home_others) for piece in pair]
    (product,) = layer_call(table, (keep, got), after=home, picks=True, name="project_home")
    phase = (first[1], home_others[3], second_other)
    first.append(to_ring(after(first[1], *phase)))
    second = [after(together(near_even, second_other), *phase)]
    second.append(to_ring(second[0]))
    even, home_here = layer_call(
        table,
        (keep, got),
        sums=(product, to_core(after(product, *phase))),
        last=home,
        picks=True,
        keeps=True,
        name="expand_home",
    )
    phase = (first[2], second[1], odd, even, third[0])
    even = to_chip(even, 2)
    home_there = to_core(after(home_here, *phase))
    first.append(to_ring(after(first[2], *phase)))
    second.append(to_ring(after(second[1], *phase)))

    phase = (first[3], second[2])
    second.append(to_ring(after(second[2], *phase)))
    third.append(to_ring(after(third[0], *phase)))

    even = after(even, second[3])
    phase = (second[3], third[1], home_there)
    third.append(to_ring(after(third[1], *phase)))
    third.append(to_ring(third[2]))

    (product,) = layer_call(table, (even, odd), after=first, name="project_first")
    even, odd, product = layer_call(
        table,
        (even, odd),
        sums=(product, to_core(product)),
        last=first,
        after=second,
        name="first_second",
    )
    even, odd, product = layer_call(
        table,
        (even, odd),
        sums=(product, to_core(product)),
        last=second,
        after=third[:3],
        name="second_third",
    )
    (product,) = layer_call(
        table, (even, odd), begun=(product,), after=third[3:], first=6, name="third_rest"
    )
    keep, give, product = layer_call(
        table,
        (even, odd),
        sums=(product, to_core(product)),
        last=third,
        after=[home_here],
        skip=1,
        swaps=True,
        name="third_home",
    )
    out = final_call(
        table, keep, to_core(give), product, to_core(product), [home_here], [home_there]
    )
    return (*states, out.reshape(hidden_states.shape))


def solution(mesh):
    placed = (
        P("section", "dp", None),
        P("section", "dp", None),
        P("section", "dp", None),
        P("section", "dp", None),
        P("section", None, "dp", None),
    )
    return jax.shard_map(
        per_device,
        mesh=mesh,
        in_specs=placed,
        out_specs=(
            P("section", "dp", None),
            P("section", "dp", None),
            P("section", "dp", None),
            P("section", None, "dp", None),
        ),
        check_vma=False,
    )
```

```python
import dataclasses
import functools

import jax
import jax.numpy as jnp
from jax import lax
from jax.experimental import pallas as pl
from jax.experimental.pallas import tpu as pltpu
from jax.sharding import PartitionSpec as P

ADAM_STEP = 1000

beta_one = 0.9
beta_two = 0.95
learn_rate = 0.0003
decay_rate = 0.1
adam_eps = 1e-08
norm_eps = 1e-05

AXES = ("section", "dp")
D = 8192
KVW = 512
ROWS = 256
SUB = 512
HALF = D // 2
LANES = 128
VMEM = 56 * 1024 * 1024
UPDATE_STEPS = 8
SUB_STEP = SUB // UPDATE_STEPS
COST = pl.CostEstimate(flops=1, bytes_accessed=1, transcendentals=0)
AHEAD = 3


def place(linear):
    section, dp = divmod(linear, 8)
    return section // 2, section % 2, dp // 4, dp % 4


def linear_of(chip, core, xlo, z):
    return ((chip % 8) * 2 + core) * 8 + (xlo % 2) * 4 + z % 4


def shift(value, move):
    pairs = [(source, linear_of(*move(*place(source)))) for source in range(128)]
    return lax.ppermute(value, AXES, pairs)


def to_core(value):
    return shift(value, lambda chip, core, xlo, z: (chip, 1 - core, xlo, z))


def to_pair(value):
    return shift(value, lambda chip, core, xlo, z: (chip, core, xlo + 1, z))


def to_ring(value):
    return shift(value, lambda chip, core, xlo, z: (chip, core, xlo, z + 1 - 2 * core))


def to_chip(value, steps):
    return shift(value, lambda chip, core, xlo, z: (chip + steps, core, xlo, z))


def to_next_pair(value):
    def move(chip, core, xlo, z):
        return chip + 1, core, xlo + (chip % 4 == 3), z

    return shift(value, move)


def to_next(value, hop):
    def move(chip, core, xlo, z):
        xhi, y = divmod(chip, 4)
        start = (y - hop + 2 * hop * core) % 4
        if start >= 2 and hop == ((start + core) % 2):
            xhi = 1 - xhi
        return xhi * 4 + (y + 1 - 2 * core) % 4, core, xlo, z

    return shift(value, move)


def adamw_update(master, moment, second, gradient):
    moment_new = beta_one * moment + (1.0 - beta_one) * gradient
    second_new = beta_two * second + (1.0 - beta_two) * gradient * gradient
    corr_one = 1.0 - beta_one**ADAM_STEP
    corr_two = 1.0 - beta_two**ADAM_STEP
    step_size = moment_new / corr_one / (jnp.sqrt(second_new / corr_two) + adam_eps)
    master_new = master - learn_rate * (step_size + decay_rate * master)
    return (master_new, moment_new, second_new)


def update_kernel(
    core_ref,
    master_ref,
    moment_ref,
    second_ref,
    gradient_ref,
    whole_ref,
    master_out,
    moment_out,
    second_out,
    keep_rows,
    give_rows,
    keep,
    give,
):
    lower = core_ref[0] == 0
    new_master, new_moment, new_second = adamw_update(
        master_ref[...], moment_ref[...], second_ref[...], gradient_ref[...]
    )
    master_out[...] = new_master
    moment_out[...] = new_moment
    second_out[...] = new_second
    first = new_master[0].astype(jnp.bfloat16)
    last = new_master[1].astype(jnp.bfloat16)
    keep_rows[...] = jnp.where(lower, first, last)
    give_rows[...] = jnp.where(lower, last, first)
    for part in range(8 // UPDATE_STEPS):
        first = whole_ref[:, 2 * part * SUB : (2 * part + 1) * SUB]
        last = whole_ref[:, (2 * part + 1) * SUB : (2 * part + 2) * SUB]
        keep[:, part * SUB : (part + 1) * SUB] = jnp.where(lower, first, last)
        give[:, part * SUB : (part + 1) * SUB] = jnp.where(lower, last, first)


def update_call(core, master, moment, second, gradient, whole):
    state = pl.BlockSpec((2, SUB_STEP, KVW), lambda i, core: (0, i, 0))
    half = pl.BlockSpec((SUB_STEP, KVW), lambda i, core: (i, 0))
    part = pl.BlockSpec((ROWS, HALF // UPDATE_STEPS), lambda i, core: (0, i))
    shaped = [a.reshape(2, SUB, KVW) for a in (master, moment, second, gradient)]
    outs = pl.pallas_call(
        update_kernel,
        grid_spec=pltpu.PrefetchScalarGridSpec(
            num_scalar_prefetch=1,
            grid=(UPDATE_STEPS,),
            in_specs=[state] * 4
            + [pl.BlockSpec((ROWS, D // UPDATE_STEPS), lambda i, core: (0, i))],
            out_specs=[state] * 3 + [half] * 2 + [part] * 2,
        ),
        out_shape=[jax.ShapeDtypeStruct((2, SUB, KVW), jnp.float32)] * 3
        + [jax.ShapeDtypeStruct((SUB, KVW), jnp.bfloat16)] * 2
        + [jax.ShapeDtypeStruct((ROWS, HALF), jnp.bfloat16)] * 2,
        compiler_params=pltpu.CompilerParams(vmem_limit_bytes=VMEM),
        cost_estimate=COST,
        name="update",
    )(core, *shaped, whole)
    return [a.reshape(master.shape) for a in outs[:3]], *outs[3:]


def read_columns(table, blocks, slots, sems, order):
    copies = {}
    for chunk in order:
        column = pl.multiple_of(table[chunk], SUB)
        for index, block in enumerate(blocks):
            copies[chunk, index] = pltpu.make_async_copy(
                block.at[:, pl.ds(column, SUB)],
                slots.at[chunk, pl.ds(index * ROWS, ROWS)],
                sems.at[chunk, index],
            )
    return copies


def picked_columns(table, arrays, slots, sems, order):
    return {
        (chunk, 0): Picked(
            table[8],
            *(
                read_columns(table, (array,), slots, sems, (chunk,))[chunk, 0]
                for array in arrays
            ),
        )
        for chunk in order
    }


@dataclasses.dataclass(frozen=True)
class Picked:
    core: jax.Array
    lower: object
    upper: object

    def start(self):
        pl.when(self.core == 0)(self.lower.start)
        pl.when(self.core == 1)(self.upper.start)

    def wait(self):
        self.lower.wait()


def chunks_of(pieces, flip):
    for piece in pieces:
        for start in range(0, piece.shape[0], SUB):
            if flip is not None and piece.shape[0] == 2 * SUB:
                start = pl.multiple_of(start + flip * (SUB - 2 * start), SUB)
            yield piece.at[pl.ds(start, SUB)]


def read_pieces(pieces, slots, sems, flip=None):
    return [
        pltpu.make_async_copy(chunk, slots.at[index], sems.at[index])
        for index, chunk in enumerate(chunks_of(pieces, flip))
    ]


def projected_of(mine, theirs):
    summed = mine[...] + theirs[...]
    scale = lax.rsqrt(summed[:, KVW : KVW + 1] * (1.0 / D) + norm_eps)
    return (summed[:, :KVW] * scale).astype(jnp.bfloat16)


def layer_kernel(plan, *refs):
    refs = list(refs)

    def take(count):
        taken, refs[:count] = refs[:count], []
        return taken

    (table,) = take(1)
    blocks = take(plan.blocks + plan.picks)
    mine = take(plan.blocks if plan.last else 0)
    theirs = take(plan.blocks if plan.last else 0)
    last = take(plan.last)
    after = take(plan.after)
    fresh = take(plan.blocks) if plan.last else []
    kept = take(1) if plan.keeps else []
    out = take(plan.blocks - plan.skip if plan.after else 0)
    columns, column_sems = take(2)
    last_slots, last_sems = take(2) if plan.last else (None, None)
    after_slots, after_sems = take(2) if plan.after else (None, None)
    (store_sems,) = take(1) if plan.last else (None,)
    (keep_sems,) = take(1) if plan.keeps else (None,)

    taken_up = range(plan.first, plan.first + plan.count)
    chunks = range(8) if plan.last else taken_up
    read = picked_columns if plan.picks else read_columns
    reads = read(table, blocks, columns, column_sems, chunks)
    flips = [None if at is None else table[at] for at in (plan.last_flip, plan.after_flip)]
    last_reads = read_pieces(last, last_slots, last_sems, flips[0]) if plan.last else []
    after_reads = read_pieces(after, after_slots, after_sems, flips[1]) if plan.after else []

    def begin(chunk):
        if chunk not in chunks:
            return
        for index in range(plan.blocks):
            reads[chunk, index].start()
        if plan.last:
            last_reads[chunk].start()
        if chunk in taken_up:
            after_reads[chunk - plan.first].start()

    for ahead in range(AHEAD):
        begin(chunks[0] + ahead)
    rows = plan.blocks * ROWS
    if plan.last:
        projected = jnp.concatenate(
            [projected_of(here, there) for here, there in zip(mine, theirs)], axis=0
        )
    skip = plan.skip * ROWS
    if plan.after:
        total = jnp.zeros((rows - skip, KVW), jnp.float32)
        squares = jnp.zeros((rows - skip, 1), jnp.float32)
    stores = []
    for chunk in chunks:
        begin(chunk + AHEAD)
        for index in range(plan.blocks):
            reads[chunk, index].wait()
        part = columns[chunk]
        if plan.last:
            last_reads[chunk].wait()
            if plan.keeps:
                stores.append(
                    pltpu.make_async_copy(
                        last_slots.at[chunk],
                        kept[0].at[pl.ds(chunk * SUB, SUB)],
                        keep_sems.at[chunk],
                    )
                )
                stores[-1].start()
            update = lax.dot_general(
                projected,
                last_slots[chunk],
                (((1,), (1,)), ((), ())),
                preferred_element_type=jnp.float32,
            )
            part = (part.astype(jnp.float32) + update).astype(jnp.bfloat16)
            columns[chunk] = part
            column = pl.multiple_of(table[chunk], SUB)
            if plan.swaps:
                own = table[8]
                sources = [own * ROWS, (1 - own) * ROWS]
            else:
                sources = [index * ROWS for index in range(plan.blocks)]
            for index in range(plan.blocks):
                stores.append(
                    pltpu.make_async_copy(
                        columns.at[chunk, pl.ds(sources[index], ROWS)],
                        fresh[index].at[:, pl.ds(column, SUB)],
                        store_sems.at[chunk, index],
                    )
                )
                stores[-1].start()
        if chunk in taken_up:
            after_reads[chunk - plan.first].wait()
            part = part[skip:]
            total += jnp.dot(
                part,
                after_slots[chunk - plan.first],
                preferred_element_type=jnp.float32,
            )
            flat = part.astype(jnp.float32)
            squares += jnp.sum(flat * flat, axis=1, keepdims=True)
    if plan.after:
        for index, product in enumerate(out):
            part = slice(index * ROWS, (index + 1) * ROWS)
            product[:, :KVW] = total[part]
            product[:, KVW:] = jnp.broadcast_to(squares[part], (ROWS, LANES))
    for store in stores:
        store.wait()


@dataclasses.dataclass(frozen=True)
class Plan:
    blocks: int
    last: int
    after: int
    first: int = 0
    count: int = 0
    skip: int = 0
    swaps: bool = False
    keeps: bool = False
    last_flip: int | None = None
    after_flip: int | None = None
    picks: bool = False


def layer_call(table, blocks, products=(), last=(), after=(), name="layer", **plan):
    count = sum(piece.shape[0] for piece in after) // SUB
    picks = plan.get("picks", False)
    plan = Plan(len(blocks) - picks, len(last), len(after), count=count, **plan)
    sums = (*products, *map(to_core, products))
    rows = plan.blocks * ROWS
    any_space = pl.BlockSpec(memory_space=pl.ANY)
    vmem = pl.BlockSpec(memory_space=pltpu.VMEM)
    out_shape, out_specs = [], []
    scratch = [
        pltpu.VMEM((8, rows, SUB), jnp.bfloat16),
        pltpu.SemaphoreType.DMA((8, plan.blocks)),
    ]
    if plan.last:
        out_shape += [jax.ShapeDtypeStruct((ROWS, HALF), jnp.bfloat16)] * plan.blocks
        out_specs += [any_space] * plan.blocks
        scratch += [pltpu.VMEM((8, SUB, KVW), jnp.bfloat16), pltpu.SemaphoreType.DMA((8,))]
    if plan.keeps:
        out_shape.append(jax.ShapeDtypeStruct((HALF, KVW), jnp.bfloat16))
        out_specs.append(any_space)
    if plan.after:
        ahead = plan.blocks - plan.skip
        out_shape += [jax.ShapeDtypeStruct((ROWS, KVW + LANES), jnp.float32)] * ahead
        out_specs += [vmem] * ahead
        scratch += [
            pltpu.VMEM((plan.count, SUB, KVW), jnp.bfloat16),
            pltpu.SemaphoreType.DMA((plan.count,)),
        ]
    if plan.last:
        scratch.append(pltpu.SemaphoreType.DMA((8, plan.blocks)))
    if plan.keeps:
        scratch.append(pltpu.SemaphoreType.DMA((8,)))
    return pl.pallas_call(
        functools.partial(layer_kernel, plan),
        in_specs=[pl.BlockSpec(memory_space=pltpu.SMEM)]
        + [any_space] * len(blocks)
        + [vmem] * len(sums)
        + [any_space] * len(last)
        + [any_space] * len(after),
        out_specs=out_specs,
        out_shape=out_shape,
        scratch_shapes=scratch,
        compiler_params=pltpu.CompilerParams(vmem_limit_bytes=VMEM),
        cost_estimate=COST,
        name=name,
    )(table, *blocks, *sums, *last, *after)


def final_kernel(table, keep, got, mine, theirs, *refs):
    pieces, (whole, slots, slot_sems, w_slots, w_sems, store_sems) = refs[:-6], refs[-6:]
    upper = table[8] == 1
    reads, stores = [], []
    for chunk in range(16):
        source = keep if chunk < 8 else got
        column = pl.multiple_of(table[(0 if chunk < 8 else 16) + chunk % 8], SUB)
        reads.append(
            pltpu.make_async_copy(
                source.at[:, pl.ds(column, SUB)], slots.at[chunk], slot_sems.at[chunk]
            )
        )
        side = table[8] if chunk < 8 else 1 - table[8]
        target = pl.multiple_of(2 * column + side * SUB, SUB)
        stores.append(
            pltpu.make_async_copy(
                slots.at[chunk], whole.at[:, pl.ds(target, SUB)], store_sems.at[chunk]
            )
        )
    weights = read_pieces(pieces, w_slots, w_sems)

    def begin(chunk):
        if chunk < 16:
            reads[chunk].start()
            weights[chunk].start()

    for ahead in range(2 * AHEAD):
        begin(ahead)
    projected = projected_of(mine, theirs)
    for chunk in range(16):
        begin(chunk + 2 * AHEAD)
        reads[chunk].wait()
        weights[chunk].wait()

        @pl.when(upper)
        def _():
            update = lax.dot_general(
                projected,
                w_slots[chunk],
                (((1,), (1,)), ((), ())),
                preferred_element_type=jnp.float32,
            )
            slots[chunk] = (slots[chunk].astype(jnp.float32) + update).astype(jnp.bfloat16)

        stores[chunk].start()
    for store in stores:
        store.wait()


def final_call(table, keep, got, mine, theirs, here, there):
    any_space = pl.BlockSpec(memory_space=pl.ANY)
    vmem = pl.BlockSpec(memory_space=pltpu.VMEM)
    return pl.pallas_call(
        final_kernel,
        in_specs=[pl.BlockSpec(memory_space=pltpu.SMEM), any_space, any_space, vmem, vmem]
        + [any_space] * (len(here) + len(there)),
        out_specs=any_space,
        out_shape=jax.ShapeDtypeStruct((ROWS, D), jnp.bfloat16),
        scratch_shapes=[
            pltpu.VMEM((16, ROWS, SUB), jnp.bfloat16),
            pltpu.SemaphoreType.DMA((16,)),
            pltpu.VMEM((16, SUB, KVW), jnp.bfloat16),
            pltpu.SemaphoreType.DMA((16,)),
            pltpu.SemaphoreType.DMA((16,)),
        ],
        compiler_params=pltpu.CompilerParams(vmem_limit_bytes=VMEM),
        cost_estimate=COST,
        name="final_layer",
    )(table, keep, got, mine, theirs, *here, *there)


def after(value, *events):
    return lax.optimization_barrier((value, *events))[0]


def together(own, other):
    return jnp.concatenate([own, other], axis=0)


def per_device(master_weights, first_moment, second_moment, gradient_shard, hidden_states):
    core = lax.rem(lax.axis_index("section"), 2)
    xlo = lax.div(lax.axis_index("dp"), 4)
    z = lax.rem(lax.axis_index("dp"), 4)
    upper = core == 1
    core_word = jnp.reshape(core, (1,)).astype(jnp.int32)
    step = jnp.arange(4, dtype=jnp.int32)

    def columns(is_upper):
        owner = lax.rem(z + jnp.where(is_upper, step, 4 - step), 4)
        return jnp.stack([owner + 4 * xlo, owner + 4 * (1 - xlo)], axis=1).reshape(8) * SUB

    y = lax.rem(lax.div(lax.axis_index("section"), 2), 4)
    flips = jnp.stack([y < 2, y == 0]).astype(jnp.int32)
    filler = jnp.zeros((5,), jnp.int32)
    table = jnp.concatenate([columns(upper), core_word, flips, filler, columns(~upper)])
    table = table.astype(jnp.int32)

    states, mine, theirs, keep, give = update_call(
        core_word,
        master_weights,
        first_moment,
        second_moment,
        gradient_shard,
        hidden_states.reshape(ROWS, D),
    )
    other = to_core(theirs)
    even_rows = jnp.where(upper, other, mine)
    odd_rows = jnp.where(upper, mine, other)
    got = to_core(after(give, other))

    queue = []

    def ring(value, *events):
        value = to_ring(after(value, *queue[-3:-1], *events))
        queue.append(value)
        return value

    home_own = [even_rows, ring(even_rows)]
    home_other = to_pair(even_rows)
    near_odd = to_next_pair(odd_rows)

    home_own.append(ring(home_own[1], near_odd))
    near_odd = after(near_odd, home_own[1])
    far = to_next_pair(near_odd)
    third_other = to_pair(near_odd)
    home_others = [home_other, ring(home_other)]
    odd = jnp.where(upper, keep, got)

    home_own.append(ring(home_own[2]))
    near_even = to_next_pair(after(even_rows, home_own[2]))
    home_others.append(ring(home_others[1], odd))
    far_other = to_pair(after(far, home_others[1]))
    odd = to_next(after(odd, far, home_others[1]), 0)
    first = [together(after(far, home_own[3]), far_other)]
    first.append(ring(first[0], third_other))
    second_other = to_pair(after(near_even, home_others[2]))
    home_others.append(ring(home_others[2], near_even))

    home = [piece for pair in zip(home_own, home_others) for piece in pair]
    (product,) = layer_call(table, (keep, got), after=home, picks=True, name="project_home")
    first.append(ring(first[1]))
    second = [together(after(near_even, first[1]), second_other)]
    third = [together(after(near_odd, first[1]), third_other)]
    second.append(ring(second[0], odd, third[0]))
    odd = to_next(after(odd, first[1]), 1)
    even, home_here = layer_call(
        table,
        (keep, got),
        products=(product,),
        last=home,
        picks=True,
        keeps=True,
        name="expand_home",
    )
    first.append(ring(first[2], even))
    even = to_next(even, 0)
    third.append(ring(third[0]))
    second.append(ring(second[1], odd))
    third.append(ring(third[1], even))
    even = to_next(after(even, third[1]), 1)
    home_there = to_core(after(home_here, second[2]))
    second.append(ring(second[2]))
    third.append(ring(third[2]))

    even = after(even, third[2])
    products = layer_call(table, (even, odd), after=first, after_flip=9, name="project_first")
    even, odd, *products = layer_call(
        table,
        (even, odd),
        products=products,
        last=first,
        after=second,
        last_flip=9,
        after_flip=10,
        name="first_second",
    )
    even, odd, *products = layer_call(
        table,
        (even, odd),
        products=products,
        last=second,
        after=third,
        last_flip=10,
        after_flip=10,
        name="second_third",
    )
    keep, give, product = layer_call(
        table,
        (even, odd),
        products=products,
        last=third,
        after=[home_here],
        last_flip=10,
        skip=1,
        swaps=True,
        name="third_home",
    )
    out = final_call(
        table, keep, to_core(give), product, to_core(product), [home_here], [home_there]
    )
    return (*states, out.reshape(hidden_states.shape))


def solution(mesh):
    placed = (
        P("section", "dp", None),
        P("section", "dp", None),
        P("section", "dp", None),
        P("section", "dp", None),
        P("section", None, "dp", None),
    )
    return jax.shard_map(
        per_device,
        mesh=mesh,
        in_specs=placed,
        out_specs=(
            P("section", "dp", None),
            P("section", "dp", None),
            P("section", "dp", None),
            P("section", None, "dp", None),
        ),
        check_vma=False,
    )
```

```python
import dataclasses
import functools

import jax
import jax.numpy as jnp
from jax import lax
from jax.experimental import pallas as pl
from jax.experimental.pallas import tpu as pltpu
from jax.sharding import PartitionSpec as P

ADAM_STEP = 1000

beta_one = 0.9
beta_two = 0.95
learn_rate = 0.0003
decay_rate = 0.1
adam_eps = 1e-08
norm_eps = 1e-05

AXES = ("section", "dp")
D = 8192
KVW = 512
ROWS = 256
SUB = 512
HALF = D // 2
LANES = 128
VMEM = 56 * 1024 * 1024
UPDATE_STEPS = 2
SUB_STEP = SUB // UPDATE_STEPS
COST = pl.CostEstimate(flops=1, bytes_accessed=1, transcendentals=0)
AHEAD = 3


def place(linear):
    section, dp = divmod(linear, 8)
    return section // 2, section % 2, dp // 4, dp % 4


def linear_of(chip, core, xlo, z):
    return ((chip % 8) * 2 + core) * 8 + (xlo % 2) * 4 + z % 4


def shift(value, move):
    pairs = [(source, linear_of(*move(*place(source)))) for source in range(128)]
    return lax.ppermute(value, AXES, pairs)


def to_core(value):
    return shift(value, lambda chip, core, xlo, z: (chip, 1 - core, xlo, z))


def to_pair(value):
    return shift(value, lambda chip, core, xlo, z: (chip, core, xlo + 1, z))


def to_ring(value):
    return shift(value, lambda chip, core, xlo, z: (chip, core, xlo, z + 1 - 2 * core))


def to_chip(value, steps):
    return shift(value, lambda chip, core, xlo, z: (chip + steps, core, xlo, z))


def to_next_pair(value):
    def move(chip, core, xlo, z):
        return chip + 1, core, xlo + (chip % 4 == 3), z

    return shift(value, move)


def adamw_update(master, moment, second, gradient):
    moment_new = beta_one * moment + (1.0 - beta_one) * gradient
    second_new = beta_two * second + (1.0 - beta_two) * gradient * gradient
    corr_one = 1.0 - beta_one**ADAM_STEP
    corr_two = 1.0 - beta_two**ADAM_STEP
    step_size = moment_new / corr_one / (jnp.sqrt(second_new / corr_two) + adam_eps)
    master_new = master - learn_rate * (step_size + decay_rate * master)
    return (master_new, moment_new, second_new)


def update_kernel(
    core_ref,
    master_ref,
    moment_ref,
    second_ref,
    gradient_ref,
    whole_ref,
    master_out,
    moment_out,
    second_out,
    keep_rows,
    give_rows,
    keep,
    give,
):
    lower = core_ref[0] == 0
    new_master, new_moment, new_second = adamw_update(
        master_ref[...], moment_ref[...], second_ref[...], gradient_ref[...]
    )
    master_out[...] = new_master
    moment_out[...] = new_moment
    second_out[...] = new_second
    first = new_master[0].astype(jnp.bfloat16)
    last = new_master[1].astype(jnp.bfloat16)
    keep_rows[...] = jnp.where(lower, first, last)
    give_rows[...] = jnp.where(lower, last, first)
    for part in range(8 // UPDATE_STEPS):
        first = whole_ref[:, 2 * part * SUB : (2 * part + 1) * SUB]
        last = whole_ref[:, (2 * part + 1) * SUB : (2 * part + 2) * SUB]
        keep[:, part * SUB : (part + 1) * SUB] = jnp.where(lower, first, last)
        give[:, part * SUB : (part + 1) * SUB] = jnp.where(lower, last, first)


def update_call(core, master, moment, second, gradient, whole):
    state = pl.BlockSpec((2, SUB_STEP, KVW), lambda i, core: (0, i, 0))
    half = pl.BlockSpec((SUB_STEP, KVW), lambda i, core: (i, 0))
    part = pl.BlockSpec((ROWS, HALF // UPDATE_STEPS), lambda i, core: (0, i))
    shaped = [a.reshape(2, SUB, KVW) for a in (master, moment, second, gradient)]
    outs = pl.pallas_call(
        update_kernel,
        grid_spec=pltpu.PrefetchScalarGridSpec(
            num_scalar_prefetch=1,
            grid=(UPDATE_STEPS,),
            in_specs=[state] * 4
            + [pl.BlockSpec((ROWS, D // UPDATE_STEPS), lambda i, core: (0, i))],
            out_specs=[state] * 3 + [half] * 2 + [part] * 2,
        ),
        out_shape=[jax.ShapeDtypeStruct((2, SUB, KVW), jnp.float32)] * 3
        + [jax.ShapeDtypeStruct((SUB, KVW), jnp.bfloat16)] * 2
        + [jax.ShapeDtypeStruct((ROWS, HALF), jnp.bfloat16)] * 2,
        compiler_params=pltpu.CompilerParams(vmem_limit_bytes=VMEM),
        cost_estimate=COST,
        name="update",
    )(core, *shaped, whole)
    return [a.reshape(master.shape) for a in outs[:3]], *outs[3:]


def read_columns(table, blocks, slots, sems, order):
    copies = {}
    for chunk in order:
        column = pl.multiple_of(table[chunk], SUB)
        for index, block in enumerate(blocks):
            copies[chunk, index] = pltpu.make_async_copy(
                block.at[:, pl.ds(column, SUB)],
                slots.at[chunk, pl.ds(index * ROWS, ROWS)],
                sems.at[chunk, index],
            )
    return copies


def picked_columns(table, arrays, slots, sems, order):
    return {
        (chunk, 0): Picked(
            table[8],
            *(
                read_columns(table, (array,), slots, sems, (chunk,))[chunk, 0]
                for array in arrays
            ),
        )
        for chunk in order
    }


@dataclasses.dataclass(frozen=True)
class Picked:
    core: jax.Array
    lower: object
    upper: object

    def start(self):
        pl.when(self.core == 0)(self.lower.start)
        pl.when(self.core == 1)(self.upper.start)

    def wait(self):
        self.lower.wait()


def chunks_of(pieces, flip):
    for piece in pieces:
        for start in range(0, piece.shape[0], SUB):
            if flip is not None and piece.shape[0] == 2 * SUB:
                start = pl.multiple_of(start + flip * (SUB - 2 * start), SUB)
            yield piece.at[pl.ds(start, SUB)]


def read_pieces(pieces, slots, sems, flip=None):
    return [
        pltpu.make_async_copy(chunk, slots.at[index], sems.at[index])
        for index, chunk in enumerate(chunks_of(pieces, flip))
    ]


def projected_of(mine, theirs):
    summed = mine[...] + theirs[...]
    scale = lax.rsqrt(summed[:, KVW : KVW + 1] * (1.0 / D) + norm_eps)
    return (summed[:, :KVW] * scale).astype(jnp.bfloat16)


def layer_kernel(plan, *refs):
    refs = list(refs)

    def take(count):
        taken, refs[:count] = refs[:count], []
        return taken

    (table,) = take(1)
    blocks = take(plan.blocks + plan.picks)
    mine = take(plan.blocks if plan.last else 0)
    theirs = take(plan.blocks if plan.last else 0)
    last = take(plan.last)
    after = take(plan.after)
    fresh = take(plan.blocks) if plan.last else []
    kept = take(1) if plan.keeps else []
    out = take(plan.blocks - plan.skip if plan.after else 0)
    columns, column_sems = take(2)
    last_slots, last_sems = take(2) if plan.last else (None, None)
    after_slots, after_sems = take(2) if plan.after else (None, None)
    (store_sems,) = take(1) if plan.last else (None,)
    (keep_sems,) = take(1) if plan.keeps else (None,)

    taken_up = range(plan.first, plan.first + plan.count)
    chunks = range(8) if plan.last else taken_up
    read = picked_columns if plan.picks else read_columns
    reads = read(table, blocks, columns, column_sems, chunks)
    flips = [None if at is None else table[at] for at in (plan.last_flip, plan.after_flip)]
    last_reads = read_pieces(last, last_slots, last_sems, flips[0]) if plan.last else []
    after_reads = read_pieces(after, after_slots, after_sems, flips[1]) if plan.after else []

    def begin(chunk):
        if chunk not in chunks:
            return
        for index in range(plan.blocks):
            reads[chunk, index].start()
        if plan.last:
            last_reads[chunk].start()
        if chunk in taken_up:
            after_reads[chunk - plan.first].start()

    for ahead in range(AHEAD):
        begin(chunks[0] + ahead)
    rows = plan.blocks * ROWS
    if plan.last:
        projected = jnp.concatenate(
            [projected_of(here, there) for here, there in zip(mine, theirs)], axis=0
        )
    skip = plan.skip * ROWS
    if plan.after:
        total = jnp.zeros((rows - skip, KVW), jnp.float32)
        squares = jnp.zeros((rows - skip, 1), jnp.float32)
    stores = []
    for chunk in chunks:
        begin(chunk + AHEAD)
        for index in range(plan.blocks):
            reads[chunk, index].wait()
        part = columns[chunk]
        if plan.last:
            last_reads[chunk].wait()
            if plan.keeps:
                stores.append(
                    pltpu.make_async_copy(
                        last_slots.at[chunk],
                        kept[0].at[pl.ds(chunk * SUB, SUB)],
                        keep_sems.at[chunk],
                    )
                )
                stores[-1].start()
            update = lax.dot_general(
                projected,
                last_slots[chunk],
                (((1,), (1,)), ((), ())),
                preferred_element_type=jnp.float32,
            )
            part = (part.astype(jnp.float32) + update).astype(jnp.bfloat16)
            columns[chunk] = part
            column = pl.multiple_of(table[chunk], SUB)
            if plan.swaps:
                own = table[8]
                sources = [own * ROWS, (1 - own) * ROWS]
            else:
                sources = [index * ROWS for index in range(plan.blocks)]
            for index in range(plan.blocks):
                stores.append(
                    pltpu.make_async_copy(
                        columns.at[chunk, pl.ds(sources[index], ROWS)],
                        fresh[index].at[:, pl.ds(column, SUB)],
                        store_sems.at[chunk, index],
                    )
                )
                stores[-1].start()
        if chunk in taken_up:
            after_reads[chunk - plan.first].wait()
            part = part[skip:]
            total += jnp.dot(
                part,
                after_slots[chunk - plan.first],
                preferred_element_type=jnp.float32,
            )
            flat = part.astype(jnp.float32)
            squares += jnp.sum(flat * flat, axis=1, keepdims=True)
    if plan.after:
        for index, product in enumerate(out):
            part = slice(index * ROWS, (index + 1) * ROWS)
            product[:, :KVW] = total[part]
            product[:, KVW:] = jnp.broadcast_to(squares[part], (ROWS, LANES))
    for store in stores:
        store.wait()


@dataclasses.dataclass(frozen=True)
class Plan:
    blocks: int
    last: int
    after: int
    first: int = 0
    count: int = 0
    skip: int = 0
    swaps: bool = False
    keeps: bool = False
    last_flip: int | None = None
    after_flip: int | None = None
    picks: bool = False


def layer_call(table, blocks, products=(), last=(), after=(), name="layer", **plan):
    count = sum(piece.shape[0] for piece in after) // SUB
    picks = plan.get("picks", False)
    plan = Plan(len(blocks) - picks, len(last), len(after), count=count, **plan)
    sums = (*products, *map(to_core, products))
    rows = plan.blocks * ROWS
    any_space = pl.BlockSpec(memory_space=pl.ANY)
    vmem = pl.BlockSpec(memory_space=pltpu.VMEM)
    out_shape, out_specs = [], []
    scratch = [
        pltpu.VMEM((8, rows, SUB), jnp.bfloat16),
        pltpu.SemaphoreType.DMA((8, plan.blocks)),
    ]
    if plan.last:
        out_shape += [jax.ShapeDtypeStruct((ROWS, HALF), jnp.bfloat16)] * plan.blocks
        out_specs += [any_space] * plan.blocks
        scratch += [pltpu.VMEM((8, SUB, KVW), jnp.bfloat16), pltpu.SemaphoreType.DMA((8,))]
    if plan.keeps:
        out_shape.append(jax.ShapeDtypeStruct((HALF, KVW), jnp.bfloat16))
        out_specs.append(any_space)
    if plan.after:
        ahead = plan.blocks - plan.skip
        out_shape += [jax.ShapeDtypeStruct((ROWS, KVW + LANES), jnp.float32)] * ahead
        out_specs += [vmem] * ahead
        scratch += [
            pltpu.VMEM((plan.count, SUB, KVW), jnp.bfloat16),
            pltpu.SemaphoreType.DMA((plan.count,)),
        ]
    if plan.last:
        scratch.append(pltpu.SemaphoreType.DMA((8, plan.blocks)))
    if plan.keeps:
        scratch.append(pltpu.SemaphoreType.DMA((8,)))
    return pl.pallas_call(
        functools.partial(layer_kernel, plan),
        in_specs=[pl.BlockSpec(memory_space=pltpu.SMEM)]
        + [any_space] * len(blocks)
        + [vmem] * len(sums)
        + [any_space] * len(last)
        + [any_space] * len(after),
        out_specs=out_specs,
        out_shape=out_shape,
        scratch_shapes=scratch,
        compiler_params=pltpu.CompilerParams(vmem_limit_bytes=VMEM),
        cost_estimate=COST,
        name=name,
    )(table, *blocks, *sums, *last, *after)


def final_kernel(table, keep, got, mine, theirs, *refs):
    pieces, (whole, slots, slot_sems, w_slots, w_sems, store_sems) = refs[:-6], refs[-6:]
    upper = table[8] == 1
    reads, stores = [], []
    for chunk in range(16):
        source = keep if chunk < 8 else got
        column = pl.multiple_of(table[(0 if chunk < 8 else 16) + chunk % 8], SUB)
        reads.append(
            pltpu.make_async_copy(
                source.at[:, pl.ds(column, SUB)], slots.at[chunk], slot_sems.at[chunk]
            )
        )
        side = table[8] if chunk < 8 else 1 - table[8]
        target = pl.multiple_of(2 * column + side * SUB, SUB)
        stores.append(
            pltpu.make_async_copy(
                slots.at[chunk], whole.at[:, pl.ds(target, SUB)], store_sems.at[chunk]
            )
        )
    weights = read_pieces(pieces, w_slots, w_sems)

    def begin(chunk):
        if chunk < 16:
            reads[chunk].start()
            weights[chunk].start()

    for ahead in range(2 * AHEAD):
        begin(ahead)
    projected = projected_of(mine, theirs)
    for chunk in range(16):
        begin(chunk + 2 * AHEAD)
        reads[chunk].wait()
        weights[chunk].wait()

        @pl.when(upper)
        def _():
            update = lax.dot_general(
                projected,
                w_slots[chunk],
                (((1,), (1,)), ((), ())),
                preferred_element_type=jnp.float32,
            )
            slots[chunk] = (slots[chunk].astype(jnp.float32) + update).astype(jnp.bfloat16)

        stores[chunk].start()
    for store in stores:
        store.wait()


def final_call(table, keep, got, mine, theirs, here, there):
    any_space = pl.BlockSpec(memory_space=pl.ANY)
    vmem = pl.BlockSpec(memory_space=pltpu.VMEM)
    return pl.pallas_call(
        final_kernel,
        in_specs=[pl.BlockSpec(memory_space=pltpu.SMEM), any_space, any_space, vmem, vmem]
        + [any_space] * (len(here) + len(there)),
        out_specs=any_space,
        out_shape=jax.ShapeDtypeStruct((ROWS, D), jnp.bfloat16),
        scratch_shapes=[
            pltpu.VMEM((16, ROWS, SUB), jnp.bfloat16),
            pltpu.SemaphoreType.DMA((16,)),
            pltpu.VMEM((16, SUB, KVW), jnp.bfloat16),
            pltpu.SemaphoreType.DMA((16,)),
            pltpu.SemaphoreType.DMA((16,)),
        ],
        compiler_params=pltpu.CompilerParams(vmem_limit_bytes=VMEM),
        cost_estimate=COST,
        name="final_layer",
    )(table, keep, got, mine, theirs, *here, *there)


def after(value, *events):
    return lax.optimization_barrier((value, *events))[0]


def together(own, other):
    return jnp.concatenate([own, other], axis=0)


def per_device(master_weights, first_moment, second_moment, gradient_shard, hidden_states):
    core = lax.rem(lax.axis_index("section"), 2)
    xlo = lax.div(lax.axis_index("dp"), 4)
    z = lax.rem(lax.axis_index("dp"), 4)
    upper = core == 1
    core_word = jnp.reshape(core, (1,)).astype(jnp.int32)
    step = jnp.arange(4, dtype=jnp.int32)

    def columns(is_upper):
        owner = lax.rem(z + jnp.where(is_upper, step, 4 - step), 4)
        return jnp.stack([owner + 4 * xlo, owner + 4 * (1 - xlo)], axis=1).reshape(8) * SUB

    y = lax.rem(lax.div(lax.axis_index("section"), 2), 4)
    flips = jnp.stack([y < 2, y == 0]).astype(jnp.int32)
    filler = jnp.zeros((5,), jnp.int32)
    table = jnp.concatenate([columns(upper), core_word, flips, filler, columns(~upper)])
    table = table.astype(jnp.int32)

    states, mine, theirs, keep, give = update_call(
        core_word,
        master_weights,
        first_moment,
        second_moment,
        gradient_shard,
        hidden_states.reshape(ROWS, D),
    )
    other = to_core(theirs)
    even_rows = jnp.where(upper, other, mine)
    odd_rows = jnp.where(upper, mine, other)
    got = to_core(after(give, other))
    odd = jnp.where(upper, keep, got)

    queue = []

    def ring(value, *events):
        value = to_ring(after(value, *queue[-3:-1], *events))
        queue.append(value)
        return value

    home_own = [even_rows, ring(even_rows)]
    home_other = to_pair(even_rows)
    near_odd = to_next_pair(odd_rows)

    home_own.append(ring(home_own[1], odd))
    home_others = [home_other, ring(home_other, near_odd)]
    far = to_next_pair(near_odd)
    near_even = to_next_pair(after(even_rows, near_odd))
    third_other = to_pair(near_odd)

    home_own.append(ring(home_own[2]))
    home_others.append(ring(home_others[1], far, third_other))
    far_other = to_pair(far)
    home_others.append(ring(home_others[2], near_even))
    second_other = to_pair(near_even)
    odd = to_chip(after(odd, near_even), 2)

    home = [piece for pair in zip(home_own, home_others) for piece in pair]
    (product,) = layer_call(table, (keep, got), after=home, picks=True, name="project_home")
    first = [together(far, far_other)]
    first.append(ring(first[0]))
    second = [together(near_even, second_other)]
    third = [together(near_odd, third_other)]
    second.append(ring(second[0], third[0]))
    first.append(ring(first[1]))
    even, home_here = layer_call(
        table,
        (keep, got),
        products=(product,),
        last=home,
        picks=True,
        keeps=True,
        name="expand_home",
    )
    third.append(ring(third[0], even))
    even = to_chip(even, 2)
    first.append(ring(first[2]))
    second.append(ring(second[1], odd))
    third.append(ring(third[1]))
    second.append(ring(second[2]))
    home_there = to_core(after(home_here, third[2]))
    third.append(ring(third[2]))

    even = after(even, third[2])
    products = layer_call(table, (even, odd), after=first, after_flip=9, name="project_first")
    even, odd, *products = layer_call(
        table,
        (even, odd),
        products=products,
        last=first,
        after=second,
        last_flip=9,
        after_flip=10,
        name="first_second",
    )
    even, odd, *products = layer_call(
        table,
        (even, odd),
        products=products,
        last=second,
        after=third,
        last_flip=10,
        after_flip=10,
        name="second_third",
    )
    keep, give, product = layer_call(
        table,
        (even, odd),
        products=products,
        last=third,
        after=[home_here],
        last_flip=10,
        skip=1,
        swaps=True,
        name="third_home",
    )
    out = final_call(
        table, keep, to_core(give), product, to_core(product), [home_here], [home_there]
    )
    return (*states, out.reshape(hidden_states.shape))


def solution(mesh):
    placed = (
        P("section", "dp", None),
        P("section", "dp", None),
        P("section", "dp", None),
        P("section", "dp", None),
        P("section", None, "dp", None),
    )
    return jax.shard_map(
        per_device,
        mesh=mesh,
        in_specs=placed,
        out_specs=(
            P("section", "dp", None),
            P("section", "dp", None),
            P("section", "dp", None),
            P("section", None, "dp", None),
        ),
        check_vma=False,
    )
```

```python
import dataclasses
import functools

import jax
import jax.numpy as jnp
from jax import lax
from jax.experimental import pallas as pl
from jax.experimental.pallas import tpu as pltpu
from jax.sharding import PartitionSpec as P

ADAM_STEP = 1000

beta_one = 0.9
beta_two = 0.95
learn_rate = 0.0003
decay_rate = 0.1
adam_eps = 1e-08
norm_eps = 1e-05

AXES = ("section", "dp")
D = 8192
KVW = 512
ROWS = 256
SUB = 512
HALF = D // 2
LANES = 128
VMEM = 56 * 1024 * 1024
UPDATE_STEPS = 2
SUB_STEP = SUB // UPDATE_STEPS
COST = pl.CostEstimate(flops=1, bytes_accessed=1, transcendentals=0)
AHEAD = 3


def place(linear):
    section, dp = divmod(linear, 8)
    return section // 2, section % 2, dp // 4, dp % 4


def linear_of(chip, core, xlo, z):
    return ((chip % 8) * 2 + core) * 8 + (xlo % 2) * 4 + z % 4


def shift(value, move):
    pairs = [(source, linear_of(*move(*place(source)))) for source in range(128)]
    return lax.ppermute(value, AXES, pairs)


def to_core(value):
    return shift(value, lambda chip, core, xlo, z: (chip, 1 - core, xlo, z))


def to_pair(value):
    return shift(value, lambda chip, core, xlo, z: (chip, core, xlo + 1, z))


def to_ring(value, way=1):
    return shift(value, lambda chip, core, xlo, z: (chip, core, xlo, z + way * (1 - 2 * core)))


def to_chip(value, steps):
    return shift(value, lambda chip, core, xlo, z: (chip + steps, core, xlo, z))


def to_next_pair(value):
    def move(chip, core, xlo, z):
        return chip + 1, core, xlo + (chip % 4 == 3), z

    return shift(value, move)


def adamw_update(master, moment, second, gradient):
    moment_new = beta_one * moment + (1.0 - beta_one) * gradient
    second_new = beta_two * second + (1.0 - beta_two) * gradient * gradient
    corr_one = 1.0 - beta_one**ADAM_STEP
    corr_two = 1.0 - beta_two**ADAM_STEP
    step_size = moment_new / corr_one / (jnp.sqrt(second_new / corr_two) + adam_eps)
    master_new = master - learn_rate * (step_size + decay_rate * master)
    return (master_new, moment_new, second_new)


def update_kernel(
    core_ref,
    master_ref,
    moment_ref,
    second_ref,
    gradient_ref,
    whole_ref,
    master_out,
    moment_out,
    second_out,
    keep_rows,
    give_rows,
    keep,
    give,
):
    lower = core_ref[0] == 0
    new_master, new_moment, new_second = adamw_update(
        master_ref[...], moment_ref[...], second_ref[...], gradient_ref[...]
    )
    master_out[...] = new_master
    moment_out[...] = new_moment
    second_out[...] = new_second
    first = new_master[0].astype(jnp.bfloat16)
    last = new_master[1].astype(jnp.bfloat16)
    keep_rows[...] = jnp.where(lower, first, last)
    give_rows[...] = jnp.where(lower, last, first)
    for part in range(8 // UPDATE_STEPS):
        first = whole_ref[:, 2 * part * SUB : (2 * part + 1) * SUB]
        last = whole_ref[:, (2 * part + 1) * SUB : (2 * part + 2) * SUB]
        keep[:, part * SUB : (part + 1) * SUB] = jnp.where(lower, first, last)
        give[:, part * SUB : (part + 1) * SUB] = jnp.where(lower, last, first)


def update_call(core, master, moment, second, gradient, whole):
    state = pl.BlockSpec((2, SUB_STEP, KVW), lambda i, core: (0, i, 0))
    half = pl.BlockSpec((SUB_STEP, KVW), lambda i, core: (i, 0))
    part = pl.BlockSpec((ROWS, HALF // UPDATE_STEPS), lambda i, core: (0, i))
    shaped = [a.reshape(2, SUB, KVW) for a in (master, moment, second, gradient)]
    outs = pl.pallas_call(
        update_kernel,
        grid_spec=pltpu.PrefetchScalarGridSpec(
            num_scalar_prefetch=1,
            grid=(UPDATE_STEPS,),
            in_specs=[state] * 4
            + [pl.BlockSpec((ROWS, D // UPDATE_STEPS), lambda i, core: (0, i))],
            out_specs=[state] * 3 + [half] * 2 + [part] * 2,
        ),
        out_shape=[jax.ShapeDtypeStruct((2, SUB, KVW), jnp.float32)] * 3
        + [jax.ShapeDtypeStruct((SUB, KVW), jnp.bfloat16)] * 2
        + [jax.ShapeDtypeStruct((ROWS, HALF), jnp.bfloat16)] * 2,
        compiler_params=pltpu.CompilerParams(vmem_limit_bytes=VMEM),
        cost_estimate=COST,
        name="update",
    )(core, *shaped, whole)
    return [a.reshape(master.shape) for a in outs[:3]], *outs[3:]


def read_columns(table, blocks, slots, sems, order):
    copies = {}
    for chunk in order:
        column = pl.multiple_of(table[chunk], SUB)
        for index, block in enumerate(blocks):
            copies[chunk, index] = pltpu.make_async_copy(
                block.at[:, pl.ds(column, SUB)],
                slots.at[chunk, pl.ds(index * ROWS, ROWS)],
                sems.at[chunk, index],
            )
    return copies


def picked_columns(table, arrays, slots, sems, order):
    return {
        (chunk, 0): Picked(
            table[8],
            *(
                read_columns(table, (array,), slots, sems, (chunk,))[chunk, 0]
                for array in arrays
            ),
        )
        for chunk in order
    }


@dataclasses.dataclass(frozen=True)
class Picked:
    core: jax.Array
    lower: object
    upper: object

    def start(self):
        pl.when(self.core == 0)(self.lower.start)
        pl.when(self.core == 1)(self.upper.start)

    def wait(self):
        self.lower.wait()


def chunks_of(pieces, flip):
    for piece in pieces:
        for start in range(0, piece.shape[0], SUB):
            if flip is not None and piece.shape[0] == 2 * SUB:
                start = pl.multiple_of(start + flip * (SUB - 2 * start), SUB)
            yield piece.at[pl.ds(start, SUB)]


def read_pieces(pieces, slots, sems, flip=None):
    return [
        pltpu.make_async_copy(chunk, slots.at[index], sems.at[index])
        for index, chunk in enumerate(chunks_of(pieces, flip))
    ]


def projected_of(mine, theirs):
    summed = mine[...] + theirs[...]
    scale = lax.rsqrt(summed[:, KVW : KVW + 1] * (1.0 / D) + norm_eps)
    return (summed[:, :KVW] * scale).astype(jnp.bfloat16)


def layer_kernel(plan, *refs):
    refs = list(refs)

    def take(count):
        taken, refs[:count] = refs[:count], []
        return taken

    (table,) = take(1)
    blocks = take(plan.blocks + plan.picks)
    mine = take(plan.blocks if plan.last else 0)
    theirs = take(plan.blocks if plan.last else 0)
    last = take(plan.last)
    after = take(plan.after)
    fresh = take(plan.blocks) if plan.last else []
    kept = take(1) if plan.keeps else []
    out = take(plan.blocks - plan.skip if plan.after else 0)
    columns, column_sems = take(2)
    last_slots, last_sems = take(2) if plan.last else (None, None)
    after_slots, after_sems = take(2) if plan.after else (None, None)
    (store_sems,) = take(1) if plan.last else (None,)
    (keep_sems,) = take(1) if plan.keeps else (None,)

    taken_up = range(plan.first, plan.first + plan.count)
    chunks = range(8) if plan.last else taken_up
    read = picked_columns if plan.picks else read_columns
    reads = read(table, blocks, columns, column_sems, chunks)
    flips = [None if at is None else table[at] for at in (plan.last_flip, plan.after_flip)]
    last_reads = read_pieces(last, last_slots, last_sems, flips[0]) if plan.last else []
    after_reads = read_pieces(after, after_slots, after_sems, flips[1]) if plan.after else []

    def begin(chunk):
        if chunk not in chunks:
            return
        for index in range(plan.blocks):
            reads[chunk, index].start()
        if plan.last:
            last_reads[chunk].start()
        if chunk in taken_up:
            after_reads[chunk - plan.first].start()

    for ahead in range(AHEAD):
        begin(chunks[0] + ahead)
    rows = plan.blocks * ROWS
    if plan.last:
        projected = jnp.concatenate(
            [projected_of(here, there) for here, there in zip(mine, theirs)], axis=0
        )
    skip = plan.skip * ROWS
    if plan.after:
        total = jnp.zeros((rows - skip, KVW), jnp.float32)
        squares = jnp.zeros((rows - skip, 1), jnp.float32)
    stores = []
    for chunk in chunks:
        begin(chunk + AHEAD)
        for index in range(plan.blocks):
            reads[chunk, index].wait()
        part = columns[chunk]
        if plan.last:
            last_reads[chunk].wait()
            if plan.keeps:
                stores.append(
                    pltpu.make_async_copy(
                        last_slots.at[chunk],
                        kept[0].at[pl.ds(chunk * SUB, SUB)],
                        keep_sems.at[chunk],
                    )
                )
                stores[-1].start()
            update = lax.dot_general(
                projected,
                last_slots[chunk],
                (((1,), (1,)), ((), ())),
                preferred_element_type=jnp.float32,
            )
            part = (part.astype(jnp.float32) + update).astype(jnp.bfloat16)
            columns[chunk] = part
            column = pl.multiple_of(table[chunk], SUB)
            if plan.swaps:
                own = table[8]
                sources = [own * ROWS, (1 - own) * ROWS]
            else:
                sources = [index * ROWS for index in range(plan.blocks)]
            for index in range(plan.blocks):
                stores.append(
                    pltpu.make_async_copy(
                        columns.at[chunk, pl.ds(sources[index], ROWS)],
                        fresh[index].at[:, pl.ds(column, SUB)],
                        store_sems.at[chunk, index],
                    )
                )
                stores[-1].start()
        if chunk in taken_up:
            after_reads[chunk - plan.first].wait()
            part = part[skip:]
            total += jnp.dot(
                part,
                after_slots[chunk - plan.first],
                preferred_element_type=jnp.float32,
            )
            flat = part.astype(jnp.float32)
            squares += jnp.sum(flat * flat, axis=1, keepdims=True)
    if plan.after:
        for index, product in enumerate(out):
            part = slice(index * ROWS, (index + 1) * ROWS)
            product[:, :KVW] = total[part]
            product[:, KVW:] = jnp.broadcast_to(squares[part], (ROWS, LANES))
    for store in stores:
        store.wait()


@dataclasses.dataclass(frozen=True)
class Plan:
    blocks: int
    last: int
    after: int
    first: int = 0
    count: int = 0
    skip: int = 0
    swaps: bool = False
    keeps: bool = False
    last_flip: int | None = None
    after_flip: int | None = None
    picks: bool = False


def layer_call(table, blocks, products=(), last=(), after=(), name="layer", **plan):
    count = sum(piece.shape[0] for piece in after) // SUB
    picks = plan.get("picks", False)
    plan = Plan(len(blocks) - picks, len(last), len(after), count=count, **plan)
    sums = (*products, *map(to_core, products))
    rows = plan.blocks * ROWS
    any_space = pl.BlockSpec(memory_space=pl.ANY)
    vmem = pl.BlockSpec(memory_space=pltpu.VMEM)
    out_shape, out_specs = [], []
    scratch = [
        pltpu.VMEM((8, rows, SUB), jnp.bfloat16),
        pltpu.SemaphoreType.DMA((8, plan.blocks)),
    ]
    if plan.last:
        out_shape += [jax.ShapeDtypeStruct((ROWS, HALF), jnp.bfloat16)] * plan.blocks
        out_specs += [any_space] * plan.blocks
        scratch += [pltpu.VMEM((8, SUB, KVW), jnp.bfloat16), pltpu.SemaphoreType.DMA((8,))]
    if plan.keeps:
        out_shape.append(jax.ShapeDtypeStruct((HALF, KVW), jnp.bfloat16))
        out_specs.append(any_space)
    if plan.after:
        ahead = plan.blocks - plan.skip
        out_shape += [jax.ShapeDtypeStruct((ROWS, KVW + LANES), jnp.float32)] * ahead
        out_specs += [vmem] * ahead
        scratch += [
            pltpu.VMEM((plan.count, SUB, KVW), jnp.bfloat16),
            pltpu.SemaphoreType.DMA((plan.count,)),
        ]
    if plan.last:
        scratch.append(pltpu.SemaphoreType.DMA((8, plan.blocks)))
    if plan.keeps:
        scratch.append(pltpu.SemaphoreType.DMA((8,)))
    return pl.pallas_call(
        functools.partial(layer_kernel, plan),
        in_specs=[pl.BlockSpec(memory_space=pltpu.SMEM)]
        + [any_space] * len(blocks)
        + [vmem] * len(sums)
        + [any_space] * len(last)
        + [any_space] * len(after),
        out_specs=out_specs,
        out_shape=out_shape,
        scratch_shapes=scratch,
        compiler_params=pltpu.CompilerParams(vmem_limit_bytes=VMEM),
        cost_estimate=COST,
        name=name,
    )(table, *blocks, *sums, *last, *after)


def final_kernel(table, keep, got, mine, theirs, *refs):
    pieces, (whole, slots, slot_sems, w_slots, w_sems, store_sems) = refs[:-6], refs[-6:]
    upper = table[8] == 1
    reads, stores = [], []
    for chunk in range(16):
        source = keep if chunk < 8 else got
        column = pl.multiple_of(table[(0 if chunk < 8 else 16) + chunk % 8], SUB)
        reads.append(
            pltpu.make_async_copy(
                source.at[:, pl.ds(column, SUB)], slots.at[chunk], slot_sems.at[chunk]
            )
        )
        side = table[8] if chunk < 8 else 1 - table[8]
        target = pl.multiple_of(2 * column + side * SUB, SUB)
        stores.append(
            pltpu.make_async_copy(
                slots.at[chunk], whole.at[:, pl.ds(target, SUB)], store_sems.at[chunk]
            )
        )
    weights = read_pieces(pieces, w_slots, w_sems)

    def begin(chunk):
        if chunk < 16:
            reads[chunk].start()
            weights[chunk].start()

    for ahead in range(2 * AHEAD):
        begin(ahead)
    projected = projected_of(mine, theirs)
    for chunk in range(16):
        begin(chunk + 2 * AHEAD)
        reads[chunk].wait()
        weights[chunk].wait()

        @pl.when(upper)
        def _():
            update = lax.dot_general(
                projected,
                w_slots[chunk],
                (((1,), (1,)), ((), ())),
                preferred_element_type=jnp.float32,
            )
            slots[chunk] = (slots[chunk].astype(jnp.float32) + update).astype(jnp.bfloat16)

        stores[chunk].start()
    for store in stores:
        store.wait()


def final_call(table, keep, got, mine, theirs, here, there):
    any_space = pl.BlockSpec(memory_space=pl.ANY)
    vmem = pl.BlockSpec(memory_space=pltpu.VMEM)
    return pl.pallas_call(
        final_kernel,
        in_specs=[pl.BlockSpec(memory_space=pltpu.SMEM), any_space, any_space, vmem, vmem]
        + [any_space] * (len(here) + len(there)),
        out_specs=any_space,
        out_shape=jax.ShapeDtypeStruct((ROWS, D), jnp.bfloat16),
        scratch_shapes=[
            pltpu.VMEM((16, ROWS, SUB), jnp.bfloat16),
            pltpu.SemaphoreType.DMA((16,)),
            pltpu.VMEM((16, SUB, KVW), jnp.bfloat16),
            pltpu.SemaphoreType.DMA((16,)),
            pltpu.SemaphoreType.DMA((16,)),
        ],
        compiler_params=pltpu.CompilerParams(vmem_limit_bytes=VMEM),
        cost_estimate=COST,
        name="final_layer",
    )(table, keep, got, mine, theirs, *here, *there)


def after(value, *events):
    return lax.optimization_barrier((value, *events))[0]


def together(own, other):
    return jnp.concatenate([own, other], axis=0)


def per_device(master_weights, first_moment, second_moment, gradient_shard, hidden_states):
    core = lax.rem(lax.axis_index("section"), 2)
    xlo = lax.div(lax.axis_index("dp"), 4)
    z = lax.rem(lax.axis_index("dp"), 4)
    upper = core == 1
    core_word = jnp.reshape(core, (1,)).astype(jnp.int32)
    step = jnp.arange(4, dtype=jnp.int32)

    def columns(is_upper):
        owner = lax.rem(z + jnp.where(is_upper, step, 4 - step), 4)
        return jnp.stack([owner + 4 * xlo, owner + 4 * (1 - xlo)], axis=1).reshape(8) * SUB

    y = lax.rem(lax.div(lax.axis_index("section"), 2), 4)
    flips = jnp.stack([y < 2, y == 0]).astype(jnp.int32)
    filler = jnp.zeros((5,), jnp.int32)
    table = jnp.concatenate([columns(upper), core_word, flips, filler, columns(~upper)])
    table = table.astype(jnp.int32)

    states, mine, theirs, keep, give = update_call(
        core_word,
        master_weights,
        first_moment,
        second_moment,
        gradient_shard,
        hidden_states.reshape(ROWS, D),
    )
    other = to_core(theirs)
    even_rows = jnp.where(upper, other, mine)
    odd_rows = jnp.where(upper, mine, other)
    got = to_core(after(give, other))
    odd = jnp.where(upper, keep, got)

    queue = []

    def ring(value, *events, way=1):
        value = to_ring(after(value, *queue[-3:-1], *events), way)
        queue.append(value)
        return value

    def back(value, *events):
        return ring(value, *events, way=-1)

    home_other = to_pair(even_rows)
    own_ahead = ring(even_rows)
    own_back = back(even_rows)
    near_odd = to_next_pair(odd_rows)

    own_two = ring(own_ahead)
    other_ahead = ring(home_other)
    other_back = back(home_other, odd)
    far = to_next_pair(after(near_odd, own_ahead))
    near_even = to_next_pair(after(even_rows, near_odd))
    third_other = to_pair(near_odd)
    other_two = ring(other_ahead, far)
    far_other = to_pair(far)
    second_other = to_pair(near_even)
    odd = to_chip(after(odd, near_even), 2)

    home = [even_rows, home_other, own_ahead, other_ahead, own_two, other_two, own_back, other_back]
    (product,) = layer_call(table, (keep, got), after=home, picks=True, name="project_home")
    first = together(far, far_other)
    first_ahead = ring(first, near_even, third_other)
    first_back = back(first)
    second = together(near_even, second_other)
    third = together(near_odd, third_other)
    second_ahead = ring(second, third)
    first = [first, first_ahead, ring(first_ahead), first_back]
    even, home_here = layer_call(
        table,
        (keep, got),
        products=(product,),
        last=home,
        picks=True,
        keeps=True,
        name="expand_home",
    )
    second_back = back(second, even)
    even = to_chip(even, 2)
    third_ahead = ring(third, odd)
    second = [second, second_ahead, ring(second_ahead, even), second_back]
    third_back = back(third)
    home_there = to_core(after(home_here, third_ahead))
    third = [third, third_ahead, ring(third_ahead), third_back]

    even = after(even, third_ahead)
    products = layer_call(table, (even, odd), after=first, after_flip=9, name="project_first")
    even, odd, *products = layer_call(
        table,
        (even, odd),
        products=products,
        last=first,
        after=second,
        last_flip=9,
        after_flip=10,
        name="first_second",
    )
    even, odd, *products = layer_call(
        table,
        (even, odd),
        products=products,
        last=second,
        after=third,
        last_flip=10,
        after_flip=10,
        name="second_third",
    )
    keep, give, product = layer_call(
        table,
        (even, odd),
        products=products,
        last=third,
        after=[home_here],
        last_flip=10,
        skip=1,
        swaps=True,
        name="third_home",
    )
    out = final_call(
        table, keep, to_core(give), product, to_core(product), [home_here], [home_there]
    )
    return (*states, out.reshape(hidden_states.shape))


def solution(mesh):
    placed = (
        P("section", "dp", None),
        P("section", "dp", None),
        P("section", "dp", None),
        P("section", "dp", None),
        P("section", None, "dp", None),
    )
    return jax.shard_map(
        per_device,
        mesh=mesh,
        in_specs=placed,
        out_specs=(
            P("section", "dp", None),
            P("section", "dp", None),
            P("section", "dp", None),
            P("section", None, "dp", None),
        ),
        check_vma=False,
    )
```

```python
import dataclasses
import functools

import jax
import jax.numpy as jnp
from jax import lax
from jax.experimental import pallas as pl
from jax.experimental.pallas import tpu as pltpu
from jax.sharding import PartitionSpec as P

ADAM_STEP = 1000

beta_one = 0.9
beta_two = 0.95
learn_rate = 0.0003
decay_rate = 0.1
adam_eps = 1e-08
norm_eps = 1e-05

AXES = ("section", "dp")
D = 8192
KVW = 512
ROWS = 256
SUB = 512
HALF = D // 2
LANES = 128
VMEM = 56 * 1024 * 1024
UPDATE_STEPS = 2
SUB_STEP = SUB // UPDATE_STEPS
COST = pl.CostEstimate(flops=1, bytes_accessed=1, transcendentals=0)
AHEAD = 3


def place(linear):
    section, dp = divmod(linear, 8)
    return section // 2, section % 2, dp // 4, dp % 4


def linear_of(chip, core, xlo, z):
    return ((chip % 8) * 2 + core) * 8 + (xlo % 2) * 4 + z % 4


def shift(value, move):
    pairs = [(source, linear_of(*move(*place(source)))) for source in range(128)]
    return lax.ppermute(value, AXES, pairs)


def to_core(value):
    return shift(value, lambda chip, core, xlo, z: (chip, 1 - core, xlo, z))


def to_pair(value):
    return shift(value, lambda chip, core, xlo, z: (chip, core, xlo + 1, z))


def to_ring(value, way=1):
    return shift(value, lambda chip, core, xlo, z: (chip, core, xlo, z + way * (1 - 2 * core)))


def to_chip(value, steps):
    return shift(value, lambda chip, core, xlo, z: (chip + steps, core, xlo, z))


def to_next_pair(value):
    def move(chip, core, xlo, z):
        return chip + 1, core, xlo + (chip % 4 == 3), z

    return shift(value, move)


def to_far_y(value):
    return shift(
        value, lambda chip, core, xlo, z: (chip // 4 * 4 + (chip + 2) % 4, core, xlo, z)
    )


def to_far_x(value):
    return shift(
        value, lambda chip, core, xlo, z: (chip if chip % 4 >= 2 else chip + 4, core, xlo, z)
    )


def adamw_update(master, moment, second, gradient):
    moment_new = beta_one * moment + (1.0 - beta_one) * gradient
    second_new = beta_two * second + (1.0 - beta_two) * gradient * gradient
    corr_one = 1.0 - beta_one**ADAM_STEP
    corr_two = 1.0 - beta_two**ADAM_STEP
    step_size = moment_new / corr_one / (jnp.sqrt(second_new / corr_two) + adam_eps)
    master_new = master - learn_rate * (step_size + decay_rate * master)
    return (master_new, moment_new, second_new)


def update_kernel(
    core_ref,
    master_ref,
    moment_ref,
    second_ref,
    gradient_ref,
    whole_ref,
    master_out,
    moment_out,
    second_out,
    keep_rows,
    give_rows,
    keep,
    give,
):
    lower = core_ref[0] == 0
    new_master, new_moment, new_second = adamw_update(
        master_ref[...], moment_ref[...], second_ref[...], gradient_ref[...]
    )
    master_out[...] = new_master
    moment_out[...] = new_moment
    second_out[...] = new_second
    first = new_master[0].astype(jnp.bfloat16)
    last = new_master[1].astype(jnp.bfloat16)
    keep_rows[...] = jnp.where(lower, first, last)
    give_rows[...] = jnp.where(lower, last, first)
    for part in range(8 // UPDATE_STEPS):
        first = whole_ref[:, 2 * part * SUB : (2 * part + 1) * SUB]
        last = whole_ref[:, (2 * part + 1) * SUB : (2 * part + 2) * SUB]
        keep[:, part * SUB : (part + 1) * SUB] = jnp.where(lower, first, last)
        give[:, part * SUB : (part + 1) * SUB] = jnp.where(lower, last, first)


def update_call(core, master, moment, second, gradient, whole):
    state = pl.BlockSpec((2, SUB_STEP, KVW), lambda i, core: (0, i, 0))
    half = pl.BlockSpec((SUB_STEP, KVW), lambda i, core: (i, 0))
    part = pl.BlockSpec((ROWS, HALF // UPDATE_STEPS), lambda i, core: (0, i))
    shaped = [a.reshape(2, SUB, KVW) for a in (master, moment, second, gradient)]
    outs = pl.pallas_call(
        update_kernel,
        grid_spec=pltpu.PrefetchScalarGridSpec(
            num_scalar_prefetch=1,
            grid=(UPDATE_STEPS,),
            in_specs=[state] * 4
            + [pl.BlockSpec((ROWS, D // UPDATE_STEPS), lambda i, core: (0, i))],
            out_specs=[state] * 3 + [half] * 2 + [part] * 2,
        ),
        out_shape=[jax.ShapeDtypeStruct((2, SUB, KVW), jnp.float32)] * 3
        + [jax.ShapeDtypeStruct((SUB, KVW), jnp.bfloat16)] * 2
        + [jax.ShapeDtypeStruct((ROWS, HALF), jnp.bfloat16)] * 2,
        compiler_params=pltpu.CompilerParams(vmem_limit_bytes=VMEM),
        cost_estimate=COST,
        name="update",
    )(core, *shaped, whole)
    return [a.reshape(master.shape) for a in outs[:3]], *outs[3:]


def read_columns(table, blocks, slots, sems, order):
    copies = {}
    for chunk in order:
        column = pl.multiple_of(table[chunk], SUB)
        for index, block in enumerate(blocks):
            copies[chunk, index] = pltpu.make_async_copy(
                block.at[:, pl.ds(column, SUB)],
                slots.at[chunk, pl.ds(index * ROWS, ROWS)],
                sems.at[chunk, index],
            )
    return copies


def picked_columns(table, arrays, slots, sems, order):
    return {
        (chunk, 0): Picked(
            table[8],
            *(
                read_columns(table, (array,), slots, sems, (chunk,))[chunk, 0]
                for array in arrays
            ),
        )
        for chunk in order
    }


@dataclasses.dataclass(frozen=True)
class Picked:
    core: jax.Array
    lower: object
    upper: object

    def start(self):
        pl.when(self.core == 0)(self.lower.start)
        pl.when(self.core == 1)(self.upper.start)

    def wait(self):
        self.lower.wait()


def chunks_of(pieces, flip):
    for piece in pieces:
        for start in range(0, piece.shape[0], SUB):
            if flip is not None and piece.shape[0] == 2 * SUB:
                start = pl.multiple_of(start + flip * (SUB - 2 * start), SUB)
            yield piece.at[pl.ds(start, SUB)]


def read_pieces(pieces, slots, sems, flip=None):
    return [
        pltpu.make_async_copy(chunk, slots.at[index], sems.at[index])
        for index, chunk in enumerate(chunks_of(pieces, flip))
    ]


def projected_of(mine, theirs):
    summed = mine[...] + theirs[...]
    scale = lax.rsqrt(summed[:, KVW : KVW + 1] * (1.0 / D) + norm_eps)
    return (summed[:, :KVW] * scale).astype(jnp.bfloat16)


def layer_kernel(plan, *refs):
    refs = list(refs)

    def take(count):
        taken, refs[:count] = refs[:count], []
        return taken

    (table,) = take(1)
    blocks = take(plan.blocks + plan.picks)
    mine = take(plan.blocks if plan.last else 0)
    theirs = take(plan.blocks if plan.last else 0)
    last = take(plan.last)
    after = take(plan.after)
    fresh = take(plan.blocks) if plan.last else []
    kept = take(1) if plan.keeps else []
    out = take(plan.blocks - plan.skip if plan.after else 0)
    columns, column_sems = take(2)
    last_slots, last_sems = take(2) if plan.last else (None, None)
    after_slots, after_sems = take(2) if plan.after else (None, None)
    (store_sems,) = take(1) if plan.last else (None,)
    (keep_sems,) = take(1) if plan.keeps else (None,)

    taken_up = range(plan.first, plan.first + plan.count)
    chunks = range(8) if plan.last else taken_up
    read = picked_columns if plan.picks else read_columns
    reads = read(table, blocks, columns, column_sems, chunks)
    flips = [None if at is None else table[at] for at in (plan.last_flip, plan.after_flip)]
    last_reads = read_pieces(last, last_slots, last_sems, flips[0]) if plan.last else []
    after_reads = read_pieces(after, after_slots, after_sems, flips[1]) if plan.after else []

    def begin(chunk):
        if chunk not in chunks:
            return
        for index in range(plan.blocks):
            reads[chunk, index].start()
        if plan.last:
            last_reads[chunk].start()
        if chunk in taken_up:
            after_reads[chunk - plan.first].start()

    for ahead in range(AHEAD):
        begin(chunks[0] + ahead)
    rows = plan.blocks * ROWS
    if plan.last:
        projected = jnp.concatenate(
            [projected_of(here, there) for here, there in zip(mine, theirs)], axis=0
        )
    skip = plan.skip * ROWS
    if plan.after:
        total = jnp.zeros((rows - skip, KVW), jnp.float32)
        squares = jnp.zeros((rows - skip, 1), jnp.float32)
    stores = []
    for chunk in chunks:
        begin(chunk + AHEAD)
        for index in range(plan.blocks):
            reads[chunk, index].wait()
        part = columns[chunk]
        if plan.last:
            last_reads[chunk].wait()
            if plan.keeps:
                stores.append(
                    pltpu.make_async_copy(
                        last_slots.at[chunk],
                        kept[0].at[pl.ds(chunk * SUB, SUB)],
                        keep_sems.at[chunk],
                    )
                )
                stores[-1].start()
            update = lax.dot_general(
                projected,
                last_slots[chunk],
                (((1,), (1,)), ((), ())),
                preferred_element_type=jnp.float32,
            )
            part = (part.astype(jnp.float32) + update).astype(jnp.bfloat16)
            columns[chunk] = part
            column = pl.multiple_of(table[chunk], SUB)
            if plan.swaps:
                own = table[8]
                sources = [own * ROWS, (1 - own) * ROWS]
            else:
                sources = [index * ROWS for index in range(plan.blocks)]
            for index in range(plan.blocks):
                stores.append(
                    pltpu.make_async_copy(
                        columns.at[chunk, pl.ds(sources[index], ROWS)],
                        fresh[index].at[:, pl.ds(column, SUB)],
                        store_sems.at[chunk, index],
                    )
                )
                stores[-1].start()
        if chunk in taken_up:
            after_reads[chunk - plan.first].wait()
            part = part[skip:]
            total += jnp.dot(
                part,
                after_slots[chunk - plan.first],
                preferred_element_type=jnp.float32,
            )
            flat = part.astype(jnp.float32)
            squares += jnp.sum(flat * flat, axis=1, keepdims=True)
    if plan.after:
        for index, product in enumerate(out):
            part = slice(index * ROWS, (index + 1) * ROWS)
            product[:, :KVW] = total[part]
            product[:, KVW:] = jnp.broadcast_to(squares[part], (ROWS, LANES))
    for store in stores:
        store.wait()


@dataclasses.dataclass(frozen=True)
class Plan:
    blocks: int
    last: int
    after: int
    first: int = 0
    count: int = 0
    skip: int = 0
    swaps: bool = False
    keeps: bool = False
    last_flip: int | None = None
    after_flip: int | None = None
    picks: bool = False


def layer_call(table, blocks, products=(), last=(), after=(), name="layer", **plan):
    count = sum(piece.shape[0] for piece in after) // SUB
    picks = plan.get("picks", False)
    plan = Plan(len(blocks) - picks, len(last), len(after), count=count, **plan)
    sums = (*products, *map(to_core, products))
    rows = plan.blocks * ROWS
    any_space = pl.BlockSpec(memory_space=pl.ANY)
    vmem = pl.BlockSpec(memory_space=pltpu.VMEM)
    out_shape, out_specs = [], []
    scratch = [
        pltpu.VMEM((8, rows, SUB), jnp.bfloat16),
        pltpu.SemaphoreType.DMA((8, plan.blocks)),
    ]
    if plan.last:
        out_shape += [jax.ShapeDtypeStruct((ROWS, HALF), jnp.bfloat16)] * plan.blocks
        out_specs += [any_space] * plan.blocks
        scratch += [pltpu.VMEM((8, SUB, KVW), jnp.bfloat16), pltpu.SemaphoreType.DMA((8,))]
    if plan.keeps:
        out_shape.append(jax.ShapeDtypeStruct((HALF, KVW), jnp.bfloat16))
        out_specs.append(any_space)
    if plan.after:
        ahead = plan.blocks - plan.skip
        out_shape += [jax.ShapeDtypeStruct((ROWS, KVW + LANES), jnp.float32)] * ahead
        out_specs += [vmem] * ahead
        scratch += [
            pltpu.VMEM((plan.count, SUB, KVW), jnp.bfloat16),
            pltpu.SemaphoreType.DMA((plan.count,)),
        ]
    if plan.last:
        scratch.append(pltpu.SemaphoreType.DMA((8, plan.blocks)))
    if plan.keeps:
        scratch.append(pltpu.SemaphoreType.DMA((8,)))
    return pl.pallas_call(
        functools.partial(layer_kernel, plan),
        in_specs=[pl.BlockSpec(memory_space=pltpu.SMEM)]
        + [any_space] * len(blocks)
        + [vmem] * len(sums)
        + [any_space] * len(last)
        + [any_space] * len(after),
        out_specs=out_specs,
        out_shape=out_shape,
        scratch_shapes=scratch,
        compiler_params=pltpu.CompilerParams(vmem_limit_bytes=VMEM),
        cost_estimate=COST,
        name=name,
    )(table, *blocks, *sums, *last, *after)


def final_kernel(table, keep, got, mine, theirs, *refs):
    pieces, (whole, slots, slot_sems, w_slots, w_sems, store_sems) = refs[:-6], refs[-6:]
    upper = table[8] == 1
    reads, stores = [], []
    for chunk in range(16):
        source = keep if chunk < 8 else got
        column = pl.multiple_of(table[(0 if chunk < 8 else 16) + chunk % 8], SUB)
        reads.append(
            pltpu.make_async_copy(
                source.at[:, pl.ds(column, SUB)], slots.at[chunk], slot_sems.at[chunk]
            )
        )
        side = table[8] if chunk < 8 else 1 - table[8]
        target = pl.multiple_of(2 * column + side * SUB, SUB)
        stores.append(
            pltpu.make_async_copy(
                slots.at[chunk], whole.at[:, pl.ds(target, SUB)], store_sems.at[chunk]
            )
        )
    weights = read_pieces(pieces, w_slots, w_sems)

    def begin(chunk):
        if chunk < 16:
            reads[chunk].start()
            weights[chunk].start()

    for ahead in range(2 * AHEAD):
        begin(ahead)
    projected = projected_of(mine, theirs)
    for chunk in range(16):
        begin(chunk + 2 * AHEAD)
        reads[chunk].wait()
        weights[chunk].wait()

        @pl.when(upper)
        def _():
            update = lax.dot_general(
                projected,
                w_slots[chunk],
                (((1,), (1,)), ((), ())),
                preferred_element_type=jnp.float32,
            )
            slots[chunk] = (slots[chunk].astype(jnp.float32) + update).astype(jnp.bfloat16)

        stores[chunk].start()
    for store in stores:
        store.wait()


def final_call(table, keep, got, mine, theirs, here, there):
    any_space = pl.BlockSpec(memory_space=pl.ANY)
    vmem = pl.BlockSpec(memory_space=pltpu.VMEM)
    return pl.pallas_call(
        final_kernel,
        in_specs=[pl.BlockSpec(memory_space=pltpu.SMEM), any_space, any_space, vmem, vmem]
        + [any_space] * (len(here) + len(there)),
        out_specs=any_space,
        out_shape=jax.ShapeDtypeStruct((ROWS, D), jnp.bfloat16),
        scratch_shapes=[
            pltpu.VMEM((16, ROWS, SUB), jnp.bfloat16),
            pltpu.SemaphoreType.DMA((16,)),
            pltpu.VMEM((16, SUB, KVW), jnp.bfloat16),
            pltpu.SemaphoreType.DMA((16,)),
            pltpu.SemaphoreType.DMA((16,)),
        ],
        compiler_params=pltpu.CompilerParams(vmem_limit_bytes=VMEM),
        cost_estimate=COST,
        name="final_layer",
    )(table, keep, got, mine, theirs, *here, *there)


def after(value, *events):
    return lax.optimization_barrier((value, *events))[0]


def together(own, other):
    return jnp.concatenate([own, other], axis=0)


def per_device(master_weights, first_moment, second_moment, gradient_shard, hidden_states):
    core = lax.rem(lax.axis_index("section"), 2)
    xlo = lax.div(lax.axis_index("dp"), 4)
    z = lax.rem(lax.axis_index("dp"), 4)
    upper = core == 1
    core_word = jnp.reshape(core, (1,)).astype(jnp.int32)
    step = jnp.arange(4, dtype=jnp.int32)

    def columns(is_upper):
        owner = lax.rem(z + jnp.where(is_upper, step, 4 - step), 4)
        return jnp.stack([owner + 4 * xlo, owner + 4 * (1 - xlo)], axis=1).reshape(8) * SUB

    y = lax.rem(lax.div(lax.axis_index("section"), 2), 4)
    flips = jnp.stack([y < 2, y == 0]).astype(jnp.int32)
    filler = jnp.zeros((5,), jnp.int32)
    table = jnp.concatenate([columns(upper), core_word, flips, filler, columns(~upper)])
    table = table.astype(jnp.int32)

    states, mine, theirs, keep, give = update_call(
        core_word,
        master_weights,
        first_moment,
        second_moment,
        gradient_shard,
        hidden_states.reshape(ROWS, D),
    )
    other = to_core(theirs)
    even_rows = jnp.where(upper, other, mine)
    odd_rows = jnp.where(upper, mine, other)
    got = to_core(after(give, other))
    odd = jnp.where(upper, keep, got)

    queue = []

    def ring(value, *events, way=1):
        value = to_ring(after(value, *queue[-3:-1], *events), way)
        queue.append(value)
        return value

    def back(value, *events):
        return ring(value, *events, way=-1)

    home_other = to_pair(even_rows)
    own_ahead = ring(even_rows)
    own_back = back(even_rows)
    near_odd = to_next_pair(odd_rows)

    own_two = ring(own_ahead)
    other_ahead = ring(home_other)
    other_back = back(home_other)
    far = to_next_pair(after(near_odd, odd))
    near_even = to_next_pair(after(even_rows, near_odd))
    far_other = to_pair(far)
    other_two = ring(other_ahead, far)
    third_other = to_pair(after(near_odd, other_ahead, far))
    odd = to_far_y(after(odd, own_two))

    home = [even_rows, home_other, own_ahead, other_ahead, own_two, other_two, own_back, other_back]
    (product,) = layer_call(table, (keep, got), after=home, picks=True, name="project_home")
    second_other = to_pair(after(near_even, product))
    first = together(far, far_other)
    first_ahead = ring(first, near_even, third_other)
    first_back = back(first)
    second = together(near_even, second_other)
    third = together(near_odd, third_other)
    second_ahead = ring(second, third)
    even, home_here = layer_call(
        table,
        (keep, got),
        products=(product,),
        last=home,
        picks=True,
        keeps=True,
        name="expand_home",
    )
    first = [first, first_ahead, ring(first_ahead, even), first_back]
    second_back = back(second, odd)
    odd = to_far_x(after(odd, first[2]))
    even = to_chip(even, 2)
    third_ahead = ring(third)
    second = [second, second_ahead, ring(second_ahead, even), second_back]
    third_back = back(third)
    home_there = to_core(after(home_here, third_ahead))
    third = [third, third_ahead, ring(third_ahead), third_back]

    even = after(even, third_ahead)
    products = layer_call(table, (even, odd), after=first, after_flip=9, name="project_first")
    even, odd, *products = layer_call(
        table,
        (even, odd),
        products=products,
        last=first,
        after=second,
        last_flip=9,
        after_flip=10,
        name="first_second",
    )
    even, odd, *products = layer_call(
        table,
        (even, odd),
        products=products,
        last=second,
        after=third,
        last_flip=10,
        after_flip=10,
        name="second_third",
    )
    keep, give, product = layer_call(
        table,
        (even, odd),
        products=products,
        last=third,
        after=[home_here],
        last_flip=10,
        skip=1,
        swaps=True,
        name="third_home",
    )
    out = final_call(
        table, keep, to_core(give), product, to_core(product), [home_here], [home_there]
    )
    return (*states, out.reshape(hidden_states.shape))


def solution(mesh):
    placed = (
        P("section", "dp", None),
        P("section", "dp", None),
        P("section", "dp", None),
        P("section", "dp", None),
        P("section", None, "dp", None),
    )
    return jax.shard_map(
        per_device,
        mesh=mesh,
        in_specs=placed,
        out_specs=(
            P("section", "dp", None),
            P("section", "dp", None),
            P("section", "dp", None),
            P("section", None, "dp", None),
        ),
        check_vma=False,
    )
```

```python
import dataclasses
import functools

import jax
import jax.numpy as jnp
from jax import lax
from jax.experimental import pallas as pl
from jax.experimental.pallas import tpu as pltpu
from jax.sharding import PartitionSpec as P

ADAM_STEP = 1000

beta_one = 0.9
beta_two = 0.95
learn_rate = 0.0003
decay_rate = 0.1
adam_eps = 1e-08
norm_eps = 1e-05

AXES = ("section", "dp")
D = 8192
KVW = 512
ROWS = 256
SUB = 512
HALF = D // 2
LANES = 128
VMEM = 56 * 1024 * 1024
UPDATE_STEPS = 2
SUB_STEP = SUB // UPDATE_STEPS
COST = pl.CostEstimate(flops=1, bytes_accessed=1, transcendentals=0)
AHEAD = 3


def place(linear):
    section, dp = divmod(linear, 8)
    return section // 2, section % 2, dp // 4, dp % 4


def linear_of(chip, core, xlo, z):
    return ((chip % 8) * 2 + core) * 8 + (xlo % 2) * 4 + z % 4


def shift(value, move):
    pairs = [(source, linear_of(*move(*place(source)))) for source in range(128)]
    return lax.ppermute(value, AXES, pairs)


def to_core(value):
    return shift(value, lambda chip, core, xlo, z: (chip, 1 - core, xlo, z))


def to_pair(value):
    return shift(value, lambda chip, core, xlo, z: (chip, core, xlo + 1, z))


def to_ring(value, way=1):
    return shift(value, lambda chip, core, xlo, z: (chip, core, xlo, z + way * (1 - 2 * core)))


def to_chip(value, steps):
    return shift(value, lambda chip, core, xlo, z: (chip + steps, core, xlo, z))


def to_next_pair(value):
    def move(chip, core, xlo, z):
        return chip + 1, core, xlo + (chip % 4 == 3), z

    return shift(value, move)


def to_far_y(value):
    return shift(
        value,
        lambda chip, core, xlo, z: (chip // 4 * 4 + (chip + 1 - 2 * core) % 4, core, xlo, z),
    )


def to_far_x(value):
    return shift(
        value, lambda chip, core, xlo, z: (chip if chip % 4 >= 2 else chip + 4, core, xlo, z)
    )


def adamw_update(master, moment, second, gradient):
    moment_new = beta_one * moment + (1.0 - beta_one) * gradient
    second_new = beta_two * second + (1.0 - beta_two) * gradient * gradient
    corr_one = 1.0 - beta_one**ADAM_STEP
    corr_two = 1.0 - beta_two**ADAM_STEP
    step_size = moment_new / corr_one / (jnp.sqrt(second_new / corr_two) + adam_eps)
    master_new = master - learn_rate * (step_size + decay_rate * master)
    return (master_new, moment_new, second_new)


def update_kernel(
    core_ref,
    master_ref,
    moment_ref,
    second_ref,
    gradient_ref,
    whole_ref,
    master_out,
    moment_out,
    second_out,
    keep_rows,
    give_rows,
    keep,
    give,
):
    lower = core_ref[0] == 0
    new_master, new_moment, new_second = adamw_update(
        master_ref[...], moment_ref[...], second_ref[...], gradient_ref[...]
    )
    master_out[...] = new_master
    moment_out[...] = new_moment
    second_out[...] = new_second
    first = new_master[0].astype(jnp.bfloat16)
    last = new_master[1].astype(jnp.bfloat16)
    keep_rows[...] = jnp.where(lower, first, last)
    give_rows[...] = jnp.where(lower, last, first)
    for part in range(8 // UPDATE_STEPS):
        first = whole_ref[:, 2 * part * SUB : (2 * part + 1) * SUB]
        last = whole_ref[:, (2 * part + 1) * SUB : (2 * part + 2) * SUB]
        keep[:, part * SUB : (part + 1) * SUB] = jnp.where(lower, first, last)
        give[:, part * SUB : (part + 1) * SUB] = jnp.where(lower, last, first)


def update_call(core, master, moment, second, gradient, whole):
    state = pl.BlockSpec((2, SUB_STEP, KVW), lambda i, core: (0, i, 0))
    half = pl.BlockSpec((SUB_STEP, KVW), lambda i, core: (i, 0))
    part = pl.BlockSpec((ROWS, HALF // UPDATE_STEPS), lambda i, core: (0, i))
    shaped = [a.reshape(2, SUB, KVW) for a in (master, moment, second, gradient)]
    outs = pl.pallas_call(
        update_kernel,
        grid_spec=pltpu.PrefetchScalarGridSpec(
            num_scalar_prefetch=1,
            grid=(UPDATE_STEPS,),
            in_specs=[state] * 4
            + [pl.BlockSpec((ROWS, D // UPDATE_STEPS), lambda i, core: (0, i))],
            out_specs=[state] * 3 + [half] * 2 + [part] * 2,
        ),
        out_shape=[jax.ShapeDtypeStruct((2, SUB, KVW), jnp.float32)] * 3
        + [jax.ShapeDtypeStruct((SUB, KVW), jnp.bfloat16)] * 2
        + [jax.ShapeDtypeStruct((ROWS, HALF), jnp.bfloat16)] * 2,
        compiler_params=pltpu.CompilerParams(vmem_limit_bytes=VMEM),
        cost_estimate=COST,
        name="update",
    )(core, *shaped, whole)
    return [a.reshape(master.shape) for a in outs[:3]], *outs[3:]


def read_columns(table, blocks, slots, sems, order):
    copies = {}
    for chunk in order:
        column = pl.multiple_of(table[chunk], SUB)
        for index, block in enumerate(blocks):
            copies[chunk, index] = pltpu.make_async_copy(
                block.at[:, pl.ds(column, SUB)],
                slots.at[chunk, pl.ds(index * ROWS, ROWS)],
                sems.at[chunk, index],
            )
    return copies


def picked_columns(table, arrays, slots, sems, order):
    return {
        (chunk, 0): Picked(
            table[8],
            *(
                read_columns(table, (array,), slots, sems, (chunk,))[chunk, 0]
                for array in arrays
            ),
        )
        for chunk in order
    }


@dataclasses.dataclass(frozen=True)
class Picked:
    core: jax.Array
    lower: object
    upper: object

    def start(self):
        pl.when(self.core == 0)(self.lower.start)
        pl.when(self.core == 1)(self.upper.start)

    def wait(self):
        self.lower.wait()


def chunks_of(pieces, flip):
    for piece in pieces:
        for start in range(0, piece.shape[0], SUB):
            if flip is not None and piece.shape[0] == 2 * SUB:
                start = pl.multiple_of(start + flip * (SUB - 2 * start), SUB)
            yield piece.at[pl.ds(start, SUB)]


def read_pieces(pieces, slots, sems, flip=None):
    return [
        pltpu.make_async_copy(chunk, slots.at[index], sems.at[index])
        for index, chunk in enumerate(chunks_of(pieces, flip))
    ]


def projected_of(mine, theirs):
    summed = mine[...] + theirs[...]
    scale = lax.rsqrt(summed[:, KVW : KVW + 1] * (1.0 / D) + norm_eps)
    return (summed[:, :KVW] * scale).astype(jnp.bfloat16)


def layer_kernel(plan, *refs):
    refs = list(refs)

    def take(count):
        taken, refs[:count] = refs[:count], []
        return taken

    (table,) = take(1)
    blocks = take(plan.blocks + plan.picks)
    mine = take(plan.blocks if plan.last else 0)
    theirs = take(plan.blocks if plan.last else 0)
    last = take(plan.last)
    after = take(plan.after)
    fresh = take(plan.blocks) if plan.last else []
    kept = take(1) if plan.keeps else []
    out = take(plan.blocks - plan.skip if plan.after else 0)
    columns, column_sems = take(2)
    last_slots, last_sems = take(2) if plan.last else (None, None)
    after_slots, after_sems = take(2) if plan.after else (None, None)
    (store_sems,) = take(1) if plan.last else (None,)
    (keep_sems,) = take(1) if plan.keeps else (None,)

    taken_up = range(plan.first, plan.first + plan.count)
    chunks = range(8) if plan.last else taken_up
    read = picked_columns if plan.picks else read_columns
    reads = read(table, blocks, columns, column_sems, chunks)
    flips = [None if at is None else table[at] for at in (plan.last_flip, plan.after_flip)]
    last_reads = read_pieces(last, last_slots, last_sems, flips[0]) if plan.last else []
    after_reads = read_pieces(after, after_slots, after_sems, flips[1]) if plan.after else []

    def begin(chunk):
        if chunk not in chunks:
            return
        for index in range(plan.blocks):
            reads[chunk, index].start()
        if plan.last:
            last_reads[chunk].start()
        if chunk in taken_up:
            after_reads[chunk - plan.first].start()

    for ahead in range(AHEAD):
        begin(chunks[0] + ahead)
    rows = plan.blocks * ROWS
    if plan.last:
        projected = jnp.concatenate(
            [projected_of(here, there) for here, there in zip(mine, theirs)], axis=0
        )
    skip = plan.skip * ROWS
    if plan.after:
        total = jnp.zeros((rows - skip, KVW), jnp.float32)
        squares = jnp.zeros((rows - skip, 1), jnp.float32)
    stores = []
    for chunk in chunks:
        begin(chunk + AHEAD)
        for index in range(plan.blocks):
            reads[chunk, index].wait()
        part = columns[chunk]
        if plan.last:
            last_reads[chunk].wait()
            if plan.keeps:
                stores.append(
                    pltpu.make_async_copy(
                        last_slots.at[chunk],
                        kept[0].at[pl.ds(chunk * SUB, SUB)],
                        keep_sems.at[chunk],
                    )
                )
                stores[-1].start()
            update = lax.dot_general(
                projected,
                last_slots[chunk],
                (((1,), (1,)), ((), ())),
                preferred_element_type=jnp.float32,
            )
            part = (part.astype(jnp.float32) + update).astype(jnp.bfloat16)
            columns[chunk] = part
            column = pl.multiple_of(table[chunk], SUB)
            if plan.swaps:
                own = table[8]
                sources = [own * ROWS, (1 - own) * ROWS]
            else:
                sources = [index * ROWS for index in range(plan.blocks)]
            for index in range(plan.blocks):
                stores.append(
                    pltpu.make_async_copy(
                        columns.at[chunk, pl.ds(sources[index], ROWS)],
                        fresh[index].at[:, pl.ds(column, SUB)],
                        store_sems.at[chunk, index],
                    )
                )
                stores[-1].start()
        if chunk in taken_up:
            after_reads[chunk - plan.first].wait()
            part = part[skip:]
            total += jnp.dot(
                part,
                after_slots[chunk - plan.first],
                preferred_element_type=jnp.float32,
            )
            flat = part.astype(jnp.float32)
            squares += jnp.sum(flat * flat, axis=1, keepdims=True)
    if plan.after:
        for index, product in enumerate(out):
            part = slice(index * ROWS, (index + 1) * ROWS)
            product[:, :KVW] = total[part]
            product[:, KVW:] = jnp.broadcast_to(squares[part], (ROWS, LANES))
    for store in stores:
        store.wait()


@dataclasses.dataclass(frozen=True)
class Plan:
    blocks: int
    last: int
    after: int
    first: int = 0
    count: int = 0
    skip: int = 0
    swaps: bool = False
    keeps: bool = False
    last_flip: int | None = None
    after_flip: int | None = None
    picks: bool = False


def layer_call(table, blocks, products=(), last=(), after=(), name="layer", **plan):
    count = sum(piece.shape[0] for piece in after) // SUB
    picks = plan.get("picks", False)
    plan = Plan(len(blocks) - picks, len(last), len(after), count=count, **plan)
    sums = (*products, *map(to_core, products))
    rows = plan.blocks * ROWS
    any_space = pl.BlockSpec(memory_space=pl.ANY)
    vmem = pl.BlockSpec(memory_space=pltpu.VMEM)
    out_shape, out_specs = [], []
    scratch = [
        pltpu.VMEM((8, rows, SUB), jnp.bfloat16),
        pltpu.SemaphoreType.DMA((8, plan.blocks)),
    ]
    if plan.last:
        out_shape += [jax.ShapeDtypeStruct((ROWS, HALF), jnp.bfloat16)] * plan.blocks
        out_specs += [any_space] * plan.blocks
        scratch += [pltpu.VMEM((8, SUB, KVW), jnp.bfloat16), pltpu.SemaphoreType.DMA((8,))]
    if plan.keeps:
        out_shape.append(jax.ShapeDtypeStruct((HALF, KVW), jnp.bfloat16))
        out_specs.append(any_space)
    if plan.after:
        ahead = plan.blocks - plan.skip
        out_shape += [jax.ShapeDtypeStruct((ROWS, KVW + LANES), jnp.float32)] * ahead
        out_specs += [vmem] * ahead
        scratch += [
            pltpu.VMEM((plan.count, SUB, KVW), jnp.bfloat16),
            pltpu.SemaphoreType.DMA((plan.count,)),
        ]
    if plan.last:
        scratch.append(pltpu.SemaphoreType.DMA((8, plan.blocks)))
    if plan.keeps:
        scratch.append(pltpu.SemaphoreType.DMA((8,)))
    return pl.pallas_call(
        functools.partial(layer_kernel, plan),
        in_specs=[pl.BlockSpec(memory_space=pltpu.SMEM)]
        + [any_space] * len(blocks)
        + [vmem] * len(sums)
        + [any_space] * len(last)
        + [any_space] * len(after),
        out_specs=out_specs,
        out_shape=out_shape,
        scratch_shapes=scratch,
        compiler_params=pltpu.CompilerParams(vmem_limit_bytes=VMEM),
        cost_estimate=COST,
        name=name,
    )(table, *blocks, *sums, *last, *after)


def final_kernel(table, keep, got, mine, theirs, *refs):
    pieces, (whole, slots, slot_sems, w_slots, w_sems, store_sems) = refs[:-6], refs[-6:]
    upper = table[8] == 1
    reads, stores = [], []
    for chunk in range(16):
        source = keep if chunk < 8 else got
        column = pl.multiple_of(table[(0 if chunk < 8 else 16) + chunk % 8], SUB)
        reads.append(
            pltpu.make_async_copy(
                source.at[:, pl.ds(column, SUB)], slots.at[chunk], slot_sems.at[chunk]
            )
        )
        side = table[8] if chunk < 8 else 1 - table[8]
        target = pl.multiple_of(2 * column + side * SUB, SUB)
        stores.append(
            pltpu.make_async_copy(
                slots.at[chunk], whole.at[:, pl.ds(target, SUB)], store_sems.at[chunk]
            )
        )
    weights = read_pieces(pieces, w_slots, w_sems)

    def begin(chunk):
        if chunk < 16:
            reads[chunk].start()
            weights[chunk].start()

    for ahead in range(2 * AHEAD):
        begin(ahead)
    projected = projected_of(mine, theirs)
    for chunk in range(16):
        begin(chunk + 2 * AHEAD)
        reads[chunk].wait()
        weights[chunk].wait()

        @pl.when(upper)
        def _():
            update = lax.dot_general(
                projected,
                w_slots[chunk],
                (((1,), (1,)), ((), ())),
                preferred_element_type=jnp.float32,
            )
            slots[chunk] = (slots[chunk].astype(jnp.float32) + update).astype(jnp.bfloat16)

        stores[chunk].start()
    for store in stores:
        store.wait()


def final_call(table, keep, got, mine, theirs, here, there):
    any_space = pl.BlockSpec(memory_space=pl.ANY)
    vmem = pl.BlockSpec(memory_space=pltpu.VMEM)
    return pl.pallas_call(
        final_kernel,
        in_specs=[pl.BlockSpec(memory_space=pltpu.SMEM), any_space, any_space, vmem, vmem]
        + [any_space] * (len(here) + len(there)),
        out_specs=any_space,
        out_shape=jax.ShapeDtypeStruct((ROWS, D), jnp.bfloat16),
        scratch_shapes=[
            pltpu.VMEM((16, ROWS, SUB), jnp.bfloat16),
            pltpu.SemaphoreType.DMA((16,)),
            pltpu.VMEM((16, SUB, KVW), jnp.bfloat16),
            pltpu.SemaphoreType.DMA((16,)),
            pltpu.SemaphoreType.DMA((16,)),
        ],
        compiler_params=pltpu.CompilerParams(vmem_limit_bytes=VMEM),
        cost_estimate=COST,
        name="final_layer",
    )(table, keep, got, mine, theirs, *here, *there)


def after(value, *events):
    return lax.optimization_barrier((value, *events))[0]


def together(own, other):
    return jnp.concatenate([own, other], axis=0)


def per_device(master_weights, first_moment, second_moment, gradient_shard, hidden_states):
    core = lax.rem(lax.axis_index("section"), 2)
    xlo = lax.div(lax.axis_index("dp"), 4)
    z = lax.rem(lax.axis_index("dp"), 4)
    upper = core == 1
    core_word = jnp.reshape(core, (1,)).astype(jnp.int32)
    step = jnp.arange(4, dtype=jnp.int32)

    def columns(is_upper):
        owner = lax.rem(z + jnp.where(is_upper, step, 4 - step), 4)
        return jnp.stack([owner + 4 * xlo, owner + 4 * (1 - xlo)], axis=1).reshape(8) * SUB

    y = lax.rem(lax.div(lax.axis_index("section"), 2), 4)
    flips = jnp.stack([y < 2, y == 0]).astype(jnp.int32)
    filler = jnp.zeros((5,), jnp.int32)
    table = jnp.concatenate([columns(upper), core_word, flips, filler, columns(~upper)])
    table = table.astype(jnp.int32)

    states, mine, theirs, keep, give = update_call(
        core_word,
        master_weights,
        first_moment,
        second_moment,
        gradient_shard,
        hidden_states.reshape(ROWS, D),
    )
    other = to_core(theirs)
    even_rows = jnp.where(upper, other, mine)
    odd_rows = jnp.where(upper, mine, other)
    got = to_core(after(give, other))
    odd = jnp.where(upper, keep, got)

    queue = []

    def ring(value, *events, way=1):
        value = to_ring(after(value, *queue[-3:-1], *events), way)
        queue.append(value)
        return value

    def back(value, *events):
        return ring(value, *events, way=-1)

    home_other = to_pair(even_rows)
    own_ahead = ring(even_rows)
    own_back = back(even_rows)
    near_odd = to_next_pair(odd_rows)

    own_two = ring(own_ahead)
    other_ahead = ring(home_other)
    other_back = back(home_other)
    far = to_next_pair(after(near_odd, own_ahead, own_back, home_other, odd))
    near_even = to_next_pair(after(even_rows, near_odd))
    far_other = to_pair(far)
    other_two = ring(other_ahead, far)
    third_other = to_pair(after(near_odd, other_ahead, far))
    odd = to_far_y(after(odd, far, own_two, other_ahead))

    home = [even_rows, home_other, own_ahead, other_ahead, own_two, other_two, own_back, other_back]
    (product,) = layer_call(table, (keep, got), after=home, picks=True, name="project_home")
    second_other = to_pair(after(near_even, product))
    first = together(far, far_other)
    first_ahead = ring(first, near_even, third_other)
    first_back = back(first)
    odd_hop = odd
    odd = to_far_y(after(odd, product))
    second = together(near_even, second_other)
    third = together(near_odd, third_other)
    second_ahead = ring(second, third, odd_hop)
    even, home_here = layer_call(
        table,
        (keep, got),
        products=(product,),
        last=home,
        picks=True,
        keeps=True,
        name="expand_home",
    )
    first = [first, first_ahead, ring(first_ahead, even), first_back]
    second_back = back(second, odd)
    odd = to_far_x(after(odd, first[2]))
    even = to_chip(even, 2)
    third_ahead = ring(third)
    second = [second, second_ahead, ring(second_ahead, even), second_back]
    third_back = back(third)
    home_there = to_core(after(home_here, third_ahead))
    third = [third, third_ahead, ring(third_ahead), third_back]

    even = after(even, third_ahead)
    products = layer_call(table, (even, odd), after=first, after_flip=9, name="project_first")
    even, odd, *products = layer_call(
        table,
        (even, odd),
        products=products,
        last=first,
        after=second,
        last_flip=9,
        after_flip=10,
        name="first_second",
    )
    even, odd, *products = layer_call(
        table,
        (even, odd),
        products=products,
        last=second,
        after=third,
        last_flip=10,
        after_flip=10,
        name="second_third",
    )
    keep, give, product = layer_call(
        table,
        (even, odd),
        products=products,
        last=third,
        after=[home_here],
        last_flip=10,
        skip=1,
        swaps=True,
        name="third_home",
    )
    out = final_call(
        table, keep, to_core(give), product, to_core(product), [home_here], [home_there]
    )
    return (*states, out.reshape(hidden_states.shape))


def solution(mesh):
    placed = (
        P("section", "dp", None),
        P("section", "dp", None),
        P("section", "dp", None),
        P("section", "dp", None),
        P("section", None, "dp", None),
    )
    return jax.shard_map(
        per_device,
        mesh=mesh,
        in_specs=placed,
        out_specs=(
            P("section", "dp", None),
            P("section", "dp", None),
            P("section", "dp", None),
            P("section", None, "dp", None),
        ),
        check_vma=False,
    )
```

```python
import dataclasses
import functools

import jax
import jax.numpy as jnp
from jax import lax
from jax.experimental import pallas as pl
from jax.experimental.pallas import tpu as pltpu
from jax.sharding import PartitionSpec as P

ADAM_STEP = 1000

beta_one = 0.9
beta_two = 0.95
learn_rate = 0.0003
decay_rate = 0.1
adam_eps = 1e-08
norm_eps = 1e-05

AXES = ("section", "dp")
D = 8192
KVW = 512
ROWS = 256
SUB = 512
HALF = D // 2
LANES = 128
VMEM = 28 * 1024 * 1024
UPDATE_STEPS = 2
SUB_STEP = SUB // UPDATE_STEPS
COST = pl.CostEstimate(flops=1, bytes_accessed=1, transcendentals=0)
AHEAD = 3


def place(linear):
    section, dp = divmod(linear, 8)
    return section // 2, section % 2, dp // 4, dp % 4


def linear_of(chip, core, xlo, z):
    return ((chip % 8) * 2 + core) * 8 + (xlo % 2) * 4 + z % 4


def shift(value, move):
    pairs = [(source, linear_of(*move(*place(source)))) for source in range(128)]
    return lax.ppermute(value, AXES, pairs)


def to_core(value):
    return shift(value, lambda chip, core, xlo, z: (chip, 1 - core, xlo, z))


def to_pair(value):
    return shift(value, lambda chip, core, xlo, z: (chip, core, xlo + 1, z))


def to_ring(value, way=1):
    return shift(value, lambda chip, core, xlo, z: (chip, core, xlo, z + way * (1 - 2 * core)))


def to_chip(value, steps):
    return shift(value, lambda chip, core, xlo, z: (chip + steps, core, xlo, z))


def to_next_pair(value):
    def move(chip, core, xlo, z):
        return chip + 1, core, xlo + (chip % 4 == 3), z

    return shift(value, move)


def adamw_update(master, moment, second, gradient):
    moment_new = beta_one * moment + (1.0 - beta_one) * gradient
    second_new = beta_two * second + (1.0 - beta_two) * gradient * gradient
    corr_one = 1.0 - beta_one**ADAM_STEP
    corr_two = 1.0 - beta_two**ADAM_STEP
    step_size = moment_new / corr_one / (jnp.sqrt(second_new / corr_two) + adam_eps)
    master_new = master - learn_rate * (step_size + decay_rate * master)
    return (master_new, moment_new, second_new)


def update_kernel(
    core_ref,
    master_ref,
    moment_ref,
    second_ref,
    gradient_ref,
    whole_ref,
    master_out,
    moment_out,
    second_out,
    keep_rows,
    give_rows,
    keep,
    give,
):
    lower = core_ref[0] == 0
    new_master, new_moment, new_second = adamw_update(
        master_ref[...], moment_ref[...], second_ref[...], gradient_ref[...]
    )
    master_out[...] = new_master
    moment_out[...] = new_moment
    second_out[...] = new_second
    first = new_master[0].astype(jnp.bfloat16)
    last = new_master[1].astype(jnp.bfloat16)
    keep_rows[...] = jnp.where(lower, first, last)
    give_rows[...] = jnp.where(lower, last, first)
    for part in range(8 // UPDATE_STEPS):
        first = whole_ref[:, 2 * part * SUB : (2 * part + 1) * SUB]
        last = whole_ref[:, (2 * part + 1) * SUB : (2 * part + 2) * SUB]
        keep[:, part * SUB : (part + 1) * SUB] = jnp.where(lower, first, last)
        give[:, part * SUB : (part + 1) * SUB] = jnp.where(lower, last, first)


def update_call(core, master, moment, second, gradient, whole):
    state = pl.BlockSpec((2, SUB_STEP, KVW), lambda i, core: (0, i, 0))
    half = pl.BlockSpec((SUB_STEP, KVW), lambda i, core: (i, 0))
    part = pl.BlockSpec((ROWS, HALF // UPDATE_STEPS), lambda i, core: (0, i))
    shaped = [a.reshape(2, SUB, KVW) for a in (master, moment, second, gradient)]
    outs = pl.pallas_call(
        update_kernel,
        grid_spec=pltpu.PrefetchScalarGridSpec(
            num_scalar_prefetch=1,
            grid=(UPDATE_STEPS,),
            in_specs=[state] * 4
            + [pl.BlockSpec((ROWS, D // UPDATE_STEPS), lambda i, core: (0, i))],
            out_specs=[state] * 3 + [half] * 2 + [part] * 2,
        ),
        out_shape=[jax.ShapeDtypeStruct((2, SUB, KVW), jnp.float32)] * 3
        + [jax.ShapeDtypeStruct((SUB, KVW), jnp.bfloat16)] * 2
        + [jax.ShapeDtypeStruct((ROWS, HALF), jnp.bfloat16)] * 2,
        compiler_params=pltpu.CompilerParams(vmem_limit_bytes=VMEM),
        cost_estimate=COST,
        name="update",
    )(core, *shaped, whole)
    return [a.reshape(master.shape) for a in outs[:3]], *outs[3:]


def read_columns(table, blocks, slots, sems, order):
    copies = {}
    for chunk in order:
        column = pl.multiple_of(table[chunk], SUB)
        for index, block in enumerate(blocks):
            copies[chunk, index] = pltpu.make_async_copy(
                block.at[:, pl.ds(column, SUB)],
                slots.at[chunk, pl.ds(index * ROWS, ROWS)],
                sems.at[chunk, index],
            )
    return copies


def picked_columns(table, arrays, slots, sems, order):
    return {
        (chunk, 0): Picked(
            table[8],
            *(
                read_columns(table, (array,), slots, sems, (chunk,))[chunk, 0]
                for array in arrays
            ),
        )
        for chunk in order
    }


@dataclasses.dataclass(frozen=True)
class Picked:
    core: jax.Array
    lower: object
    upper: object

    def start(self):
        pl.when(self.core == 0)(self.lower.start)
        pl.when(self.core == 1)(self.upper.start)

    def wait(self):
        self.lower.wait()


def chunks_of(pieces, flip):
    for piece in pieces:
        for start in range(0, piece.shape[0], SUB):
            if flip is not None and piece.shape[0] == 2 * SUB:
                start = pl.multiple_of(start + flip * (SUB - 2 * start), SUB)
            yield piece.at[pl.ds(start, SUB)]


def read_pieces(pieces, slots, sems, flip=None):
    return [
        pltpu.make_async_copy(chunk, slots.at[index], sems.at[index])
        for index, chunk in enumerate(chunks_of(pieces, flip))
    ]


def projected_of(mine, theirs):
    summed = mine[...] + theirs[...]
    scale = lax.rsqrt(summed[:, KVW : KVW + 1] * (1.0 / D) + norm_eps)
    return (summed[:, :KVW] * scale).astype(jnp.bfloat16)


def layer_kernel(plan, *refs):
    refs = list(refs)

    def take(count):
        taken, refs[:count] = refs[:count], []
        return taken

    (table,) = take(1)
    blocks = take(plan.blocks + plan.picks)
    mine = take(plan.blocks if plan.last else 0)
    theirs = take(plan.blocks if plan.last else 0)
    last = take(plan.last)
    after = take(plan.after)
    fresh = take(plan.blocks) if plan.last else []
    kept = take(1) if plan.keeps else []
    out = take(plan.blocks - plan.skip if plan.after else 0)
    columns, column_sems = take(2)
    last_slots, last_sems = take(2) if plan.last else (None, None)
    after_slots, after_sems = take(2) if plan.after else (None, None)
    (store_sems,) = take(1) if plan.last else (None,)
    (keep_sems,) = take(1) if plan.keeps else (None,)

    taken_up = range(plan.first, plan.first + plan.count)
    chunks = range(8) if plan.last else taken_up
    read = picked_columns if plan.picks else read_columns
    reads = read(table, blocks, columns, column_sems, chunks)
    flips = [None if at is None else table[at] for at in (plan.last_flip, plan.after_flip)]
    last_reads = read_pieces(last, last_slots, last_sems, flips[0]) if plan.last else []
    after_reads = read_pieces(after, after_slots, after_sems, flips[1]) if plan.after else []

    def begin(chunk):
        if chunk not in chunks:
            return
        for index in range(plan.blocks):
            reads[chunk, index].start()
        if plan.last:
            last_reads[chunk].start()
        if chunk in taken_up:
            after_reads[chunk - plan.first].start()

    for ahead in range(AHEAD):
        begin(chunks[0] + ahead)
    rows = plan.blocks * ROWS
    if plan.last:
        projected = jnp.concatenate(
            [projected_of(here, there) for here, there in zip(mine, theirs)], axis=0
        )
    skip = plan.skip * ROWS
    if plan.after:
        total = jnp.zeros((rows - skip, KVW), jnp.float32)
        squares = jnp.zeros((rows - skip, 1), jnp.float32)
    stores = []
    for chunk in chunks:
        begin(chunk + AHEAD)
        for index in range(plan.blocks):
            reads[chunk, index].wait()
        part = columns[chunk]
        if plan.last:
            last_reads[chunk].wait()
            if plan.keeps:
                stores.append(
                    pltpu.make_async_copy(
                        last_slots.at[chunk],
                        kept[0].at[pl.ds(chunk * SUB, SUB)],
                        keep_sems.at[chunk],
                    )
                )
                stores[-1].start()
            update = lax.dot_general(
                projected,
                last_slots[chunk],
                (((1,), (1,)), ((), ())),
                preferred_element_type=jnp.float32,
            )
            part = (part.astype(jnp.float32) + update).astype(jnp.bfloat16)
            columns[chunk] = part
            column = pl.multiple_of(table[chunk], SUB)
            if plan.swaps:
                own = table[8]
                sources = [own * ROWS, (1 - own) * ROWS]
            else:
                sources = [index * ROWS for index in range(plan.blocks)]
            for index in range(plan.blocks):
                stores.append(
                    pltpu.make_async_copy(
                        columns.at[chunk, pl.ds(sources[index], ROWS)],
                        fresh[index].at[:, pl.ds(column, SUB)],
                        store_sems.at[chunk, index],
                    )
                )
                stores[-1].start()
        if chunk in taken_up:
            after_reads[chunk - plan.first].wait()
            part = part[skip:]
            total += jnp.dot(
                part,
                after_slots[chunk - plan.first],
                preferred_element_type=jnp.float32,
            )
            flat = part.astype(jnp.float32)
            squares += jnp.sum(flat * flat, axis=1, keepdims=True)
    if plan.after:
        for index, product in enumerate(out):
            part = slice(index * ROWS, (index + 1) * ROWS)
            product[:, :KVW] = total[part]
            product[:, KVW:] = jnp.broadcast_to(squares[part], (ROWS, LANES))
    for store in stores:
        store.wait()


@dataclasses.dataclass(frozen=True)
class Plan:
    blocks: int
    last: int
    after: int
    first: int = 0
    count: int = 0
    skip: int = 0
    swaps: bool = False
    keeps: bool = False
    last_flip: int | None = None
    after_flip: int | None = None
    picks: bool = False


def layer_call(table, blocks, products=(), last=(), after=(), name="layer", **plan):
    count = sum(piece.shape[0] for piece in after) // SUB
    picks = plan.get("picks", False)
    plan = Plan(len(blocks) - picks, len(last), len(after), count=count, **plan)
    sums = (*products, *map(to_core, products))
    rows = plan.blocks * ROWS
    any_space = pl.BlockSpec(memory_space=pl.ANY)
    vmem = pl.BlockSpec(memory_space=pltpu.VMEM)
    out_shape, out_specs = [], []
    scratch = [
        pltpu.VMEM((8, rows, SUB), jnp.bfloat16),
        pltpu.SemaphoreType.DMA((8, plan.blocks)),
    ]
    if plan.last:
        out_shape += [jax.ShapeDtypeStruct((ROWS, HALF), jnp.bfloat16)] * plan.blocks
        out_specs += [any_space] * plan.blocks
        scratch += [pltpu.VMEM((8, SUB, KVW), jnp.bfloat16), pltpu.SemaphoreType.DMA((8,))]
    if plan.keeps:
        out_shape.append(jax.ShapeDtypeStruct((HALF, KVW), jnp.bfloat16))
        out_specs.append(any_space)
    if plan.after:
        ahead = plan.blocks - plan.skip
        out_shape += [jax.ShapeDtypeStruct((ROWS, KVW + LANES), jnp.float32)] * ahead
        out_specs += [vmem] * ahead
        scratch += [
            pltpu.VMEM((plan.count, SUB, KVW), jnp.bfloat16),
            pltpu.SemaphoreType.DMA((plan.count,)),
        ]
    if plan.last:
        scratch.append(pltpu.SemaphoreType.DMA((8, plan.blocks)))
    if plan.keeps:
        scratch.append(pltpu.SemaphoreType.DMA((8,)))
    return pl.pallas_call(
        functools.partial(layer_kernel, plan),
        in_specs=[pl.BlockSpec(memory_space=pltpu.SMEM)]
        + [any_space] * len(blocks)
        + [vmem] * len(sums)
        + [any_space] * len(last)
        + [any_space] * len(after),
        out_specs=out_specs,
        out_shape=out_shape,
        scratch_shapes=scratch,
        compiler_params=pltpu.CompilerParams(vmem_limit_bytes=VMEM),
        cost_estimate=COST,
        name=name,
    )(table, *blocks, *sums, *last, *after)


def final_kernel(table, keep, got, mine, theirs, *refs):
    pieces, (whole, slots, slot_sems, w_slots, w_sems, store_sems) = refs[:-6], refs[-6:]
    upper = table[8] == 1
    reads, stores = [], []
    for chunk in range(16):
        source = keep if chunk < 8 else got
        column = pl.multiple_of(table[(0 if chunk < 8 else 16) + chunk % 8], SUB)
        reads.append(
            pltpu.make_async_copy(
                source.at[:, pl.ds(column, SUB)], slots.at[chunk], slot_sems.at[chunk]
            )
        )
        side = table[8] if chunk < 8 else 1 - table[8]
        target = pl.multiple_of(2 * column + side * SUB, SUB)
        stores.append(
            pltpu.make_async_copy(
                slots.at[chunk], whole.at[:, pl.ds(target, SUB)], store_sems.at[chunk]
            )
        )
    weights = read_pieces(pieces, w_slots, w_sems)

    def begin(chunk):
        if chunk < 16:
            reads[chunk].start()
            weights[chunk].start()

    for ahead in range(2 * AHEAD):
        begin(ahead)
    projected = projected_of(mine, theirs)
    for chunk in range(16):
        begin(chunk + 2 * AHEAD)
        reads[chunk].wait()
        weights[chunk].wait()

        @pl.when(upper)
        def _():
            update = lax.dot_general(
                projected,
                w_slots[chunk],
                (((1,), (1,)), ((), ())),
                preferred_element_type=jnp.float32,
            )
            slots[chunk] = (slots[chunk].astype(jnp.float32) + update).astype(jnp.bfloat16)

        stores[chunk].start()
    for store in stores:
        store.wait()


def final_call(table, keep, got, mine, theirs, here, there):
    any_space = pl.BlockSpec(memory_space=pl.ANY)
    vmem = pl.BlockSpec(memory_space=pltpu.VMEM)
    return pl.pallas_call(
        final_kernel,
        in_specs=[pl.BlockSpec(memory_space=pltpu.SMEM), any_space, any_space, vmem, vmem]
        + [any_space] * (len(here) + len(there)),
        out_specs=any_space,
        out_shape=jax.ShapeDtypeStruct((ROWS, D), jnp.bfloat16),
        scratch_shapes=[
            pltpu.VMEM((16, ROWS, SUB), jnp.bfloat16),
            pltpu.SemaphoreType.DMA((16,)),
            pltpu.VMEM((16, SUB, KVW), jnp.bfloat16),
            pltpu.SemaphoreType.DMA((16,)),
            pltpu.SemaphoreType.DMA((16,)),
        ],
        compiler_params=pltpu.CompilerParams(vmem_limit_bytes=VMEM),
        cost_estimate=COST,
        name="final_layer",
    )(table, keep, got, mine, theirs, *here, *there)


def after(value, *events):
    return lax.optimization_barrier((value, *events))[0]


def together(own, other):
    return jnp.concatenate([own, other], axis=0)


def per_device(master_weights, first_moment, second_moment, gradient_shard, hidden_states):
    core = lax.rem(lax.axis_index("section"), 2)
    xlo = lax.div(lax.axis_index("dp"), 4)
    z = lax.rem(lax.axis_index("dp"), 4)
    upper = core == 1
    core_word = jnp.reshape(core, (1,)).astype(jnp.int32)
    step = jnp.arange(4, dtype=jnp.int32)

    def columns(is_upper):
        owner = lax.rem(z + jnp.where(is_upper, step, 4 - step), 4)
        return jnp.stack([owner + 4 * xlo, owner + 4 * (1 - xlo)], axis=1).reshape(8) * SUB

    y = lax.rem(lax.div(lax.axis_index("section"), 2), 4)
    flips = jnp.stack([y < 2, y == 0]).astype(jnp.int32)
    filler = jnp.zeros((5,), jnp.int32)
    table = jnp.concatenate([columns(upper), core_word, flips, filler, columns(~upper)])
    table = table.astype(jnp.int32)

    states, mine, theirs, keep, give = update_call(
        core_word,
        master_weights,
        first_moment,
        second_moment,
        gradient_shard,
        hidden_states.reshape(ROWS, D),
    )
    other = to_core(theirs)
    even_rows = jnp.where(upper, other, mine)
    odd_rows = jnp.where(upper, mine, other)
    got = to_core(after(give, other))
    odd = jnp.where(upper, keep, got)

    queue = []

    def ring(value, *events, way=1):
        value = to_ring(after(value, *queue[-3:-1], *events), way)
        queue.append(value)
        return value

    def back(value, *events):
        return ring(value, *events, way=-1)

    home_other = to_pair(even_rows)
    own_ahead = ring(even_rows)
    own_back = back(even_rows)
    near_odd = to_next_pair(odd_rows)

    own_two = ring(own_ahead)
    other_ahead = ring(home_other)
    other_back = back(home_other)
    far = to_next_pair(after(near_odd, own_ahead, own_back, home_other, odd))
    near_even = to_next_pair(after(even_rows, near_odd))
    other_two = ring(other_ahead, far)
    far_other = to_pair(far)
    third_other = to_pair(after(near_odd, far, other_ahead))
    odd = to_chip(after(odd, near_odd), 2)

    home = [even_rows, home_other, own_ahead, other_ahead, own_two, other_two, own_back, other_back]
    (product,) = layer_call(table, (keep, got), after=home, picks=True, name="project_home")
    first = together(far, far_other)
    first_ahead = ring(first, near_even, third_other)
    first_back = back(first)
    even, home_here = layer_call(
        table,
        (keep, got),
        products=(product,),
        last=home,
        picks=True,
        keeps=True,
        name="expand_home",
    )
    second_other = to_pair(after(near_even, odd, even))
    even = to_chip(even, 2)
    second = together(near_even, second_other)
    third = together(near_odd, third_other)
    second_ahead = ring(second, third)
    first = [first, first_ahead, ring(first_ahead), first_back]
    second_back = back(second)
    third_ahead = ring(third)
    second = [second, second_ahead, ring(second_ahead, even), second_back]
    third_back = back(third)
    home_there = to_core(after(home_here, third_ahead))
    third = [third, third_ahead, ring(third_ahead), third_back]

    even = after(even, third_ahead)
    products = layer_call(table, (even, odd), after=first, after_flip=9, name="project_first")
    even, odd, *products = layer_call(
        table,
        (even, odd),
        products=products,
        last=first,
        after=second,
        last_flip=9,
        after_flip=10,
        name="first_second",
    )
    even, odd, *products = layer_call(
        table,
        (even, odd),
        products=products,
        last=second,
        after=third,
        last_flip=10,
        after_flip=10,
        name="second_third",
    )
    keep, give, product = layer_call(
        table,
        (even, odd),
        products=products,
        last=third,
        after=[home_here],
        last_flip=10,
        skip=1,
        swaps=True,
        name="third_home",
    )
    out = final_call(
        table, keep, to_core(give), product, to_core(product), [home_here], [home_there]
    )
    return (*states, out.reshape(hidden_states.shape))


def solution(mesh):
    placed = (
        P("section", "dp", None),
        P("section", "dp", None),
        P("section", "dp", None),
        P("section", "dp", None),
        P("section", None, "dp", None),
    )
    return jax.shard_map(
        per_device,
        mesh=mesh,
        in_specs=placed,
        out_specs=(
            P("section", "dp", None),
            P("section", "dp", None),
            P("section", "dp", None),
            P("section", None, "dp", None),
        ),
        check_vma=False,
    )
```

```python
import dataclasses
import functools

import jax
import jax.numpy as jnp
from jax import lax
from jax.experimental import pallas as pl
from jax.experimental.pallas import tpu as pltpu
from jax.sharding import PartitionSpec as P

ADAM_STEP = 1000

beta_one = 0.9
beta_two = 0.95
learn_rate = 0.0003
decay_rate = 0.1
adam_eps = 1e-08
norm_eps = 1e-05

AXES = ("section", "dp")
D = 8192
KVW = 512
ROWS = 256
SUB = 512
HALF = D // 2
LANES = 128
VMEM = 28 * 1024 * 1024
UPDATE_STEPS = 2
SUB_STEP = SUB // UPDATE_STEPS
COST = pl.CostEstimate(flops=1, bytes_accessed=1, transcendentals=0)
AHEAD = 3


def place(linear):
    section, dp = divmod(linear, 8)
    return section // 2, section % 2, dp // 4, dp % 4


def linear_of(chip, core, xlo, z):
    return ((chip % 8) * 2 + core) * 8 + (xlo % 2) * 4 + z % 4


def shift(value, move):
    pairs = [(source, linear_of(*move(*place(source)))) for source in range(128)]
    return lax.ppermute(value, AXES, pairs)


def to_core(value):
    return shift(value, lambda chip, core, xlo, z: (chip, 1 - core, xlo, z))


def to_pair(value):
    return shift(value, lambda chip, core, xlo, z: (chip, core, xlo + 1, z))


def to_ring(value, way=1):
    return shift(value, lambda chip, core, xlo, z: (chip, core, xlo, z + way * (1 - 2 * core)))


def to_chip(value, steps):
    return shift(value, lambda chip, core, xlo, z: (chip + steps, core, xlo, z))


def to_next_pair(value):
    def move(chip, core, xlo, z):
        return chip + 1, core, xlo + (chip % 4 == 3), z

    return shift(value, move)


def adamw_update(master, moment, second, gradient):
    moment_new = beta_one * moment + (1.0 - beta_one) * gradient
    second_new = beta_two * second + (1.0 - beta_two) * gradient * gradient
    corr_one = 1.0 - beta_one**ADAM_STEP
    corr_two = 1.0 - beta_two**ADAM_STEP
    step_size = moment_new / corr_one / (jnp.sqrt(second_new / corr_two) + adam_eps)
    master_new = master - learn_rate * (step_size + decay_rate * master)
    return (master_new, moment_new, second_new)


def update_kernel(
    core_ref,
    master_ref,
    moment_ref,
    second_ref,
    gradient_ref,
    whole_ref,
    master_out,
    moment_out,
    second_out,
    keep_rows,
    give_rows,
    keep,
    give,
):
    lower = core_ref[0] == 0
    new_master, new_moment, new_second = adamw_update(
        master_ref[...], moment_ref[...], second_ref[...], gradient_ref[...]
    )
    master_out[...] = new_master
    moment_out[...] = new_moment
    second_out[...] = new_second
    first = new_master[0].astype(jnp.bfloat16)
    last = new_master[1].astype(jnp.bfloat16)
    keep_rows[...] = jnp.where(lower, first, last)
    give_rows[...] = jnp.where(lower, last, first)
    for part in range(8 // UPDATE_STEPS):
        first = whole_ref[:, 2 * part * SUB : (2 * part + 1) * SUB]
        last = whole_ref[:, (2 * part + 1) * SUB : (2 * part + 2) * SUB]
        keep[:, part * SUB : (part + 1) * SUB] = jnp.where(lower, first, last)
        give[:, part * SUB : (part + 1) * SUB] = jnp.where(lower, last, first)


def update_call(core, master, moment, second, gradient, whole):
    state = pl.BlockSpec((2, SUB_STEP, KVW), lambda i, core: (0, i, 0))
    half = pl.BlockSpec((SUB_STEP, KVW), lambda i, core: (i, 0))
    part = pl.BlockSpec((ROWS, HALF // UPDATE_STEPS), lambda i, core: (0, i))
    shaped = [a.reshape(2, SUB, KVW) for a in (master, moment, second, gradient)]
    outs = pl.pallas_call(
        update_kernel,
        grid_spec=pltpu.PrefetchScalarGridSpec(
            num_scalar_prefetch=1,
            grid=(UPDATE_STEPS,),
            in_specs=[state] * 4
            + [pl.BlockSpec((ROWS, D // UPDATE_STEPS), lambda i, core: (0, i))],
            out_specs=[state] * 3 + [half] * 2 + [part] * 2,
        ),
        out_shape=[jax.ShapeDtypeStruct((2, SUB, KVW), jnp.float32)] * 3
        + [jax.ShapeDtypeStruct((SUB, KVW), jnp.bfloat16)] * 2
        + [jax.ShapeDtypeStruct((ROWS, HALF), jnp.bfloat16)] * 2,
        compiler_params=pltpu.CompilerParams(vmem_limit_bytes=VMEM),
        cost_estimate=COST,
        name="update",
    )(core, *shaped, whole)
    return [a.reshape(master.shape) for a in outs[:3]], *outs[3:]


def read_columns(table, blocks, slots, sems, order):
    copies = {}
    for chunk in order:
        column = pl.multiple_of(table[chunk], SUB)
        for index, block in enumerate(blocks):
            copies[chunk, index] = pltpu.make_async_copy(
                block.at[:, pl.ds(column, SUB)],
                slots.at[chunk, pl.ds(index * ROWS, ROWS)],
                sems.at[chunk, index],
            )
    return copies


def picked_columns(table, arrays, slots, sems, order):
    return {
        (chunk, 0): Picked(
            table[8],
            *(
                read_columns(table, (array,), slots, sems, (chunk,))[chunk, 0]
                for array in arrays
            ),
        )
        for chunk in order
    }


@dataclasses.dataclass(frozen=True)
class Picked:
    core: jax.Array
    lower: object
    upper: object

    def start(self):
        pl.when(self.core == 0)(self.lower.start)
        pl.when(self.core == 1)(self.upper.start)

    def wait(self):
        self.lower.wait()


def chunks_of(pieces, flip):
    for piece in pieces:
        for start in range(0, piece.shape[0], SUB):
            if flip is not None and piece.shape[0] == 2 * SUB:
                start = pl.multiple_of(start + flip * (SUB - 2 * start), SUB)
            yield piece.at[pl.ds(start, SUB)]


def read_pieces(pieces, slots, sems, flip=None):
    return [
        pltpu.make_async_copy(chunk, slots.at[index], sems.at[index])
        for index, chunk in enumerate(chunks_of(pieces, flip))
    ]


def projected_of(mine, theirs):
    summed = mine[...] + theirs[...]
    scale = lax.rsqrt(summed[:, KVW : KVW + 1] * (1.0 / D) + norm_eps)
    return (summed[:, :KVW] * scale).astype(jnp.bfloat16)


def layer_kernel(plan, *refs):
    refs = list(refs)

    def take(count):
        taken, refs[:count] = refs[:count], []
        return taken

    (table,) = take(1)
    blocks = take(plan.blocks + plan.picks)
    mine = take(plan.blocks if plan.last else 0)
    theirs = take(plan.blocks if plan.last else 0)
    last = take(plan.last)
    after = take(plan.after)
    fresh = take(plan.blocks) if plan.last else []
    kept = take(1) if plan.keeps else []
    out = take(plan.blocks - plan.skip if plan.after else 0)
    columns, column_sems = take(2)
    last_slots, last_sems = take(2) if plan.last else (None, None)
    after_slots, after_sems = take(2) if plan.after else (None, None)
    (store_sems,) = take(1) if plan.last else (None,)
    (keep_sems,) = take(1) if plan.keeps else (None,)

    taken_up = range(plan.first, plan.first + plan.count)
    chunks = range(8) if plan.last else taken_up
    read = picked_columns if plan.picks else read_columns
    reads = read(table, blocks, columns, column_sems, chunks)
    flips = [None if at is None else table[at] for at in (plan.last_flip, plan.after_flip)]
    last_reads = read_pieces(last, last_slots, last_sems, flips[0]) if plan.last else []
    after_reads = read_pieces(after, after_slots, after_sems, flips[1]) if plan.after else []

    def begin(chunk):
        if chunk not in chunks:
            return
        for index in range(plan.blocks):
            reads[chunk, index].start()
        if plan.last:
            last_reads[chunk].start()
        if chunk in taken_up:
            after_reads[chunk - plan.first].start()

    for ahead in range(AHEAD):
        begin(chunks[0] + ahead)
    rows = plan.blocks * ROWS
    if plan.last:
        projected = jnp.concatenate(
            [projected_of(here, there) for here, there in zip(mine, theirs)], axis=0
        )
    skip = plan.skip * ROWS
    if plan.after:
        total = jnp.zeros((rows - skip, KVW), jnp.float32)
        squares = jnp.zeros((rows - skip, 1), jnp.float32)
    stores = []
    for chunk in chunks:
        begin(chunk + AHEAD)
        for index in range(plan.blocks):
            reads[chunk, index].wait()
        part = columns[chunk]
        if plan.last:
            last_reads[chunk].wait()
            if plan.keeps:
                stores.append(
                    pltpu.make_async_copy(
                        last_slots.at[chunk],
                        kept[0].at[pl.ds(chunk * SUB, SUB)],
                        keep_sems.at[chunk],
                    )
                )
                stores[-1].start()
            update = lax.dot_general(
                projected,
                last_slots[chunk],
                (((1,), (1,)), ((), ())),
                preferred_element_type=jnp.float32,
            )
            part = (part.astype(jnp.float32) + update).astype(jnp.bfloat16)
            columns[chunk] = part
            column = pl.multiple_of(table[chunk], SUB)
            if plan.swaps:
                own = table[8]
                sources = [own * ROWS, (1 - own) * ROWS]
            else:
                sources = [index * ROWS for index in range(plan.blocks)]
            for index in range(plan.blocks):
                stores.append(
                    pltpu.make_async_copy(
                        columns.at[chunk, pl.ds(sources[index], ROWS)],
                        fresh[index].at[:, pl.ds(column, SUB)],
                        store_sems.at[chunk, index],
                    )
                )
                stores[-1].start()
        if chunk in taken_up:
            after_reads[chunk - plan.first].wait()
            part = part[skip:]
            total += jnp.dot(
                part,
                after_slots[chunk - plan.first],
                preferred_element_type=jnp.float32,
            )
            flat = part.astype(jnp.float32)
            squares += jnp.sum(flat * flat, axis=1, keepdims=True)
    if plan.after:
        for index, product in enumerate(out):
            part = slice(index * ROWS, (index + 1) * ROWS)
            product[:, :KVW] = total[part]
            product[:, KVW:] = jnp.broadcast_to(squares[part], (ROWS, LANES))
    for store in stores:
        store.wait()


@dataclasses.dataclass(frozen=True)
class Plan:
    blocks: int
    last: int
    after: int
    first: int = 0
    count: int = 0
    skip: int = 0
    swaps: bool = False
    keeps: bool = False
    last_flip: int | None = None
    after_flip: int | None = None
    picks: bool = False


def layer_call(table, blocks, products=(), last=(), after=(), name="layer", **plan):
    count = sum(piece.shape[0] for piece in after) // SUB
    picks = plan.get("picks", False)
    plan = Plan(len(blocks) - picks, len(last), len(after), count=count, **plan)
    sums = (*products, *map(to_core, products))
    rows = plan.blocks * ROWS
    any_space = pl.BlockSpec(memory_space=pl.ANY)
    vmem = pl.BlockSpec(memory_space=pltpu.VMEM)
    out_shape, out_specs = [], []
    scratch = [
        pltpu.VMEM((8, rows, SUB), jnp.bfloat16),
        pltpu.SemaphoreType.DMA((8, plan.blocks)),
    ]
    if plan.last:
        out_shape += [jax.ShapeDtypeStruct((ROWS, HALF), jnp.bfloat16)] * plan.blocks
        out_specs += [any_space] * plan.blocks
        scratch += [pltpu.VMEM((8, SUB, KVW), jnp.bfloat16), pltpu.SemaphoreType.DMA((8,))]
    if plan.keeps:
        out_shape.append(jax.ShapeDtypeStruct((HALF, KVW), jnp.bfloat16))
        out_specs.append(any_space)
    if plan.after:
        ahead = plan.blocks - plan.skip
        out_shape += [jax.ShapeDtypeStruct((ROWS, KVW + LANES), jnp.float32)] * ahead
        out_specs += [vmem] * ahead
        scratch += [
            pltpu.VMEM((plan.count, SUB, KVW), jnp.bfloat16),
            pltpu.SemaphoreType.DMA((plan.count,)),
        ]
    if plan.last:
        scratch.append(pltpu.SemaphoreType.DMA((8, plan.blocks)))
    if plan.keeps:
        scratch.append(pltpu.SemaphoreType.DMA((8,)))
    return pl.pallas_call(
        functools.partial(layer_kernel, plan),
        in_specs=[pl.BlockSpec(memory_space=pltpu.SMEM)]
        + [any_space] * len(blocks)
        + [vmem] * len(sums)
        + [any_space] * len(last)
        + [any_space] * len(after),
        out_specs=out_specs,
        out_shape=out_shape,
        scratch_shapes=scratch,
        compiler_params=pltpu.CompilerParams(vmem_limit_bytes=VMEM),
        cost_estimate=COST,
        name=name,
    )(table, *blocks, *sums, *last, *after)


def final_kernel(table, keep, got, mine, theirs, *refs):
    pieces, (whole, slots, slot_sems, w_slots, w_sems, store_sems) = refs[:-6], refs[-6:]
    upper = table[8] == 1
    reads, stores = [], []
    for chunk in range(16):
        source = keep if chunk < 8 else got
        column = pl.multiple_of(table[(0 if chunk < 8 else 16) + chunk % 8], SUB)
        reads.append(
            pltpu.make_async_copy(
                source.at[:, pl.ds(column, SUB)], slots.at[chunk], slot_sems.at[chunk]
            )
        )
        side = table[8] if chunk < 8 else 1 - table[8]
        target = pl.multiple_of(2 * column + side * SUB, SUB)
        stores.append(
            pltpu.make_async_copy(
                slots.at[chunk], whole.at[:, pl.ds(target, SUB)], store_sems.at[chunk]
            )
        )
    weights = read_pieces(pieces, w_slots, w_sems)

    def begin(chunk):
        if chunk < 16:
            reads[chunk].start()
            weights[chunk].start()

    for ahead in range(2 * AHEAD):
        begin(ahead)
    projected = projected_of(mine, theirs)
    for chunk in range(16):
        begin(chunk + 2 * AHEAD)
        reads[chunk].wait()
        weights[chunk].wait()

        @pl.when(upper)
        def _():
            update = lax.dot_general(
                projected,
                w_slots[chunk],
                (((1,), (1,)), ((), ())),
                preferred_element_type=jnp.float32,
            )
            slots[chunk] = (slots[chunk].astype(jnp.float32) + update).astype(jnp.bfloat16)

        stores[chunk].start()
    for store in stores:
        store.wait()


def final_call(table, keep, got, mine, theirs, here, there):
    any_space = pl.BlockSpec(memory_space=pl.ANY)
    vmem = pl.BlockSpec(memory_space=pltpu.VMEM)
    return pl.pallas_call(
        final_kernel,
        in_specs=[pl.BlockSpec(memory_space=pltpu.SMEM), any_space, any_space, vmem, vmem]
        + [any_space] * (len(here) + len(there)),
        out_specs=any_space,
        out_shape=jax.ShapeDtypeStruct((ROWS, D), jnp.bfloat16),
        scratch_shapes=[
            pltpu.VMEM((16, ROWS, SUB), jnp.bfloat16),
            pltpu.SemaphoreType.DMA((16,)),
            pltpu.VMEM((16, SUB, KVW), jnp.bfloat16),
            pltpu.SemaphoreType.DMA((16,)),
            pltpu.SemaphoreType.DMA((16,)),
        ],
        compiler_params=pltpu.CompilerParams(vmem_limit_bytes=VMEM),
        cost_estimate=COST,
        name="final_layer",
    )(table, keep, got, mine, theirs, *here, *there)


def after(value, *events):
    return lax.optimization_barrier((value, *events))[0]


def together(own, other):
    return jnp.concatenate([own, other], axis=0)


def per_device(master_weights, first_moment, second_moment, gradient_shard, hidden_states):
    core = lax.rem(lax.axis_index("section"), 2)
    xlo = lax.div(lax.axis_index("dp"), 4)
    z = lax.rem(lax.axis_index("dp"), 4)
    upper = core == 1
    core_word = jnp.reshape(core, (1,)).astype(jnp.int32)
    step = jnp.arange(4, dtype=jnp.int32)

    def columns(is_upper):
        owner = lax.rem(z + jnp.where(is_upper, step, 4 - step), 4)
        return jnp.stack([owner + 4 * xlo, owner + 4 * (1 - xlo)], axis=1).reshape(8) * SUB

    y = lax.rem(lax.div(lax.axis_index("section"), 2), 4)
    flips = jnp.stack([y < 2, y == 0]).astype(jnp.int32)
    filler = jnp.zeros((5,), jnp.int32)
    table = jnp.concatenate([columns(upper), core_word, flips, filler, columns(~upper)])
    table = table.astype(jnp.int32)

    states, mine, theirs, keep, give = update_call(
        core_word,
        master_weights,
        first_moment,
        second_moment,
        gradient_shard,
        hidden_states.reshape(ROWS, D),
    )
    other = to_core(theirs)
    even_rows = jnp.where(upper, other, mine)
    odd_rows = jnp.where(upper, mine, other)
    got = to_core(after(give, other))
    odd = jnp.where(upper, keep, got)

    queue = []

    def ring(value, *events, way=1):
        value = to_ring(after(value, *queue[-3:-1], *events), way)
        queue.append(value)
        return value

    home_own = [even_rows, ring(even_rows)]
    own_back = ring(even_rows, way=-1)
    home_other = to_pair(even_rows)
    near_odd = to_next_pair(odd_rows)

    home_own += [ring(home_own[1], odd), own_back]
    home_others = [home_other, ring(home_other, near_odd)]
    other_back = ring(home_other, way=-1)
    far = to_next_pair(near_odd)
    near_even = to_next_pair(after(even_rows, near_odd))
    third_other = to_pair(near_odd)

    home_others += [ring(home_others[1]), other_back]
    far_other = to_pair(far)
    odd = to_chip(after(odd, far), 2)

    home = [piece for pair in zip(home_own, home_others) for piece in pair]
    (product,) = layer_call(table, (keep, got), after=home, picks=True, name="project_home")
    second_other = to_pair(after(near_even, product))
    first = [together(far, far_other)]
    first.append(ring(first[0], near_even, third_other, home_others[2]))
    second = [together(near_even, second_other)]
    third = [together(near_odd, third_other)]
    second.append(ring(second[0], third[0]))
    first.append(ring(first[1]))
    even, home_here = layer_call(
        table,
        (keep, got),
        products=(product,),
        last=home,
        picks=True,
        keeps=True,
        name="expand_home",
    )
    third.append(ring(third[0], even))
    even = to_chip(even, 2)
    first.append(ring(first[2], odd))
    second.append(ring(second[1]))
    third.append(ring(third[1]))
    second.append(ring(second[2], even))
    home_there = to_core(after(home_here, third[2]))
    third.append(ring(third[2]))

    even = after(even, third[2])
    products = layer_call(table, (even, odd), after=first, after_flip=9, name="project_first")
    even, odd, *products = layer_call(
        table,
        (even, odd),
        products=products,
        last=first,
        after=second,
        last_flip=9,
        after_flip=10,
        name="first_second",
    )
    even, odd, *products = layer_call(
        table,
        (even, odd),
        products=products,
        last=second,
        after=third,
        last_flip=10,
        after_flip=10,
        name="second_third",
    )
    keep, give, product = layer_call(
        table,
        (even, odd),
        products=products,
        last=third,
        after=[home_here],
        last_flip=10,
        skip=1,
        swaps=True,
        name="third_home",
    )
    out = final_call(
        table, keep, to_core(give), product, to_core(product), [home_here], [home_there]
    )
    return (*states, out.reshape(hidden_states.shape))


def solution(mesh):
    placed = (
        P("section", "dp", None),
        P("section", "dp", None),
        P("section", "dp", None),
        P("section", "dp", None),
        P("section", None, "dp", None),
    )
    return jax.shard_map(
        per_device,
        mesh=mesh,
        in_specs=placed,
        out_specs=(
            P("section", "dp", None),
            P("section", "dp", None),
            P("section", "dp", None),
            P("section", None, "dp", None),
        ),
        check_vma=False,
    )
```

```python
import dataclasses
import functools

import jax
import jax.numpy as jnp
from jax import lax
from jax.experimental import pallas as pl
from jax.experimental.pallas import tpu as pltpu
from jax.sharding import PartitionSpec as P

ADAM_STEP = 1000

beta_one = 0.9
beta_two = 0.95
learn_rate = 0.0003
decay_rate = 0.1
adam_eps = 1e-08
norm_eps = 1e-05

AXES = ("section", "dp")
D = 8192
KVW = 512
ROWS = 256
SUB = 512
HALF = D // 2
LANES = 128
VMEM = 28 * 1024 * 1024
UPDATE_VMEM = 56 * 1024 * 1024
UPDATE_STEPS = 2
SUB_STEP = SUB // UPDATE_STEPS
COST = pl.CostEstimate(flops=1, bytes_accessed=1, transcendentals=0)
AHEAD = 3


def place(linear):
    section, dp = divmod(linear, 8)
    return section // 2, section % 2, dp // 4, dp % 4


def linear_of(chip, core, xlo, z):
    return ((chip % 8) * 2 + core) * 8 + (xlo % 2) * 4 + z % 4


def shift(value, move):
    pairs = [(source, linear_of(*move(*place(source)))) for source in range(128)]
    return lax.ppermute(value, AXES, pairs)


def to_core(value):
    return shift(value, lambda chip, core, xlo, z: (chip, 1 - core, xlo, z))


def to_pair(value):
    return shift(value, lambda chip, core, xlo, z: (chip, core, xlo + 1, z))


def to_ring(value):
    return shift(value, lambda chip, core, xlo, z: (chip, core, xlo, z + 1 - 2 * core))


def to_chip(value, steps):
    return shift(value, lambda chip, core, xlo, z: (chip + steps, core, xlo, z))


def to_next_pair(value):
    def move(chip, core, xlo, z):
        return chip + 1, core, xlo + (chip % 4 == 3), z

    return shift(value, move)


def adamw_update(master, moment, second, gradient):
    moment_new = beta_one * moment + (1.0 - beta_one) * gradient
    second_new = beta_two * second + (1.0 - beta_two) * gradient * gradient
    corr_one = 1.0 - beta_one**ADAM_STEP
    corr_two = 1.0 - beta_two**ADAM_STEP
    step_size = moment_new / corr_one / (jnp.sqrt(second_new / corr_two) + adam_eps)
    master_new = master - learn_rate * (step_size + decay_rate * master)
    return (master_new, moment_new, second_new)


def update_kernel(
    core_ref,
    master_ref,
    moment_ref,
    second_ref,
    gradient_ref,
    whole_ref,
    master_out,
    moment_out,
    second_out,
    keep_rows,
    give_rows,
    keep,
    give,
):
    lower = core_ref[0] == 0
    new_master, new_moment, new_second = adamw_update(
        master_ref[...], moment_ref[...], second_ref[...], gradient_ref[...]
    )
    master_out[...] = new_master
    moment_out[...] = new_moment
    second_out[...] = new_second
    first = new_master[0].astype(jnp.bfloat16)
    last = new_master[1].astype(jnp.bfloat16)
    keep_rows[...] = jnp.where(lower, first, last)
    give_rows[...] = jnp.where(lower, last, first)
    for part in range(8 // UPDATE_STEPS):
        first = whole_ref[:, 2 * part * SUB : (2 * part + 1) * SUB]
        last = whole_ref[:, (2 * part + 1) * SUB : (2 * part + 2) * SUB]
        keep[:, part * SUB : (part + 1) * SUB] = jnp.where(lower, first, last)
        give[:, part * SUB : (part + 1) * SUB] = jnp.where(lower, last, first)


def update_call(core, master, moment, second, gradient, whole):
    state = pl.BlockSpec((2, SUB_STEP, KVW), lambda i, core: (0, i, 0))
    half = pl.BlockSpec((SUB_STEP, KVW), lambda i, core: (i, 0))
    part = pl.BlockSpec((ROWS, HALF // UPDATE_STEPS), lambda i, core: (0, i))
    shaped = [a.reshape(2, SUB, KVW) for a in (master, moment, second, gradient)]
    outs = pl.pallas_call(
        update_kernel,
        grid_spec=pltpu.PrefetchScalarGridSpec(
            num_scalar_prefetch=1,
            grid=(UPDATE_STEPS,),
            in_specs=[state] * 4
            + [pl.BlockSpec((ROWS, D // UPDATE_STEPS), lambda i, core: (0, i))],
            out_specs=[state] * 3 + [half] * 2 + [part] * 2,
        ),
        out_shape=[jax.ShapeDtypeStruct((2, SUB, KVW), jnp.float32)] * 3
        + [jax.ShapeDtypeStruct((SUB, KVW), jnp.bfloat16)] * 2
        + [jax.ShapeDtypeStruct((ROWS, HALF), jnp.bfloat16)] * 2,
        compiler_params=pltpu.CompilerParams(vmem_limit_bytes=UPDATE_VMEM),
        cost_estimate=COST,
        name="update",
    )(core, *shaped, whole)
    return [a.reshape(master.shape) for a in outs[:3]], *outs[3:]


def read_columns(table, blocks, slots, sems, order):
    copies = {}
    for chunk in order:
        column = pl.multiple_of(table[chunk], SUB)
        for index, block in enumerate(blocks):
            copies[chunk, index] = pltpu.make_async_copy(
                block.at[:, pl.ds(column, SUB)],
                slots.at[chunk, pl.ds(index * ROWS, ROWS)],
                sems.at[chunk, index],
            )
    return copies


def picked_columns(table, arrays, slots, sems, order):
    return {
        (chunk, 0): Picked(
            table[8],
            *(
                read_columns(table, (array,), slots, sems, (chunk,))[chunk, 0]
                for array in arrays
            ),
        )
        for chunk in order
    }


@dataclasses.dataclass(frozen=True)
class Picked:
    core: jax.Array
    lower: object
    upper: object

    def start(self):
        pl.when(self.core == 0)(self.lower.start)
        pl.when(self.core == 1)(self.upper.start)

    def wait(self):
        self.lower.wait()


def chunks_of(pieces, flip):
    for piece in pieces:
        for start in range(0, piece.shape[0], SUB):
            if flip is not None and piece.shape[0] == 2 * SUB:
                start = pl.multiple_of(start + flip * (SUB - 2 * start), SUB)
            yield piece.at[pl.ds(start, SUB)]


def read_pieces(pieces, slots, sems, flip=None):
    return [
        pltpu.make_async_copy(chunk, slots.at[index], sems.at[index])
        for index, chunk in enumerate(chunks_of(pieces, flip))
    ]


def projected_of(mine, theirs):
    summed = mine[...] + theirs[...]
    scale = lax.rsqrt(summed[:, KVW : KVW + 1] * (1.0 / D) + norm_eps)
    return (summed[:, :KVW] * scale).astype(jnp.bfloat16)


def layer_kernel(plan, *refs):
    refs = list(refs)

    def take(count):
        taken, refs[:count] = refs[:count], []
        return taken

    (table,) = take(1)
    blocks = take(plan.blocks + plan.picks)
    mine = take(plan.blocks if plan.last else 0)
    theirs = take(plan.blocks if plan.last else 0)
    last = take(plan.last)
    after = take(plan.after)
    fresh = take(plan.blocks) if plan.last else []
    kept = take(1) if plan.keeps else []
    out = take(plan.blocks - plan.skip if plan.after else 0)
    columns, column_sems = take(2)
    last_slots, last_sems = take(2) if plan.last else (None, None)
    after_slots, after_sems = take(2) if plan.after else (None, None)
    (store_sems,) = take(1) if plan.last else (None,)
    (keep_sems,) = take(1) if plan.keeps else (None,)

    taken_up = range(plan.first, plan.first + plan.count)
    chunks = range(8) if plan.last else taken_up
    read = picked_columns if plan.picks else read_columns
    reads = read(table, blocks, columns, column_sems, chunks)
    flips = [None if at is None else table[at] for at in (plan.last_flip, plan.after_flip)]
    last_reads = read_pieces(last, last_slots, last_sems, flips[0]) if plan.last else []
    after_reads = read_pieces(after, after_slots, after_sems, flips[1]) if plan.after else []

    def begin(chunk):
        if chunk not in chunks:
            return
        for index in range(plan.blocks):
            reads[chunk, index].start()
        if plan.last:
            last_reads[chunk].start()
        if chunk in taken_up:
            after_reads[chunk - plan.first].start()

    for ahead in range(AHEAD):
        begin(chunks[0] + ahead)
    rows = plan.blocks * ROWS
    if plan.last:
        projected = jnp.concatenate(
            [projected_of(here, there) for here, there in zip(mine, theirs)], axis=0
        )
    skip = plan.skip * ROWS
    if plan.after:
        total = jnp.zeros((rows - skip, KVW), jnp.float32)
        squares = jnp.zeros((rows - skip, 1), jnp.float32)
    stores = []
    for chunk in chunks:
        begin(chunk + AHEAD)
        for index in range(plan.blocks):
            reads[chunk, index].wait()
        part = columns[chunk]
        if plan.last:
            last_reads[chunk].wait()
            if plan.keeps:
                stores.append(
                    pltpu.make_async_copy(
                        last_slots.at[chunk],
                        kept[0].at[pl.ds(chunk * SUB, SUB)],
                        keep_sems.at[chunk],
                    )
                )
                stores[-1].start()
            update = lax.dot_general(
                projected,
                last_slots[chunk],
                (((1,), (1,)), ((), ())),
                preferred_element_type=jnp.float32,
            )
            part = (part.astype(jnp.float32) + update).astype(jnp.bfloat16)
            columns[chunk] = part
            column = pl.multiple_of(table[chunk], SUB)
            if plan.swaps:
                own = table[8]
                sources = [own * ROWS, (1 - own) * ROWS]
            else:
                sources = [index * ROWS for index in range(plan.blocks)]
            for index in range(plan.blocks):
                stores.append(
                    pltpu.make_async_copy(
                        columns.at[chunk, pl.ds(sources[index], ROWS)],
                        fresh[index].at[:, pl.ds(column, SUB)],
                        store_sems.at[chunk, index],
                    )
                )
                stores[-1].start()
        if chunk in taken_up:
            after_reads[chunk - plan.first].wait()
            part = part[skip:]
            total += jnp.dot(
                part,
                after_slots[chunk - plan.first],
                preferred_element_type=jnp.float32,
            )
            flat = part.astype(jnp.float32)
            squares += jnp.sum(flat * flat, axis=1, keepdims=True)
    if plan.after:
        for index, product in enumerate(out):
            part = slice(index * ROWS, (index + 1) * ROWS)
            product[:, :KVW] = total[part]
            product[:, KVW:] = jnp.broadcast_to(squares[part], (ROWS, LANES))
    for store in stores:
        store.wait()


@dataclasses.dataclass(frozen=True)
class Plan:
    blocks: int
    last: int
    after: int
    first: int = 0
    count: int = 0
    skip: int = 0
    swaps: bool = False
    keeps: bool = False
    last_flip: int | None = None
    after_flip: int | None = None
    picks: bool = False


def layer_call(table, blocks, products=(), last=(), after=(), name="layer", **plan):
    count = sum(piece.shape[0] for piece in after) // SUB
    picks = plan.get("picks", False)
    plan = Plan(len(blocks) - picks, len(last), len(after), count=count, **plan)
    sums = (*products, *map(to_core, products))
    rows = plan.blocks * ROWS
    any_space = pl.BlockSpec(memory_space=pl.ANY)
    vmem = pl.BlockSpec(memory_space=pltpu.VMEM)
    out_shape, out_specs = [], []
    scratch = [
        pltpu.VMEM((8, rows, SUB), jnp.bfloat16),
        pltpu.SemaphoreType.DMA((8, plan.blocks)),
    ]
    if plan.last:
        out_shape += [jax.ShapeDtypeStruct((ROWS, HALF), jnp.bfloat16)] * plan.blocks
        out_specs += [any_space] * plan.blocks
        scratch += [pltpu.VMEM((8, SUB, KVW), jnp.bfloat16), pltpu.SemaphoreType.DMA((8,))]
    if plan.keeps:
        out_shape.append(jax.ShapeDtypeStruct((HALF, KVW), jnp.bfloat16))
        out_specs.append(any_space)
    if plan.after:
        ahead = plan.blocks - plan.skip
        out_shape += [jax.ShapeDtypeStruct((ROWS, KVW + LANES), jnp.float32)] * ahead
        out_specs += [vmem] * ahead
        scratch += [
            pltpu.VMEM((plan.count, SUB, KVW), jnp.bfloat16),
            pltpu.SemaphoreType.DMA((plan.count,)),
        ]
    if plan.last:
        scratch.append(pltpu.SemaphoreType.DMA((8, plan.blocks)))
    if plan.keeps:
        scratch.append(pltpu.SemaphoreType.DMA((8,)))
    return pl.pallas_call(
        functools.partial(layer_kernel, plan),
        in_specs=[pl.BlockSpec(memory_space=pltpu.SMEM)]
        + [any_space] * len(blocks)
        + [vmem] * len(sums)
        + [any_space] * len(last)
        + [any_space] * len(after),
        out_specs=out_specs,
        out_shape=out_shape,
        scratch_shapes=scratch,
        compiler_params=pltpu.CompilerParams(vmem_limit_bytes=VMEM),
        cost_estimate=COST,
        name=name,
    )(table, *blocks, *sums, *last, *after)


def final_kernel(table, keep, got, mine, theirs, *refs):
    pieces, (whole, slots, slot_sems, w_slots, w_sems, store_sems) = refs[:-6], refs[-6:]
    upper = table[8] == 1
    reads, stores = [], []
    for chunk in range(16):
        source = keep if chunk < 8 else got
        column = pl.multiple_of(table[(0 if chunk < 8 else 16) + chunk % 8], SUB)
        reads.append(
            pltpu.make_async_copy(
                source.at[:, pl.ds(column, SUB)], slots.at[chunk], slot_sems.at[chunk]
            )
        )
        side = table[8] if chunk < 8 else 1 - table[8]
        target = pl.multiple_of(2 * column + side * SUB, SUB)
        stores.append(
            pltpu.make_async_copy(
                slots.at[chunk], whole.at[:, pl.ds(target, SUB)], store_sems.at[chunk]
            )
        )
    weights = read_pieces(pieces, w_slots, w_sems)

    def begin(chunk):
        if chunk < 16:
            reads[chunk].start()
            weights[chunk].start()

    for ahead in range(2 * AHEAD):
        begin(ahead)
    projected = projected_of(mine, theirs)
    for chunk in range(16):
        begin(chunk + 2 * AHEAD)
        reads[chunk].wait()
        weights[chunk].wait()

        @pl.when(upper)
        def _():
            update = lax.dot_general(
                projected,
                w_slots[chunk],
                (((1,), (1,)), ((), ())),
                preferred_element_type=jnp.float32,
            )
            slots[chunk] = (slots[chunk].astype(jnp.float32) + update).astype(jnp.bfloat16)

        stores[chunk].start()
    for store in stores:
        store.wait()


def final_call(table, keep, got, mine, theirs, here, there):
    any_space = pl.BlockSpec(memory_space=pl.ANY)
    vmem = pl.BlockSpec(memory_space=pltpu.VMEM)
    return pl.pallas_call(
        final_kernel,
        in_specs=[pl.BlockSpec(memory_space=pltpu.SMEM), any_space, any_space, vmem, vmem]
        + [any_space] * (len(here) + len(there)),
        out_specs=any_space,
        out_shape=jax.ShapeDtypeStruct((ROWS, D), jnp.bfloat16),
        scratch_shapes=[
            pltpu.VMEM((16, ROWS, SUB), jnp.bfloat16),
            pltpu.SemaphoreType.DMA((16,)),
            pltpu.VMEM((16, SUB, KVW), jnp.bfloat16),
            pltpu.SemaphoreType.DMA((16,)),
            pltpu.SemaphoreType.DMA((16,)),
        ],
        compiler_params=pltpu.CompilerParams(vmem_limit_bytes=VMEM),
        cost_estimate=COST,
        name="final_layer",
    )(table, keep, got, mine, theirs, *here, *there)


def after(value, *events):
    return lax.optimization_barrier((value, *events))[0]


def together(own, other):
    return jnp.concatenate([own, other], axis=0)


def per_device(master_weights, first_moment, second_moment, gradient_shard, hidden_states):
    core = lax.rem(lax.axis_index("section"), 2)
    xlo = lax.div(lax.axis_index("dp"), 4)
    z = lax.rem(lax.axis_index("dp"), 4)
    upper = core == 1
    core_word = jnp.reshape(core, (1,)).astype(jnp.int32)
    step = jnp.arange(4, dtype=jnp.int32)

    def columns(is_upper):
        owner = lax.rem(z + jnp.where(is_upper, step, 4 - step), 4)
        return jnp.stack([owner + 4 * xlo, owner + 4 * (1 - xlo)], axis=1).reshape(8) * SUB

    y = lax.rem(lax.div(lax.axis_index("section"), 2), 4)
    flips = jnp.stack([y < 2, y == 0]).astype(jnp.int32)
    filler = jnp.zeros((5,), jnp.int32)
    table = jnp.concatenate([columns(upper), core_word, flips, filler, columns(~upper)])
    table = table.astype(jnp.int32)

    states, mine, theirs, keep, give = update_call(
        core_word,
        master_weights,
        first_moment,
        second_moment,
        gradient_shard,
        hidden_states.reshape(ROWS, D),
    )
    other = to_core(theirs)
    even_rows = jnp.where(upper, other, mine)
    odd_rows = jnp.where(upper, mine, other)
    got = to_core(after(give, other))
    odd = jnp.where(upper, keep, got)

    queue = []

    def ring(value, *events):
        value = to_ring(after(value, *queue[-3:-1], *events))
        queue.append(value)
        return value

    home_own = [even_rows, ring(even_rows)]
    home_other = to_pair(even_rows)
    near_odd = to_next_pair(odd_rows)

    home_own.append(ring(home_own[1], odd))
    home_others = [home_other, ring(home_other, near_odd)]
    far = to_next_pair(near_odd)
    near_even = to_next_pair(after(even_rows, near_odd))
    third_other = to_pair(near_odd)

    home_own.append(ring(home_own[2]))
    home_others.append(ring(home_others[1], far, third_other))
    far_other = to_pair(far)
    home_others.append(ring(home_others[2], near_even))
    second_other = to_pair(near_even)
    odd = to_chip(after(odd, near_even), 2)

    home = [piece for pair in zip(home_own, home_others) for piece in pair]
    (product,) = layer_call(table, (keep, got), after=home, picks=True, name="project_home")
    first = [together(far, far_other)]
    first.append(ring(first[0]))
    second = [together(near_even, second_other)]
    third = [together(near_odd, third_other)]
    second.append(ring(second[0], third[0]))
    first.append(ring(first[1]))
    even, home_here = layer_call(
        table,
        (keep, got),
        products=(product,),
        last=home,
        picks=True,
        keeps=True,
        name="expand_home",
    )
    third.append(ring(third[0], even))
    even = to_chip(even, 2)
    first.append(ring(first[2]))
    second.append(ring(second[1], odd))
    third.append(ring(third[1]))
    second.append(ring(second[2]))
    home_there = to_core(after(home_here, third[2]))
    third.append(ring(third[2]))

    even = after(even, third[2])
    products = layer_call(table, (even, odd), after=first, after_flip=9, name="project_first")
    even, odd, *products = layer_call(
        table,
        (even, odd),
        products=products,
        last=first,
        after=second,
        last_flip=9,
        after_flip=10,
        name="first_second",
    )
    even, odd, *products = layer_call(
        table,
        (even, odd),
        products=products,
        last=second,
        after=third,
        last_flip=10,
        after_flip=10,
        name="second_third",
    )
    keep, give, product = layer_call(
        table,
        (even, odd),
        products=products,
        last=third,
        after=[home_here],
        last_flip=10,
        skip=1,
        swaps=True,
        name="third_home",
    )
    out = final_call(
        table, keep, to_core(give), product, to_core(product), [home_here], [home_there]
    )
    return (*states, out.reshape(hidden_states.shape))


def solution(mesh):
    placed = (
        P("section", "dp", None),
        P("section", "dp", None),
        P("section", "dp", None),
        P("section", "dp", None),
        P("section", None, "dp", None),
    )
    return jax.shard_map(
        per_device,
        mesh=mesh,
        in_specs=placed,
        out_specs=(
            P("section", "dp", None),
            P("section", "dp", None),
            P("section", "dp", None),
            P("section", None, "dp", None),
        ),
        check_vma=False,
    )
```

```python
import dataclasses
import functools

import jax
import jax.numpy as jnp
from jax import lax
from jax.experimental import pallas as pl
from jax.experimental.pallas import tpu as pltpu
from jax.sharding import PartitionSpec as P

ADAM_STEP = 1000

beta_one = 0.9
beta_two = 0.95
learn_rate = 0.0003
decay_rate = 0.1
adam_eps = 1e-08
norm_eps = 1e-05

AXES = ("section", "dp")
D = 8192
KVW = 512
ROWS = 256
SUB = 512
HALF = D // 2
LANES = 128
VMEM = 22 * 1024 * 1024
UPDATE_VMEM = 56 * 1024 * 1024
UPDATE_STEPS = 2
SUB_STEP = SUB // UPDATE_STEPS
COST = pl.CostEstimate(flops=1, bytes_accessed=1, transcendentals=0)
AHEAD = 3


def place(linear):
    section, dp = divmod(linear, 8)
    return section // 2, section % 2, dp // 4, dp % 4


def linear_of(chip, core, xlo, z):
    return ((chip % 8) * 2 + core) * 8 + (xlo % 2) * 4 + z % 4


def shift(value, move):
    pairs = [(source, linear_of(*move(*place(source)))) for source in range(128)]
    return lax.ppermute(value, AXES, pairs)


def to_core(value):
    return shift(value, lambda chip, core, xlo, z: (chip, 1 - core, xlo, z))


def to_pair(value):
    return shift(value, lambda chip, core, xlo, z: (chip, core, xlo + 1, z))


def to_ring(value):
    return shift(value, lambda chip, core, xlo, z: (chip, core, xlo, z + 1 - 2 * core))


def to_chip(value, steps):
    return shift(value, lambda chip, core, xlo, z: (chip + steps, core, xlo, z))


def to_next_pair(value):
    def move(chip, core, xlo, z):
        return chip + 1, core, xlo + (chip % 4 == 3), z

    return shift(value, move)


def adamw_update(master, moment, second, gradient):
    moment_new = beta_one * moment + (1.0 - beta_one) * gradient
    second_new = beta_two * second + (1.0 - beta_two) * gradient * gradient
    corr_one = 1.0 - beta_one**ADAM_STEP
    corr_two = 1.0 - beta_two**ADAM_STEP
    step_size = moment_new / corr_one / (jnp.sqrt(second_new / corr_two) + adam_eps)
    master_new = master - learn_rate * (step_size + decay_rate * master)
    return (master_new, moment_new, second_new)


def update_kernel(
    core_ref,
    master_ref,
    moment_ref,
    second_ref,
    gradient_ref,
    whole_ref,
    master_out,
    moment_out,
    second_out,
    keep_rows,
    give_rows,
    keep,
    give,
):
    lower = core_ref[0] == 0
    new_master, new_moment, new_second = adamw_update(
        master_ref[...], moment_ref[...], second_ref[...], gradient_ref[...]
    )
    master_out[...] = new_master
    moment_out[...] = new_moment
    second_out[...] = new_second
    first = new_master[0].astype(jnp.bfloat16)
    last = new_master[1].astype(jnp.bfloat16)
    keep_rows[...] = jnp.where(lower, first, last)
    give_rows[...] = jnp.where(lower, last, first)
    for part in range(8 // UPDATE_STEPS):
        first = whole_ref[:, 2 * part * SUB : (2 * part + 1) * SUB]
        last = whole_ref[:, (2 * part + 1) * SUB : (2 * part + 2) * SUB]
        keep[:, part * SUB : (part + 1) * SUB] = jnp.where(lower, first, last)
        give[:, part * SUB : (part + 1) * SUB] = jnp.where(lower, last, first)


def update_call(core, master, moment, second, gradient, whole):
    state = pl.BlockSpec((2, SUB_STEP, KVW), lambda i, core: (0, i, 0))
    half = pl.BlockSpec((SUB_STEP, KVW), lambda i, core: (i, 0))
    part = pl.BlockSpec((ROWS, HALF // UPDATE_STEPS), lambda i, core: (0, i))
    shaped = [a.reshape(2, SUB, KVW) for a in (master, moment, second, gradient)]
    outs = pl.pallas_call(
        update_kernel,
        grid_spec=pltpu.PrefetchScalarGridSpec(
            num_scalar_prefetch=1,
            grid=(UPDATE_STEPS,),
            in_specs=[state] * 4
            + [pl.BlockSpec((ROWS, D // UPDATE_STEPS), lambda i, core: (0, i))],
            out_specs=[state] * 3 + [half] * 2 + [part] * 2,
        ),
        out_shape=[jax.ShapeDtypeStruct((2, SUB, KVW), jnp.float32)] * 3
        + [jax.ShapeDtypeStruct((SUB, KVW), jnp.bfloat16)] * 2
        + [jax.ShapeDtypeStruct((ROWS, HALF), jnp.bfloat16)] * 2,
        compiler_params=pltpu.CompilerParams(vmem_limit_bytes=UPDATE_VMEM),
        cost_estimate=COST,
        name="update",
    )(core, *shaped, whole)
    return [a.reshape(master.shape) for a in outs[:3]], *outs[3:]


def read_columns(table, blocks, slots, sems, order):
    copies = {}
    for chunk in order:
        column = pl.multiple_of(table[chunk], SUB)
        for index, block in enumerate(blocks):
            copies[chunk, index] = pltpu.make_async_copy(
                block.at[:, pl.ds(column, SUB)],
                slots.at[chunk, pl.ds(index * ROWS, ROWS)],
                sems.at[chunk, index],
            )
    return copies


def picked_columns(table, arrays, slots, sems, order):
    return {
        (chunk, 0): Picked(
            table[8],
            *(
                read_columns(table, (array,), slots, sems, (chunk,))[chunk, 0]
                for array in arrays
            ),
        )
        for chunk in order
    }


@dataclasses.dataclass(frozen=True)
class Picked:
    core: jax.Array
    lower: object
    upper: object

    def start(self):
        pl.when(self.core == 0)(self.lower.start)
        pl.when(self.core == 1)(self.upper.start)

    def wait(self):
        self.lower.wait()


def chunks_of(pieces, flip):
    for piece in pieces:
        for start in range(0, piece.shape[0], SUB):
            if flip is not None and piece.shape[0] == 2 * SUB:
                start = pl.multiple_of(start + flip * (SUB - 2 * start), SUB)
            yield piece.at[pl.ds(start, SUB)]


def read_pieces(pieces, slots, sems, flip=None):
    return [
        pltpu.make_async_copy(chunk, slots.at[index], sems.at[index])
        for index, chunk in enumerate(chunks_of(pieces, flip))
    ]


def projected_of(mine, theirs):
    summed = mine[...] + theirs[...]
    scale = lax.rsqrt(summed[:, KVW : KVW + 1] * (1.0 / D) + norm_eps)
    return (summed[:, :KVW] * scale).astype(jnp.bfloat16)


def layer_kernel(plan, *refs):
    refs = list(refs)

    def take(count):
        taken, refs[:count] = refs[:count], []
        return taken

    (table,) = take(1)
    blocks = take(plan.blocks + plan.picks)
    mine = take(plan.blocks if plan.last else 0)
    theirs = take(plan.blocks if plan.last else 0)
    last = take(plan.last)
    after = take(plan.after)
    fresh = take(plan.blocks) if plan.last else []
    kept = take(1) if plan.keeps else []
    out = take(plan.blocks - plan.skip if plan.after else 0)
    columns, column_sems = take(2)
    last_slots, last_sems = take(2) if plan.last else (None, None)
    after_slots, after_sems = take(2) if plan.after else (None, None)
    (store_sems,) = take(1) if plan.last else (None,)
    (keep_sems,) = take(1) if plan.keeps else (None,)

    taken_up = range(plan.first, plan.first + plan.count)
    chunks = range(8) if plan.last else taken_up
    read = picked_columns if plan.picks else read_columns
    reads = read(table, blocks, columns, column_sems, chunks)
    flips = [None if at is None else table[at] for at in (plan.last_flip, plan.after_flip)]
    last_reads = read_pieces(last, last_slots, last_sems, flips[0]) if plan.last else []
    after_reads = read_pieces(after, after_slots, after_sems, flips[1]) if plan.after else []

    def begin(chunk):
        if chunk not in chunks:
            return
        for index in range(plan.blocks):
            reads[chunk, index].start()
        if plan.last:
            last_reads[chunk].start()
        if chunk in taken_up:
            after_reads[chunk - plan.first].start()

    for ahead in range(AHEAD):
        begin(chunks[0] + ahead)
    rows = plan.blocks * ROWS
    if plan.last:
        projected = jnp.concatenate(
            [projected_of(here, there) for here, there in zip(mine, theirs)], axis=0
        )
    skip = plan.skip * ROWS
    if plan.after:
        total = jnp.zeros((rows - skip, KVW), jnp.float32)
        squares = jnp.zeros((rows - skip, 1), jnp.float32)
    stores = []
    for chunk in chunks:
        begin(chunk + AHEAD)
        for index in range(plan.blocks):
            reads[chunk, index].wait()
        part = columns[chunk]
        if plan.last:
            last_reads[chunk].wait()
            if plan.keeps:
                stores.append(
                    pltpu.make_async_copy(
                        last_slots.at[chunk],
                        kept[0].at[pl.ds(chunk * SUB, SUB)],
                        keep_sems.at[chunk],
                    )
                )
                stores[-1].start()
            update = lax.dot_general(
                projected,
                last_slots[chunk],
                (((1,), (1,)), ((), ())),
                preferred_element_type=jnp.float32,
            )
            part = (part.astype(jnp.float32) + update).astype(jnp.bfloat16)
            columns[chunk] = part
            column = pl.multiple_of(table[chunk], SUB)
            if plan.swaps:
                own = table[8]
                sources = [own * ROWS, (1 - own) * ROWS]
            else:
                sources = [index * ROWS for index in range(plan.blocks)]
            for index in range(plan.blocks):
                stores.append(
                    pltpu.make_async_copy(
                        columns.at[chunk, pl.ds(sources[index], ROWS)],
                        fresh[index].at[:, pl.ds(column, SUB)],
                        store_sems.at[chunk, index],
                    )
                )
                stores[-1].start()
        if chunk in taken_up:
            after_reads[chunk - plan.first].wait()
            part = part[skip:]
            total += jnp.dot(
                part,
                after_slots[chunk - plan.first],
                preferred_element_type=jnp.float32,
            )
            flat = part.astype(jnp.float32)
            squares += jnp.sum(flat * flat, axis=1, keepdims=True)
    if plan.after:
        for index, product in enumerate(out):
            part = slice(index * ROWS, (index + 1) * ROWS)
            product[:, :KVW] = total[part]
            product[:, KVW:] = jnp.broadcast_to(squares[part], (ROWS, LANES))
    for store in stores:
        store.wait()


@dataclasses.dataclass(frozen=True)
class Plan:
    blocks: int
    last: int
    after: int
    first: int = 0
    count: int = 0
    skip: int = 0
    swaps: bool = False
    keeps: bool = False
    last_flip: int | None = None
    after_flip: int | None = None
    picks: bool = False


def layer_call(table, blocks, products=(), last=(), after=(), name="layer", **plan):
    count = sum(piece.shape[0] for piece in after) // SUB
    picks = plan.get("picks", False)
    plan = Plan(len(blocks) - picks, len(last), len(after), count=count, **plan)
    sums = (*products, *map(to_core, products))
    rows = plan.blocks * ROWS
    any_space = pl.BlockSpec(memory_space=pl.ANY)
    vmem = pl.BlockSpec(memory_space=pltpu.VMEM)
    out_shape, out_specs = [], []
    scratch = [
        pltpu.VMEM((8, rows, SUB), jnp.bfloat16),
        pltpu.SemaphoreType.DMA((8, plan.blocks)),
    ]
    if plan.last:
        out_shape += [jax.ShapeDtypeStruct((ROWS, HALF), jnp.bfloat16)] * plan.blocks
        out_specs += [any_space] * plan.blocks
        scratch += [pltpu.VMEM((8, SUB, KVW), jnp.bfloat16), pltpu.SemaphoreType.DMA((8,))]
    if plan.keeps:
        out_shape.append(jax.ShapeDtypeStruct((HALF, KVW), jnp.bfloat16))
        out_specs.append(any_space)
    if plan.after:
        ahead = plan.blocks - plan.skip
        out_shape += [jax.ShapeDtypeStruct((ROWS, KVW + LANES), jnp.float32)] * ahead
        out_specs += [vmem] * ahead
        scratch += [
            pltpu.VMEM((plan.count, SUB, KVW), jnp.bfloat16),
            pltpu.SemaphoreType.DMA((plan.count,)),
        ]
    if plan.last:
        scratch.append(pltpu.SemaphoreType.DMA((8, plan.blocks)))
    if plan.keeps:
        scratch.append(pltpu.SemaphoreType.DMA((8,)))
    return pl.pallas_call(
        functools.partial(layer_kernel, plan),
        in_specs=[pl.BlockSpec(memory_space=pltpu.SMEM)]
        + [any_space] * len(blocks)
        + [vmem] * len(sums)
        + [any_space] * len(last)
        + [any_space] * len(after),
        out_specs=out_specs,
        out_shape=out_shape,
        scratch_shapes=scratch,
        compiler_params=pltpu.CompilerParams(vmem_limit_bytes=VMEM),
        cost_estimate=COST,
        name=name,
    )(table, *blocks, *sums, *last, *after)


def final_kernel(table, keep, got, mine, theirs, *refs):
    pieces, (whole, slots, slot_sems, w_slots, w_sems, store_sems) = refs[:-6], refs[-6:]
    upper = table[8] == 1
    reads, stores = [], []
    for chunk in range(16):
        source = keep if chunk < 8 else got
        column = pl.multiple_of(table[(0 if chunk < 8 else 16) + chunk % 8], SUB)
        reads.append(
            pltpu.make_async_copy(
                source.at[:, pl.ds(column, SUB)], slots.at[chunk], slot_sems.at[chunk]
            )
        )
        side = table[8] if chunk < 8 else 1 - table[8]
        target = pl.multiple_of(2 * column + side * SUB, SUB)
        stores.append(
            pltpu.make_async_copy(
                slots.at[chunk], whole.at[:, pl.ds(target, SUB)], store_sems.at[chunk]
            )
        )
    weights = read_pieces(pieces, w_slots, w_sems)

    def begin(chunk):
        if chunk < 16:
            reads[chunk].start()
            weights[chunk].start()

    for ahead in range(2 * AHEAD):
        begin(ahead)
    projected = projected_of(mine, theirs)
    for chunk in range(16):
        begin(chunk + 2 * AHEAD)
        reads[chunk].wait()
        weights[chunk].wait()

        @pl.when(upper)
        def _():
            update = lax.dot_general(
                projected,
                w_slots[chunk],
                (((1,), (1,)), ((), ())),
                preferred_element_type=jnp.float32,
            )
            slots[chunk] = (slots[chunk].astype(jnp.float32) + update).astype(jnp.bfloat16)

        stores[chunk].start()
    for store in stores:
        store.wait()


def final_call(table, keep, got, mine, theirs, here, there):
    any_space = pl.BlockSpec(memory_space=pl.ANY)
    vmem = pl.BlockSpec(memory_space=pltpu.VMEM)
    return pl.pallas_call(
        final_kernel,
        in_specs=[pl.BlockSpec(memory_space=pltpu.SMEM), any_space, any_space, vmem, vmem]
        + [any_space] * (len(here) + len(there)),
        out_specs=any_space,
        out_shape=jax.ShapeDtypeStruct((ROWS, D), jnp.bfloat16),
        scratch_shapes=[
            pltpu.VMEM((16, ROWS, SUB), jnp.bfloat16),
            pltpu.SemaphoreType.DMA((16,)),
            pltpu.VMEM((16, SUB, KVW), jnp.bfloat16),
            pltpu.SemaphoreType.DMA((16,)),
            pltpu.SemaphoreType.DMA((16,)),
        ],
        compiler_params=pltpu.CompilerParams(vmem_limit_bytes=VMEM),
        cost_estimate=COST,
        name="final_layer",
    )(table, keep, got, mine, theirs, *here, *there)


def after(value, *events):
    return lax.optimization_barrier((value, *events))[0]


def together(own, other):
    return jnp.concatenate([own, other], axis=0)


def per_device(master_weights, first_moment, second_moment, gradient_shard, hidden_states):
    core = lax.rem(lax.axis_index("section"), 2)
    xlo = lax.div(lax.axis_index("dp"), 4)
    z = lax.rem(lax.axis_index("dp"), 4)
    upper = core == 1
    core_word = jnp.reshape(core, (1,)).astype(jnp.int32)
    step = jnp.arange(4, dtype=jnp.int32)

    def columns(is_upper):
        owner = lax.rem(z + jnp.where(is_upper, step, 4 - step), 4)
        return jnp.stack([owner + 4 * xlo, owner + 4 * (1 - xlo)], axis=1).reshape(8) * SUB

    y = lax.rem(lax.div(lax.axis_index("section"), 2), 4)
    flips = jnp.stack([y < 2, y == 0]).astype(jnp.int32)
    filler = jnp.zeros((5,), jnp.int32)
    table = jnp.concatenate([columns(upper), core_word, flips, filler, columns(~upper)])
    table = table.astype(jnp.int32)

    states, mine, theirs, keep, give = update_call(
        core_word,
        master_weights,
        first_moment,
        second_moment,
        gradient_shard,
        hidden_states.reshape(ROWS, D),
    )
    other = to_core(theirs)
    even_rows = jnp.where(upper, other, mine)
    odd_rows = jnp.where(upper, mine, other)
    got = to_core(after(give, other))
    odd = jnp.where(upper, keep, got)

    queue = []

    def ring(value, *events):
        value = to_ring(after(value, *queue[-3:-1], *events))
        queue.append(value)
        return value

    home_own = [even_rows, ring(even_rows)]
    home_other = to_pair(even_rows)
    near_odd = to_next_pair(odd_rows)

    home_own.append(ring(home_own[1], odd))
    home_others = [home_other, ring(home_other, near_odd)]
    far = to_next_pair(near_odd)
    near_even = to_next_pair(after(even_rows, near_odd))
    third_other = to_pair(near_odd)

    home_own.append(ring(home_own[2]))
    home_others.append(ring(home_others[1], far, third_other))
    far_other = to_pair(far)
    home_others.append(ring(home_others[2], near_even))
    second_other = to_pair(near_even)
    odd = to_chip(after(odd, near_even), 2)

    home = [piece for pair in zip(home_own, home_others) for piece in pair]
    (product,) = layer_call(table, (keep, got), after=home, picks=True, name="project_home")
    first = [together(far, far_other)]
    first.append(ring(first[0]))
    second = [together(near_even, second_other)]
    third = [together(near_odd, third_other)]
    second.append(ring(second[0], third[0]))
    first.append(ring(first[1]))
    even, home_here = layer_call(
        table,
        (keep, got),
        products=(product,),
        last=home,
        picks=True,
        keeps=True,
        name="expand_home",
    )
    third.append(ring(third[0], even))
    even = to_chip(even, 2)
    first.append(ring(first[2]))
    second.append(ring(second[1], odd))
    third.append(ring(third[1]))
    second.append(ring(second[2]))
    home_there = to_core(after(home_here, third[2]))
    third.append(ring(third[2]))

    even = after(even, third[2])
    products = layer_call(table, (even, odd), after=first, after_flip=9, name="project_first")
    even, odd, *products = layer_call(
        table,
        (even, odd),
        products=products,
        last=first,
        after=second,
        last_flip=9,
        after_flip=10,
        name="first_second",
    )
    even, odd, *products = layer_call(
        table,
        (even, odd),
        products=products,
        last=second,
        after=third,
        last_flip=10,
        after_flip=10,
        name="second_third",
    )
    keep, give, product = layer_call(
        table,
        (even, odd),
        products=products,
        last=third,
        after=[home_here],
        last_flip=10,
        skip=1,
        swaps=True,
        name="third_home",
    )
    out = final_call(
        table, keep, to_core(give), product, to_core(product), [home_here], [home_there]
    )
    return (*states, out.reshape(hidden_states.shape))


def solution(mesh):
    placed = (
        P("section", "dp", None),
        P("section", "dp", None),
        P("section", "dp", None),
        P("section", "dp", None),
        P("section", None, "dp", None),
    )
    return jax.shard_map(
        per_device,
        mesh=mesh,
        in_specs=placed,
        out_specs=(
            P("section", "dp", None),
            P("section", "dp", None),
            P("section", "dp", None),
            P("section", None, "dp", None),
        ),
        check_vma=False,
    )
```

```python
import dataclasses
import functools

import jax
import jax.numpy as jnp
from jax import lax
from jax.experimental import pallas as pl
from jax.experimental.pallas import tpu as pltpu
from jax.sharding import PartitionSpec as P

ADAM_STEP = 1000

beta_one = 0.9
beta_two = 0.95
learn_rate = 0.0003
decay_rate = 0.1
adam_eps = 1e-08
norm_eps = 1e-05

AXES = ("section", "dp")
D = 8192
KVW = 512
ROWS = 256
SUB = 512
HALF = D // 2
LANES = 128
VMEM = 22 * 1024 * 1024
UPDATE_VMEM = 56 * 1024 * 1024
UPDATE_STEPS = 2
SUB_STEP = SUB // UPDATE_STEPS
COST = pl.CostEstimate(flops=1, bytes_accessed=1, transcendentals=0)
AHEAD = 3


def place(linear):
    section, dp = divmod(linear, 8)
    return section // 2, section % 2, dp // 4, dp % 4


def linear_of(chip, core, xlo, z):
    return ((chip % 8) * 2 + core) * 8 + (xlo % 2) * 4 + z % 4


def shift(value, move):
    pairs = [(source, linear_of(*move(*place(source)))) for source in range(128)]
    return lax.ppermute(value, AXES, pairs)


def to_core(value):
    return shift(value, lambda chip, core, xlo, z: (chip, 1 - core, xlo, z))


def to_pair(value):
    return shift(value, lambda chip, core, xlo, z: (chip, core, xlo + 1, z))


def to_ring(value):
    return shift(value, lambda chip, core, xlo, z: (chip, core, xlo, z + 1 - 2 * core))


def to_chip(value, steps):
    return shift(value, lambda chip, core, xlo, z: (chip + steps, core, xlo, z))


def to_next_pair(value):
    def move(chip, core, xlo, z):
        return chip + 1, core, xlo + (chip % 4 == 3), z

    return shift(value, move)


def adamw_update(master, moment, second, gradient):
    moment_new = beta_one * moment + (1.0 - beta_one) * gradient
    second_new = beta_two * second + (1.0 - beta_two) * gradient * gradient
    corr_one = 1.0 - beta_one**ADAM_STEP
    corr_two = 1.0 - beta_two**ADAM_STEP
    step_size = moment_new / corr_one / (jnp.sqrt(second_new / corr_two) + adam_eps)
    master_new = master - learn_rate * (step_size + decay_rate * master)
    return (master_new, moment_new, second_new)


def update_kernel(
    core_ref,
    master_ref,
    moment_ref,
    second_ref,
    gradient_ref,
    whole_ref,
    master_out,
    moment_out,
    second_out,
    keep_rows,
    give_rows,
    keep,
    give,
):
    lower = core_ref[0] == 0
    new_master, new_moment, new_second = adamw_update(
        master_ref[...], moment_ref[...], second_ref[...], gradient_ref[...]
    )
    master_out[...] = new_master
    moment_out[...] = new_moment
    second_out[...] = new_second
    first = new_master[0].astype(jnp.bfloat16)
    last = new_master[1].astype(jnp.bfloat16)
    keep_rows[...] = jnp.where(lower, first, last)
    give_rows[...] = jnp.where(lower, last, first)
    for part in range(8 // UPDATE_STEPS):
        first = whole_ref[:, 2 * part * SUB : (2 * part + 1) * SUB]
        last = whole_ref[:, (2 * part + 1) * SUB : (2 * part + 2) * SUB]
        keep[:, part * SUB : (part + 1) * SUB] = jnp.where(lower, first, last)
        give[:, part * SUB : (part + 1) * SUB] = jnp.where(lower, last, first)


def update_call(core, master, moment, second, gradient, whole):
    state = pl.BlockSpec((2, SUB_STEP, KVW), lambda i, core: (0, i, 0))
    half = pl.BlockSpec((SUB_STEP, KVW), lambda i, core: (i, 0))
    part = pl.BlockSpec((ROWS, HALF // UPDATE_STEPS), lambda i, core: (0, i))
    shaped = [a.reshape(2, SUB, KVW) for a in (master, moment, second, gradient)]
    outs = pl.pallas_call(
        update_kernel,
        grid_spec=pltpu.PrefetchScalarGridSpec(
            num_scalar_prefetch=1,
            grid=(UPDATE_STEPS,),
            in_specs=[state] * 4
            + [pl.BlockSpec((ROWS, D // UPDATE_STEPS), lambda i, core: (0, i))],
            out_specs=[state] * 3 + [half] * 2 + [part] * 2,
        ),
        out_shape=[jax.ShapeDtypeStruct((2, SUB, KVW), jnp.float32)] * 3
        + [jax.ShapeDtypeStruct((SUB, KVW), jnp.bfloat16)] * 2
        + [jax.ShapeDtypeStruct((ROWS, HALF), jnp.bfloat16)] * 2,
        compiler_params=pltpu.CompilerParams(vmem_limit_bytes=UPDATE_VMEM),
        cost_estimate=COST,
        name="update",
    )(core, *shaped, whole)
    return [a.reshape(master.shape) for a in outs[:3]], *outs[3:]


def read_columns(table, blocks, slots, sems, order):
    copies = {}
    for chunk in order:
        column = pl.multiple_of(table[chunk], SUB)
        for index, block in enumerate(blocks):
            copies[chunk, index] = pltpu.make_async_copy(
                block.at[:, pl.ds(column, SUB)],
                slots.at[chunk, pl.ds(index * ROWS, ROWS)],
                sems.at[chunk, index],
            )
    return copies


def picked_columns(table, arrays, slots, sems, order):
    return {
        (chunk, 0): Picked(
            table[8],
            *(
                read_columns(table, (array,), slots, sems, (chunk,))[chunk, 0]
                for array in arrays
            ),
        )
        for chunk in order
    }


@dataclasses.dataclass(frozen=True)
class Picked:
    core: jax.Array
    lower: object
    upper: object

    def start(self):
        pl.when(self.core == 0)(self.lower.start)
        pl.when(self.core == 1)(self.upper.start)

    def wait(self):
        self.lower.wait()


def chunks_of(pieces, flip):
    for piece in pieces:
        for start in range(0, piece.shape[0], SUB):
            if flip is not None and piece.shape[0] == 2 * SUB:
                start = pl.multiple_of(start + flip * (SUB - 2 * start), SUB)
            yield piece.at[pl.ds(start, SUB)]


def read_pieces(pieces, slots, sems, flip=None):
    return [
        pltpu.make_async_copy(chunk, slots.at[index], sems.at[index])
        for index, chunk in enumerate(chunks_of(pieces, flip))
    ]


def projected_of(mine, theirs):
    summed = mine[...] + theirs[...]
    scale = lax.rsqrt(summed[:, KVW : KVW + 1] * (1.0 / D) + norm_eps)
    return (summed[:, :KVW] * scale).astype(jnp.bfloat16)


def layer_kernel(plan, *refs):
    refs = list(refs)

    def take(count):
        taken, refs[:count] = refs[:count], []
        return taken

    (table,) = take(1)
    blocks = take(plan.blocks + plan.picks)
    mine = take(plan.blocks if plan.last else 0)
    theirs = take(plan.blocks if plan.last else 0)
    last = take(plan.last)
    after = take(plan.after)
    fresh = take(plan.blocks) if plan.last else []
    kept = take(1) if plan.keeps else []
    out = take(plan.blocks - plan.skip if plan.after else 0)
    columns, column_sems = take(2)
    last_slots, last_sems = take(2) if plan.last else (None, None)
    after_slots, after_sems = take(2) if plan.after else (None, None)
    (store_sems,) = take(1) if plan.last else (None,)
    (keep_sems,) = take(1) if plan.keeps else (None,)

    taken_up = range(plan.first, plan.first + plan.count)
    chunks = range(8) if plan.last else taken_up
    read = picked_columns if plan.picks else read_columns
    reads = read(table, blocks, columns, column_sems, chunks)
    flips = [None if at is None else table[at] for at in (plan.last_flip, plan.after_flip)]
    last_reads = read_pieces(last, last_slots, last_sems, flips[0]) if plan.last else []
    after_reads = read_pieces(after, after_slots, after_sems, flips[1]) if plan.after else []

    def begin(chunk):
        if chunk not in chunks:
            return
        for index in range(plan.blocks):
            reads[chunk, index].start()
        if plan.last:
            last_reads[chunk].start()
        if chunk in taken_up:
            after_reads[chunk - plan.first].start()

    for ahead in range(AHEAD):
        begin(chunks[0] + ahead)
    rows = plan.blocks * ROWS
    if plan.last:
        projected = jnp.concatenate(
            [projected_of(here, there) for here, there in zip(mine, theirs)], axis=0
        )
    skip = plan.skip * ROWS
    if plan.after:
        total = jnp.zeros((rows - skip, KVW), jnp.float32)
        squares = jnp.zeros((rows - skip, 1), jnp.float32)
    stores = []
    for chunk in chunks:
        begin(chunk + AHEAD)
        for index in range(plan.blocks):
            reads[chunk, index].wait()
        part = columns[chunk]
        if plan.last:
            last_reads[chunk].wait()
            if plan.keeps:
                stores.append(
                    pltpu.make_async_copy(
                        last_slots.at[chunk],
                        kept[0].at[pl.ds(chunk * SUB, SUB)],
                        keep_sems.at[chunk],
                    )
                )
                stores[-1].start()
            update = lax.dot_general(
                projected,
                last_slots[chunk],
                (((1,), (1,)), ((), ())),
                preferred_element_type=jnp.float32,
            )
            part = (part.astype(jnp.float32) + update).astype(jnp.bfloat16)
            columns[chunk] = part
            column = pl.multiple_of(table[chunk], SUB)
            if plan.swaps:
                own = table[8]
                sources = [own * ROWS, (1 - own) * ROWS]
            else:
                sources = [index * ROWS for index in range(plan.blocks)]
            for index in range(plan.blocks):
                stores.append(
                    pltpu.make_async_copy(
                        columns.at[chunk, pl.ds(sources[index], ROWS)],
                        fresh[index].at[:, pl.ds(column, SUB)],
                        store_sems.at[chunk, index],
                    )
                )
                stores[-1].start()
        if chunk in taken_up:
            after_reads[chunk - plan.first].wait()
            part = part[skip:]
            total += jnp.dot(
                part,
                after_slots[chunk - plan.first],
                preferred_element_type=jnp.float32,
            )
            flat = part.astype(jnp.float32)
            squares += jnp.sum(flat * flat, axis=1, keepdims=True)
    if plan.after:
        for index, product in enumerate(out):
            part = slice(index * ROWS, (index + 1) * ROWS)
            product[:, :KVW] = total[part]
            product[:, KVW:] = jnp.broadcast_to(squares[part], (ROWS, LANES))
    for store in stores:
        store.wait()


@dataclasses.dataclass(frozen=True)
class Plan:
    blocks: int
    last: int
    after: int
    first: int = 0
    count: int = 0
    skip: int = 0
    swaps: bool = False
    keeps: bool = False
    last_flip: int | None = None
    after_flip: int | None = None
    picks: bool = False


def layer_call(table, blocks, products=(), last=(), after=(), name="layer", **plan):
    count = sum(piece.shape[0] for piece in after) // SUB
    picks = plan.get("picks", False)
    plan = Plan(len(blocks) - picks, len(last), len(after), count=count, **plan)
    sums = (*products, *map(to_core, products))
    rows = plan.blocks * ROWS
    any_space = pl.BlockSpec(memory_space=pl.ANY)
    vmem = pl.BlockSpec(memory_space=pltpu.VMEM)
    out_shape, out_specs = [], []
    scratch = [
        pltpu.VMEM((8, rows, SUB), jnp.bfloat16),
        pltpu.SemaphoreType.DMA((8, plan.blocks)),
    ]
    if plan.last:
        out_shape += [jax.ShapeDtypeStruct((ROWS, HALF), jnp.bfloat16)] * plan.blocks
        out_specs += [any_space] * plan.blocks
        scratch += [pltpu.VMEM((8, SUB, KVW), jnp.bfloat16), pltpu.SemaphoreType.DMA((8,))]
    if plan.keeps:
        out_shape.append(jax.ShapeDtypeStruct((HALF, KVW), jnp.bfloat16))
        out_specs.append(any_space)
    if plan.after:
        ahead = plan.blocks - plan.skip
        out_shape += [jax.ShapeDtypeStruct((ROWS, KVW + LANES), jnp.float32)] * ahead
        out_specs += [vmem] * ahead
        scratch += [
            pltpu.VMEM((plan.count, SUB, KVW), jnp.bfloat16),
            pltpu.SemaphoreType.DMA((plan.count,)),
        ]
    if plan.last:
        scratch.append(pltpu.SemaphoreType.DMA((8, plan.blocks)))
    if plan.keeps:
        scratch.append(pltpu.SemaphoreType.DMA((8,)))
    return pl.pallas_call(
        functools.partial(layer_kernel, plan),
        in_specs=[pl.BlockSpec(memory_space=pltpu.SMEM)]
        + [any_space] * len(blocks)
        + [vmem] * len(sums)
        + [any_space] * len(last)
        + [any_space] * len(after),
        out_specs=out_specs,
        out_shape=out_shape,
        scratch_shapes=scratch,
        compiler_params=pltpu.CompilerParams(vmem_limit_bytes=VMEM),
        cost_estimate=COST,
        name=name,
    )(table, *blocks, *sums, *last, *after)


def final_kernel(table, keep, got, mine, theirs, *refs):
    pieces, (whole, slots, slot_sems, w_slots, w_sems, store_sems) = refs[:-6], refs[-6:]
    upper = table[8] == 1
    reads, stores = [], []
    for chunk in range(16):
        source = keep if chunk < 8 else got
        column = pl.multiple_of(table[(0 if chunk < 8 else 16) + chunk % 8], SUB)
        reads.append(
            pltpu.make_async_copy(
                source.at[:, pl.ds(column, SUB)], slots.at[chunk], slot_sems.at[chunk]
            )
        )
        side = table[8] if chunk < 8 else 1 - table[8]
        target = pl.multiple_of(2 * column + side * SUB, SUB)
        stores.append(
            pltpu.make_async_copy(
                slots.at[chunk], whole.at[:, pl.ds(target, SUB)], store_sems.at[chunk]
            )
        )
    weights = read_pieces(pieces, w_slots, w_sems)

    def begin(chunk):
        if chunk < 16:
            reads[chunk].start()
            weights[chunk].start()

    for ahead in range(2 * AHEAD):
        begin(ahead)
    projected = projected_of(mine, theirs)
    for chunk in range(16):
        begin(chunk + 2 * AHEAD)
        reads[chunk].wait()
        weights[chunk].wait()

        @pl.when(upper)
        def _():
            update = lax.dot_general(
                projected,
                w_slots[chunk],
                (((1,), (1,)), ((), ())),
                preferred_element_type=jnp.float32,
            )
            slots[chunk] = (slots[chunk].astype(jnp.float32) + update).astype(jnp.bfloat16)

        stores[chunk].start()
    for store in stores:
        store.wait()


def final_call(table, keep, got, mine, theirs, here, there):
    any_space = pl.BlockSpec(memory_space=pl.ANY)
    vmem = pl.BlockSpec(memory_space=pltpu.VMEM)
    return pl.pallas_call(
        final_kernel,
        in_specs=[pl.BlockSpec(memory_space=pltpu.SMEM), any_space, any_space, vmem, vmem]
        + [any_space] * (len(here) + len(there)),
        out_specs=any_space,
        out_shape=jax.ShapeDtypeStruct((ROWS, D), jnp.bfloat16),
        scratch_shapes=[
            pltpu.VMEM((16, ROWS, SUB), jnp.bfloat16),
            pltpu.SemaphoreType.DMA((16,)),
            pltpu.VMEM((16, SUB, KVW), jnp.bfloat16),
            pltpu.SemaphoreType.DMA((16,)),
            pltpu.SemaphoreType.DMA((16,)),
        ],
        compiler_params=pltpu.CompilerParams(vmem_limit_bytes=VMEM),
        cost_estimate=COST,
        name="final_layer",
    )(table, keep, got, mine, theirs, *here, *there)


def after(value, *events):
    return lax.optimization_barrier((value, *events))[0]


def together(own, other):
    return jnp.concatenate([own, other], axis=0)


def per_device(master_weights, first_moment, second_moment, gradient_shard, hidden_states):
    core = lax.rem(lax.axis_index("section"), 2)
    xlo = lax.div(lax.axis_index("dp"), 4)
    z = lax.rem(lax.axis_index("dp"), 4)
    upper = core == 1
    core_word = jnp.reshape(core, (1,)).astype(jnp.int32)
    step = jnp.arange(4, dtype=jnp.int32)

    def columns(is_upper):
        owner = lax.rem(z + jnp.where(is_upper, step, 4 - step), 4)
        return jnp.stack([owner + 4 * xlo, owner + 4 * (1 - xlo)], axis=1).reshape(8) * SUB

    y = lax.rem(lax.div(lax.axis_index("section"), 2), 4)
    flips = jnp.stack([y < 2, y == 0]).astype(jnp.int32)
    filler = jnp.zeros((5,), jnp.int32)
    table = jnp.concatenate([columns(upper), core_word, flips, filler, columns(~upper)])
    table = table.astype(jnp.int32)

    states, mine, theirs, keep, give = update_call(
        core_word,
        master_weights,
        first_moment,
        second_moment,
        gradient_shard,
        hidden_states.reshape(ROWS, D),
    )
    other = to_core(theirs)
    even_rows = jnp.where(upper, other, mine)
    odd_rows = jnp.where(upper, mine, other)
    got = to_core(after(give, other))
    odd = jnp.where(upper, keep, got)

    queue = []

    def ring(value, *events):
        value = to_ring(after(value, *queue[-3:-1], *events))
        queue.append(value)
        return value

    home_own = [even_rows, ring(even_rows)]
    home_other = to_pair(even_rows)
    near_odd = to_next_pair(odd_rows)

    home_own.append(ring(home_own[1], odd))
    home_others = [home_other, ring(home_other, near_odd)]
    far = to_next_pair(near_odd)
    near_even = to_next_pair(after(even_rows, near_odd))
    third_other = to_pair(near_odd)

    home_own.append(ring(home_own[2]))
    home_others.append(ring(home_others[1], far, third_other))
    far_other = to_pair(far)
    home_others.append(ring(home_others[2], near_even))
    second_other = to_pair(near_even)
    odd = to_chip(after(odd, near_even), 2)

    home = [piece for pair in zip(home_own, home_others) for piece in pair]
    (product,) = layer_call(table, (keep, got), after=home, picks=True, name="project_home")
    first = [together(far, far_other)]
    first.append(ring(first[0]))
    second = [together(near_even, second_other)]
    third = [together(near_odd, third_other)]
    second.append(ring(second[0], third[0]))
    first.append(ring(first[1]))
    even, home_here = layer_call(
        table,
        (keep, got),
        products=(product,),
        last=home,
        picks=True,
        keeps=True,
        name="expand_home",
    )
    third.append(ring(third[0], even))
    even = to_chip(even, 2)
    first.append(ring(first[2]))
    second.append(ring(second[1], odd))
    third.append(ring(third[1]))
    second.append(ring(second[2]))
    home_there = to_core(after(home_here, third[2]))
    third.append(ring(third[2]))

    even = after(even, second[3])
    products = layer_call(table, (even, odd), after=first, after_flip=9, name="project_first")
    even, odd, *products = layer_call(
        table,
        (even, odd),
        products=products,
        last=first,
        after=second,
        last_flip=9,
        after_flip=10,
        name="first_second",
    )
    even, odd, *products = layer_call(
        table,
        (even, odd),
        products=products,
        last=second,
        after=third,
        last_flip=10,
        after_flip=10,
        name="second_third",
    )
    keep, give, product = layer_call(
        table,
        (even, odd),
        products=products,
        last=third,
        after=[home_here],
        last_flip=10,
        skip=1,
        swaps=True,
        name="third_home",
    )
    out = final_call(
        table, keep, to_core(give), product, to_core(product), [home_here], [home_there]
    )
    return (*states, out.reshape(hidden_states.shape))


def solution(mesh):
    placed = (
        P("section", "dp", None),
        P("section", "dp", None),
        P("section", "dp", None),
        P("section", "dp", None),
        P("section", None, "dp", None),
    )
    return jax.shard_map(
        per_device,
        mesh=mesh,
        in_specs=placed,
        out_specs=(
            P("section", "dp", None),
            P("section", "dp", None),
            P("section", "dp", None),
            P("section", None, "dp", None),
        ),
        check_vma=False,
    )
```
